32 devices in a mesh: dp: 8 (over y, x, core), expert: 4 (over z).
Axes of the slice: x: 2, y: 2, z: 4, core: 2. Of those that a mesh axis runs over, the one named last changes fastest.
Arguments:
- tokens: bfloat16 [4096, 1536], P(('dp', 'expert')), may hold values from -6 to 6
- cotangent: float32 [4096, 1536], P(('dp', 'expert')), may hold values from -6 to 6
- segments: int32 [32, 128], P(('dp', 'expert')), may hold values from 0 to 3, never falling along the last dimension, each value on 1 to 64 neighbouring positions
- expert_ids: int32 [4096, 8], P(('dp', 'expert')), may hold values from 0 to 39, all different within a row; in each aligned block of 128 rows (0 to 127, 128 to 255, ...) at most 32 rows name the same one
- route_weights: float32 [4096, 8], P(('dp', 'expert')), may hold values from 0.2 to 1
- w_qkv: float32 [1536, 2560], P(('dp', 'expert')), may hold values from -0.15625 to 0.15625
- w_out: float32 [1536, 1536], P(('dp', 'expert')), may hold values from -0.625 to 0.625
- gains: float32 [2, 1536], P(None, ('dp', 'expert')), may hold values from 0.5 to 1.5
- w_gate_up: float32 [40, 1536, 1024], P('expert', 'dp'), may hold values from -0.15625 to 0.15625
- w_down: float32 [40, 512, 1536], P('expert', 'dp'), may hold values from -0.25 to 0.25
- first_moment_projection: float32 [1536, 2560], P(('dp', 'expert')), may hold values from -96 to 96
- first_out: float32 [1536, 1536], P(('dp', 'expert')), may hold values from -19.2 to 19.2
- first_gains: float32 [2, 1536], P(None, ('dp', 'expert')), may hold values from -76.8 to 76.8
- first_gate_up: float32 [40, 1536, 1024], P('expert', 'dp'), may hold values from -12.021101 to 12.021101
- first_down: float32 [40, 512, 1536], P('expert', 'dp'), may hold values from -6.8692008 to 6.8692008
- second_moment_projection: float32 [1536, 2560], P(('dp', 'expert')), may hold values from 1310.72 to 5406.72
- second_out: float32 [1536, 1536], P(('dp', 'expert')), may hold values from 53.248 to 217.088
- second_gains: float32 [2, 1536], P(None, ('dp', 'expert')), may hold values from 860.16 to 3481.6
- second_gate_up: float32 [40, 1536, 1024], P('expert', 'dp'), may hold values from 20.48 to 85.1968
- second_down: float32 [40, 512, 1536], P('expert', 'dp'), may hold values from 6.88128 to 27.8528
Outputs:
- out_tokens: float32 [4096, 1536], P(('dp', 'expert'))
- grad_tokens: float32 [4096, 1536], P(('dp', 'expert'))
- grad_qkv: float32 [1536, 2560], P(('dp', 'expert'))
- grad_out: float32 [1536, 1536], P(('dp', 'expert'))
- grad_gains: float32 [2, 1536], P(None, ('dp', 'expert'))
- grad_gate_up: float32 [40, 1536, 1024], P('expert', 'dp')
- grad_down: float32 [40, 512, 1536], P('expert', 'dp')
- new_qkv: float32 [1536, 2560], P(('dp', 'expert'))
- new_out: float32 [1536, 1536], P(('dp', 'expert'))
- new_gains: float32 [2, 1536], P(None, ('dp', 'expert'))
- new_gate_up: float32 [40, 1536, 1024], P('expert', 'dp')
- new_down: float32 [40, 512, 1536], P('expert', 'dp')
- new_first_qkv: float32 [1536, 2560], P(('dp', 'expert'))
- new_first_out: float32 [1536, 1536], P(('dp', 'expert'))
- new_first_gains: float32 [2, 1536], P(None, ('dp', 'expert'))
- new_first_gate_up: float32 [40, 1536, 1024], P('expert', 'dp')
- new_first_down: float32 [40, 512, 1536], P('expert', 'dp')
- new_second_qkv: float32 [1536, 2560], P(('dp', 'expert'))
- new_second_out: float32 [1536, 1536], P(('dp', 'expert'))
- new_second_gains: float32 [2, 1536], P(None, ('dp', 'expert'))
- new_second_gate_up: float32 [40, 1536, 1024], P('expert', 'dp')
- new_second_down: float32 [40, 512, 1536], P('expert', 'dp')
The draws below stay inside these ranges and needn't reach their ends.
Inputs may be any that keep to these rules, and one draw needn't show every extreme that they name: `segments`: segment numbers never fall along a sequence; each segment spans at most half of 128 positions. `expert_ids`: each row names 8 different experts; within the rows of one device no expert is named more than 32 times, and in every draw some device names some expert exactly 32 times.
All inputs are finite; a program needn't handle non-finite values.
Results may differ from the reference program's by a relative error of at most 0.014.
The reference program's roundings to bfloat16 on the way count: a program that leaves them out, or rounds other values in their place, can miss the bound.
Values may be sent and summed in bfloat16 or wider, within the bound.
No kernel may reach another device: no remote copies, remote signals or barrier semaphores. Data moves between devices by JAX's collectives and lax.ppermute only.
A program may use at most 448 MiB of HBM per device.

```python
import math
import jax
import jax.numpy as jnp
import numpy as np
from jax import lax

MODEL_WIDTH = 1536
QUERY_HEADS = 24
KEY_VALUE_HEADS = 8
HEAD_SIZE = 64
FF = 512
EXPERTS = 40
TOP = 8
SEQ = 128
CAP = 32
SEQS = 32
TOKENS = 4096
N_DP = 8
N_EXPERT = 4


def grad_size(which):
    pair_share = TOKENS * TOP / EXPERTS
    if which == 'qkv':
        return 2.5 * math.sqrt(TOKENS)
    if which == 'out':
        return 0.5 * math.sqrt(TOKENS)
    if which == 'gains':
        return 2.0 * math.sqrt(TOKENS)
    if which == 'gate_up':
        return 0.7 * math.sqrt(pair_share)
    return 0.4 * math.sqrt(pair_share)


def first_moment(key, which, shape):
    sampled = jax.random.truncated_normal(key, -4.0, 4.0, shape, jnp.float32)
    return sampled * (0.15 * grad_size(which))


def second_moment(key, which, shape):
    factor = jnp.exp(jax.random.uniform(key, shape, jnp.float32, -math.log(2.0), math.log(2.0)))
    return factor * (0.1053 * grad_size(which) ** 2)


def draw_first_moment_projection(key, part):
    return first_moment(key, 'qkv', (MODEL_WIDTH, (QUERY_HEADS + 2 * KEY_VALUE_HEADS) * HEAD_SIZE))


def draw_first_out(key, part):
    return first_moment(key, 'out', (QUERY_HEADS * HEAD_SIZE, MODEL_WIDTH))


def draw_first_gains(key, part):
    return first_moment(key, 'gains', (2, MODEL_WIDTH))


def draw_first_gate_up(key, part):
    return first_moment(key, 'gate_up', (EXPERTS, MODEL_WIDTH, 2 * FF))


def draw_first_down(key, part):
    return first_moment(key, 'down', (EXPERTS, FF, MODEL_WIDTH))


def draw_second_moment_projection(key, part):
    return second_moment(key, 'qkv', (MODEL_WIDTH, (QUERY_HEADS + 2 * KEY_VALUE_HEADS) * HEAD_SIZE))


def draw_second_out(key, part):
    return second_moment(key, 'out', (QUERY_HEADS * HEAD_SIZE, MODEL_WIDTH))


def draw_second_gains(key, part):
    return second_moment(key, 'gains', (2, MODEL_WIDTH))


def draw_second_gate_up(key, part):
    return second_moment(key, 'gate_up', (EXPERTS, MODEL_WIDTH, 2 * FF))


def draw_second_down(key, part):
    return second_moment(key, 'down', (EXPERTS, FF, MODEL_WIDTH))


def shard_levels(key, extent, shards, smallest, largest):
    loudness = 1.0
    for dim, shards_of in shards:
        steps = jax.random.uniform(jax.random.fold_in(jax.random.fold_in(key, 6), dim), (shards_of,), jnp.float32, smallest / len(shards), largest / len(shards))
        loudness = loudness * jnp.repeat(jnp.exp(steps), extent[dim] // shards_of).reshape((-1,) + (1,) * (len(extent) - 1 - dim))
    return loudness


def length_profile(amount, total, limit, slope):
    portions = [(1 << 20) // math.isqrt(grade ** slope) + 1 for grade in range(2, amount + 1)]
    spare, holding = total - limit - (amount - 1), [1] * (amount - 1)
    while spare > 0:
        candidates = [i for i in range(amount - 1) if holding[i] < limit]
        whole, remaining = sum([portions[i] for i in candidates]), spare
        for i in candidates:
            more = min(limit - holding[i], max(1, remaining * portions[i] // whole), spare)
            holding[i] = holding[i] + more
            spare = spare - more
    return np.array([limit] + holding)


def uneven(key, amount, total, reach, skew):
    if amount == 2:
        one = jax.random.randint(key, (), max(1, total - reach), min(reach, total - 1) + 1)
        return jnp.stack([one, total - one])
    lengths = jnp.asarray(length_profile(amount, total, reach, skew), jnp.int32)
    twos = (amount - 1) // 2
    giver, receiver = lengths[1:1 + 2 * twos:2], lengths[2:2 + 2 * twos:2]
    room = jnp.minimum(giver - 1, reach - receiver)
    moved = jax.random.randint(jax.random.fold_in(key, 1), (twos,), 0, 1 << 20) % (room + 1)
    lengths = lengths.at[1:1 + 2 * twos:2].set(giver - moved).at[2:2 + 2 * twos:2].set(receiver + moved)
    return lengths[jax.random.permutation(jax.random.fold_in(key, 2), amount)]


def routed_block(stream_key, own, number, rows, amount, top, bound, lean):
    sequence = jax.random.permutation(stream_key, amount)
    heavy_load, common = shares(amount, rows * top, bound, lean, True), shares(amount, rows * top, bound, lean, False)
    places = jnp.arange(amount)

    def named(lengths, rotation):
        used = int((lengths > 0).sum())
        fixed = max(1, used // 4)
        shifted = fixed + (places - fixed + rotation * (used - fixed)) % max(1, amount - fixed)
        return jnp.zeros((amount,), jnp.int32).at[sequence[jnp.where(places < fixed, places, shifted)]].set(jnp.asarray(lengths, jnp.int32))

    lengths = jnp.where(number % 4 == 0, named(heavy_load, number // 4), named(common, number - number // 4 - 1))
    mixed = jax.random.permutation(jax.random.fold_in(own, 3), amount)
    source_of, sink = mixed[0:amount // 2 * 2:2], mixed[1:amount // 2 * 2:2]
    margin = jnp.minimum(lengths[source_of] - 1, bound - lengths[sink]) // 2
    margin = jnp.where((source_of == sequence[0]) | (sink == sequence[0]) | (lengths[sink] == 0), 0, jnp.maximum(margin, 0))
    shifted = jax.random.randint(jax.random.fold_in(own, 4), (amount // 2,), 0, 1 << 20) % (margin + 1)
    lengths = lengths.at[source_of].add(-shifted).at[sink].add(shifted)
    items = jnp.searchsorted(jnp.cumsum(lengths), jnp.arange(rows * top), side="right").astype(jnp.int32)
    listing = items.reshape(top, rows).T
    listing = listing[jax.random.permutation(jax.random.fold_in(own, 1), rows)]
    rotation = jax.random.randint(jax.random.fold_in(own, 2), (rows, 1), 0, top)
    return jnp.take_along_axis(listing, (jnp.arange(top)[None, :] + rotation) % top, axis=1)


def shares(count, total, bound, skew, full):
    portions = [(1 << 20) // math.isqrt(standing ** skew) + 1 for standing in range(1, count + 1)]
    largest = bound if full else min(bound, max(-(-total // count), total * portions[0] // sum(portions)))
    least = 1 if total - largest >= count - 1 else 0
    holding, rest = [largest] + [least] * (count - 1), total - largest - least * (count - 1)
    while rest > 0:
        candidates = [i for i in range(1, count) if holding[i] < largest] or [i for i in range(1, count) if holding[i] < bound]
        mass, left = sum([portions[i] for i in candidates]), rest
        for i in candidates:
            extra = min(bound - holding[i], max(1, left * portions[i] // mass), rest)
            holding[i] = holding[i] + extra
            rest = rest - extra
    return np.array(holding)


def centred(stream_key, shape, width, limit, cuts=(), kind=jnp.bfloat16):
    drawn = jax.random.normal(stream_key, shape, jnp.float32) * width
    if len(cuts) > 0:
        drawn = shard_levels(stream_key, shape, cuts, -0.22, 0.18) * drawn
    return jnp.clip(drawn, min=-limit, max=limit).astype(kind)


def setup_inputs(seed: int = 0) -> dict:
    seeds = jax.random.split(jax.random.key(seed), 21)
    tokens = centred(seeds[0], (TOKENS, MODEL_WIDTH), 1.0, 6.0, ((0, 32),))
    cotangent = centred(seeds[1], (TOKENS, MODEL_WIDTH), 1.0, 6.0, ((0, 32),), jnp.float32)
    segments = jax.vmap(lambda own: jnp.searchsorted(jnp.cumsum(uneven(own, 4, SEQ, SEQ // 2, 2)), jnp.arange(SEQ), side="right"))(jax.random.split(seeds[2], SEQS)).reshape((SEQS, SEQ)).astype(jnp.int32)
    expert_ids_keys = jax.random.split(jax.random.fold_in(seeds[3], 1), TOKENS // SEQ)
    expert_ids_turns = jax.random.permutation(jax.random.fold_in(seeds[3], 3), TOKENS // SEQ)
    expert_ids = jax.vmap(lambda own, number: routed_block(jax.random.fold_in(seeds[3], 2), own, number, SEQ, EXPERTS, TOP, CAP, 2))(expert_ids_keys, expert_ids_turns).reshape((TOKENS, TOP))
    route_weights = jnp.clip(0.2 + 0.8 * jax.random.uniform(seeds[4], (TOKENS, TOP), jnp.float32) ** shard_levels(seeds[4], (TOKENS, TOP), ((0, 32),), -0.2, 0.2), 0.2, 1.0)
    w_qkv = centred(seeds[5], (MODEL_WIDTH, (QUERY_HEADS + 2 * KEY_VALUE_HEADS) * HEAD_SIZE), MODEL_WIDTH ** -0.5, 0.15625, ((0, 32),), jnp.float32)
    w_out = centred(seeds[6], (QUERY_HEADS * HEAD_SIZE, MODEL_WIDTH), (MODEL_WIDTH // 16) ** -0.5, 0.625, ((0, 32),), jnp.float32)
    gains = jnp.clip(1.0 + 0.1 * jax.random.normal(seeds[7], (2, MODEL_WIDTH), jnp.float32), 0.5, 1.5)
    w_gate_up = centred(seeds[8], (EXPERTS, MODEL_WIDTH, 2 * FF), MODEL_WIDTH ** -0.5, 0.15625, ((0, 4), (1, 8)), jnp.float32)
    w_down = centred(seeds[9], (EXPERTS, FF, MODEL_WIDTH), FF ** -0.5, 0.25, ((0, 4), (1, 8)), jnp.float32)
    first_moment_projection = draw_first_moment_projection(jax.random.fold_in(seeds[20], 71), 0)
    first_out = draw_first_out(jax.random.fold_in(seeds[20], 71), 0)
    first_gains = draw_first_gains(jax.random.fold_in(seeds[20], 71), 0)
    first_gate_up = draw_first_gate_up(jax.random.fold_in(seeds[20], 71), 0)
    first_down = draw_first_down(jax.random.fold_in(seeds[20], 71), 0)
    second_moment_projection = draw_second_moment_projection(jax.random.fold_in(seeds[20], 71), 0)
    second_out = draw_second_out(jax.random.fold_in(seeds[20], 71), 0)
    second_gains = draw_second_gains(jax.random.fold_in(seeds[20], 71), 0)
    second_gate_up = draw_second_gate_up(jax.random.fold_in(seeds[20], 71), 0)
    second_down = draw_second_down(jax.random.fold_in(seeds[20], 71), 0)
    return dict(tokens=tokens, cotangent=cotangent, segments=segments, expert_ids=expert_ids, route_weights=route_weights, w_qkv=w_qkv, w_out=w_out, gains=gains, w_gate_up=w_gate_up, w_down=w_down, first_moment_projection=first_moment_projection, first_out=first_out, first_gains=first_gains, first_gate_up=first_gate_up, first_down=first_down, second_moment_projection=second_moment_projection, second_out=second_out, second_gains=second_gains, second_gate_up=second_gate_up, second_down=second_down)


eps_norm = 1e-05
beta_one = 0.9
beta_two = 0.95
adam_eps = 1e-08
learn_rate = 0.01
out_rate = 0.04
gain_rate = 0.2
weight_decay = 0.1
correct_one = 1.0 - beta_one ** 3
correct_two = 1.0 - beta_two ** 3

def norm_scale(rows):
    return lax.rsqrt(lax.optimization_barrier(jnp.mean(rows * rows, -1, keepdims=True)) + eps_norm)

def rotary_tables(sequence_length, half_dim):
    position = jnp.arange(sequence_length, dtype=jnp.float32)[:, None]
    frequency = 10000.0 ** (-jnp.arange(half_dim, dtype=jnp.float32) / half_dim)
    angles = position * frequency[None, :]
    return (jnp.cos(angles), jnp.sin(angles))

def apply_rotary(value_rows, cosine_table, sine_table, middle):
    half_dim = value_rows.shape[-1] // 2
    shape = (cosine_table.shape[0],) + (1,) * middle + (half_dim,)
    cosine_table = cosine_table.reshape(shape)
    sine_table = sine_table.reshape(shape)
    first = value_rows[..., :half_dim]
    second = value_rows[..., half_dim:]
    return jnp.concatenate([first * cosine_table - second * sine_table, second * cosine_table + first * sine_table], -1)

def split_heads(projected_rows, sequence_length, cosine_table, sine_table):
    query_total_width = QUERY_HEADS * HEAD_SIZE
    key_columns_width = KEY_VALUE_HEADS * HEAD_SIZE
    query_block = apply_rotary(projected_rows[:, :query_total_width].reshape(sequence_length, KEY_VALUE_HEADS, QUERY_HEADS // KEY_VALUE_HEADS, HEAD_SIZE), cosine_table, sine_table, 2)
    key_rows = apply_rotary(projected_rows[:, query_total_width:query_total_width + key_columns_width].reshape(sequence_length, KEY_VALUE_HEADS, HEAD_SIZE), cosine_table, sine_table, 1)
    value_rows = projected_rows[:, query_total_width + key_columns_width:].reshape(sequence_length, KEY_VALUE_HEADS, HEAD_SIZE)
    return (query_block.astype(jnp.bfloat16), key_rows.astype(jnp.bfloat16), value_rows.astype(jnp.bfloat16))

def allowed_mask(segment):
    spots = jnp.arange(segment.shape[0])
    return (spots[:, None] >= spots[None, :]) & (segment[:, None] == segment[None, :])

def score_block(query_block, key_rows, segment):
    scores = jnp.einsum('qhgd,khd->hgqk', query_block.astype(jnp.float32), key_rows.astype(jnp.float32)) * query_block.shape[-1] ** (-0.5)
    return jnp.where(allowed_mask(segment)[None, None], scores, -1e+30)

def attend(query_block, key_rows, value_rows, segment):
    scores = score_block(query_block, key_rows, segment)
    highest = lax.optimization_barrier(jnp.max(scores, -1, keepdims=True))
    logsum = highest + jnp.log(lax.optimization_barrier(jnp.sum(jnp.exp(scores - highest), -1, keepdims=True)))
    probs = jnp.exp(scores - logsum).astype(jnp.bfloat16)
    attended = jnp.einsum('hgqk,khd->qhgd', probs.astype(jnp.float32), value_rows.astype(jnp.float32))
    return (attended.astype(jnp.bfloat16), logsum)

def attend_back(query_block, key_rows, value_rows, segment, logsum, attended_gradient):
    factor = query_block.shape[-1] ** (-0.5)
    probs = jnp.exp(score_block(query_block, key_rows, segment) - logsum)
    grad_wide = attended_gradient.astype(jnp.float32)
    grad_probs = jnp.einsum('qhgd,khd->hgqk', grad_wide, value_rows.astype(jnp.float32))
    inner_sum = lax.optimization_barrier(jnp.sum(probs * grad_probs, -1, keepdims=True))
    grad_scores = (probs * (grad_probs - inner_sum) * factor).astype(jnp.bfloat16).astype(jnp.float32)
    grad_values = jnp.einsum('hgqk,qhgd->khd', probs.astype(jnp.bfloat16).astype(jnp.float32), grad_wide)
    grad_query = jnp.einsum('hgqk,khd->qhgd', grad_scores, key_rows.astype(jnp.float32))
    grad_keys = jnp.einsum('hgqk,qhgd->khd', grad_scores, query_block.astype(jnp.float32))
    return (grad_query, grad_keys, grad_values)

def join_grads(grad_query, grad_keys, grad_values, cosine_table, sine_table):
    sequence_length = grad_query.shape[0]
    grad_query = apply_rotary(grad_query, cosine_table, -sine_table, 2).reshape(sequence_length, -1)
    grad_keys = apply_rotary(grad_keys, cosine_table, -sine_table, 1).reshape(sequence_length, -1)
    return jnp.concatenate([grad_query, grad_keys, grad_values.reshape(sequence_length, -1)], -1).astype(jnp.bfloat16)

def adam_step(weight, grad, first, second, step_rate, shrink):
    first = beta_one * first + (1.0 - beta_one) * grad
    second = beta_two * second + (1.0 - beta_two) * grad * grad
    update = first / correct_one / (jnp.sqrt(second / correct_two) + adam_eps)
    return (weight - step_rate * (update + shrink * weight), first, second)

def reference(tokens, cotangent, segments, expert_ids, route_weights, w_qkv, w_out, gains, w_gate_up, w_down, first_moment_projection, first_out, first_gains, first_gate_up, first_down, second_moment_projection, second_out, second_gains, second_gate_up, second_down):
    sequence_count = segments.shape[0]
    sequence_length = segments.shape[1]
    device_count = N_DP * N_EXPERT
    tok_block = tokens.shape[0] // device_count
    qkv_half = w_qkv.astype(jnp.bfloat16)
    out_half = w_out.astype(jnp.bfloat16)
    gate_up_half = w_gate_up.astype(jnp.bfloat16)
    down_half = w_down.astype(jnp.bfloat16)
    gain_wide = lax.optimization_barrier(gains.astype(jnp.bfloat16)).astype(jnp.float32)
    gain_attn = gain_wide[0]
    gain_moe = gain_wide[1]
    cosine_table, sine_table = rotary_tables(sequence_length, HEAD_SIZE // 2)
    inputs = tokens.astype(jnp.float32)
    scale_one = norm_scale(inputs)
    normed_one = (inputs * scale_one * gain_attn).astype(jnp.bfloat16)
    normed_seqs = normed_one.reshape(sequence_count, sequence_length, -1)

    def forward_seq(carry, slab):
        normed_seq, segment = slab
        projected_rows = jnp.dot(normed_seq, qkv_half, preferred_element_type=jnp.float32)
        query_block, key_rows, value_rows = split_heads(projected_rows, sequence_length, cosine_table, sine_table)
        attended_seq, logsum = attend(query_block, key_rows, value_rows, segment)
        return (carry, (attended_seq.reshape(sequence_length, QUERY_HEADS * HEAD_SIZE), logsum))
    unused, (attended, logsums) = lax.scan(forward_seq, jnp.zeros((), jnp.float32), (normed_seqs, segments))
    attended = attended.reshape(-1, QUERY_HEADS * HEAD_SIZE)
    resid = inputs + jnp.dot(attended, out_half, preferred_element_type=jnp.float32)
    scale_two = norm_scale(resid)
    normed_two = (resid * scale_two * gain_moe).astype(jnp.bfloat16)
    flat_ids = expert_ids.reshape(device_count, tok_block * TOP)
    one_hot = (flat_ids[..., None] == jnp.arange(EXPERTS, dtype=jnp.int32)).astype(jnp.int32)
    ranking = lax.optimization_barrier(jnp.sum(jnp.cumsum(one_hot, 1) * one_hot, -1)) - 1
    target = flat_ids * CAP + ranking + (jnp.arange(device_count, dtype=jnp.int32) * (EXPERTS * CAP))[:, None]
    pair_total = device_count * tok_block * TOP
    owners = jnp.full((device_count * EXPERTS * CAP,), -1, jnp.int32).at[target.reshape(-1)].set(jnp.arange(pair_total, dtype=jnp.int32))
    owners = owners.reshape(device_count, EXPERTS, CAP).transpose(1, 0, 2).reshape(EXPERTS, device_count * CAP)
    route_flat = route_weights.reshape(-1)

    def expert_rows(owner_rows, gate_up_one):
        filled = (owner_rows >= 0)[:, None]
        safe_owner = jnp.maximum(owner_rows, 0)
        rows = jnp.where(filled, normed_two[safe_owner // TOP], jnp.zeros((), jnp.bfloat16))
        mixed = jnp.dot(rows, gate_up_one, preferred_element_type=jnp.float32)
        gate = mixed[:, :FF]
        upper = mixed[:, FF:]
        hidden = (jax.nn.silu(gate) * upper).astype(jnp.bfloat16)
        return (filled, safe_owner, rows, gate, upper, hidden)

    def expert_forward(total, slab):
        owner_rows, gate_up_one, down_one = slab
        filled, safe_owner, rows, gate, upper, hidden = expert_rows(owner_rows, gate_up_one)
        expert_out = jnp.dot(hidden, down_one, preferred_element_type=jnp.float32).astype(jnp.bfloat16)
        weighting = jnp.where(filled[:, 0], route_flat[safe_owner], jnp.zeros((), jnp.float32))
        total = total.at[safe_owner // TOP].add(weighting[:, None] * expert_out.astype(jnp.float32))
        return (total, None)
    moe_sum, unused = lax.scan(expert_forward, jnp.zeros_like(resid), (owners, gate_up_half, down_half))
    out_tokens = resid + moe_sum

    def expert_backward(total, slab):
        owner_rows, gate_up_one, down_one = slab
        filled, safe_owner, rows, gate, upper, hidden = expert_rows(owner_rows, gate_up_one)
        tok_index = safe_owner // TOP
        grad_rows = jnp.where(filled, (route_flat[safe_owner][:, None] * cotangent[tok_index]).astype(jnp.bfloat16), jnp.zeros((), jnp.bfloat16))
        grad_hidden = jnp.dot(grad_rows, down_one.T, preferred_element_type=jnp.float32)
        grad_down_one = jnp.dot(hidden.T, grad_rows, preferred_element_type=jnp.float32)
        sigma = jax.nn.sigmoid(gate)
        grad_mixed = jnp.concatenate([grad_hidden * upper * sigma * (1.0 + gate * (1.0 - sigma)), grad_hidden * gate * sigma], -1).astype(jnp.bfloat16)
        grad_gate_up_one = jnp.dot(rows.T, grad_mixed, preferred_element_type=jnp.float32)
        grad_in = jnp.dot(grad_mixed, gate_up_one.T, preferred_element_type=jnp.float32).astype(jnp.bfloat16)
        total = total.at[tok_index].add(grad_in.astype(jnp.float32))
        return (total, (grad_gate_up_one, grad_down_one))
    grad_normed_two, (grad_gate_up, grad_down) = lax.scan(expert_backward, jnp.zeros_like(resid), (owners, gate_up_half, down_half))
    hat_two = grad_normed_two * gain_moe
    grad_gain_moe = lax.optimization_barrier(jnp.sum(grad_normed_two * resid * scale_two, 0))
    grad_resid = cotangent + scale_two * (hat_two - resid * scale_two ** 2 * lax.optimization_barrier(jnp.mean(hat_two * resid, -1, keepdims=True)))
    grad_resid_half = grad_resid.astype(jnp.bfloat16)
    grad_out = jnp.dot(attended.T, grad_resid_half, preferred_element_type=jnp.float32)
    attended_gradient = jnp.dot(grad_resid_half, out_half.T, preferred_element_type=jnp.float32).astype(jnp.bfloat16)
    attended_gradient = attended_gradient.reshape(sequence_count, sequence_length, KEY_VALUE_HEADS, QUERY_HEADS // KEY_VALUE_HEADS, HEAD_SIZE)

    def backward_seq(total, slab):
        normed_seq, segment, logsum, grad_seq = slab
        projected_rows = jnp.dot(normed_seq, qkv_half, preferred_element_type=jnp.float32)
        query_block, key_rows, value_rows = split_heads(projected_rows, sequence_length, cosine_table, sine_table)
        grad_query, grad_keys, grad_values = attend_back(query_block, key_rows, value_rows, segment, logsum, grad_seq)
        grad_proj = join_grads(grad_query, grad_keys, grad_values, cosine_table, sine_table)
        total = total + jnp.dot(normed_seq.T, grad_proj, preferred_element_type=jnp.float32)
        return (total, jnp.dot(grad_proj, qkv_half.T, preferred_element_type=jnp.float32))
    grad_qkv, grad_normed_one = lax.scan(backward_seq, jnp.zeros(w_qkv.shape, jnp.float32), (normed_seqs, segments, logsums, attended_gradient))
    grad_normed_one = grad_normed_one.reshape(-1, grad_normed_one.shape[-1])
    hat_one = grad_normed_one * gain_attn
    grad_gain_attn = lax.optimization_barrier(jnp.sum(grad_normed_one * inputs * scale_one, 0))
    grad_tokens = grad_resid + scale_one * (hat_one - inputs * scale_one ** 2 * lax.optimization_barrier(jnp.mean(hat_one * inputs, -1, keepdims=True)))
    grad_gains = jnp.stack([grad_gain_attn, grad_gain_moe])
    new_qkv, new_first_qkv, new_second_qkv = adam_step(w_qkv, grad_qkv, first_moment_projection, second_moment_projection, learn_rate, weight_decay)
    new_out, new_first_out, new_second_out = adam_step(w_out, grad_out, first_out, second_out, out_rate, weight_decay)
    new_gains, new_first_gains, new_second_gains = adam_step(gains, grad_gains, first_gains, second_gains, gain_rate, 0.0)
    new_gate_up, new_first_gate_up, new_second_gate_up = adam_step(w_gate_up, grad_gate_up, first_gate_up, second_gate_up, learn_rate, weight_decay)
    new_down, new_first_down, new_second_down = adam_step(w_down, grad_down, first_down, second_down, learn_rate, weight_decay)
    return (out_tokens, grad_tokens, grad_qkv, grad_out, grad_gains, grad_gate_up, grad_down, new_qkv, new_out, new_gains, new_gate_up, new_down, new_first_qkv, new_first_out, new_first_gains, new_first_gate_up, new_first_down, new_second_qkv, new_second_out, new_second_gains, new_second_gate_up, new_second_down)
```

```python
import functools

import jax
import jax.numpy as jnp
import numpy as np
from jax import lax
from jax.experimental import pallas as pl
from jax.experimental.pallas import tpu as pltpu
from jax.sharding import PartitionSpec as P

MODEL_WIDTH = 1536
QUERY_HEADS = 24
KEY_VALUE_HEADS = 8
HEAD_SIZE = 64
FF = 512
EXPERTS = 40
TOP = 8
CAP = 32


eps_norm = 1e-05
beta_one = 0.9
beta_two = 0.95
adam_eps = 1e-08
learn_rate = 0.01
out_rate = 0.04
gain_rate = 0.2
weight_decay = 0.1
correct_one = 1.0 - beta_one**3
correct_two = 1.0 - beta_two**3


def norm_scale(rows):
    return lax.rsqrt(jnp.mean(rows * rows, -1, keepdims=True) + eps_norm)


def rotary_tables(sequence_length, half_dim):
    position = jnp.arange(sequence_length, dtype=jnp.float32)[:, None]
    frequency = 10000.0 ** (-jnp.arange(half_dim, dtype=jnp.float32) / half_dim)
    angles = position * frequency[None, :]
    return (jnp.cos(angles), jnp.sin(angles))


def apply_rotary(value_rows, cosine_table, sine_table, middle):
    half_dim = value_rows.shape[-1] // 2
    shape = (cosine_table.shape[0],) + (1,) * middle + (half_dim,)
    cosine_table = cosine_table.reshape(shape)
    sine_table = sine_table.reshape(shape)
    first = value_rows[..., :half_dim]
    second = value_rows[..., half_dim:]
    return jnp.concatenate(
        [first * cosine_table - second * sine_table, second * cosine_table + first * sine_table], -1
    )


def split_heads(projected_rows, sequence_count, sequence_length, cosine_table, sine_table):
    query_total_width = QUERY_HEADS * HEAD_SIZE
    key_columns_width = KEY_VALUE_HEADS * HEAD_SIZE
    reshaped_rows = projected_rows.reshape(sequence_count, sequence_length, -1)
    query_block = apply_rotary(
        reshaped_rows[..., :query_total_width].reshape(
            sequence_count,
            sequence_length,
            KEY_VALUE_HEADS,
            QUERY_HEADS // KEY_VALUE_HEADS,
            HEAD_SIZE,
        ),
        cosine_table,
        sine_table,
        2,
    )
    key_rows = apply_rotary(
        reshaped_rows[..., query_total_width : query_total_width + key_columns_width].reshape(
            sequence_count, sequence_length, KEY_VALUE_HEADS, HEAD_SIZE
        ),
        cosine_table,
        sine_table,
        1,
    )
    value_rows = reshaped_rows[..., query_total_width + key_columns_width :].reshape(
        sequence_count, sequence_length, KEY_VALUE_HEADS, HEAD_SIZE
    )
    return (
        query_block.astype(jnp.bfloat16),
        key_rows.astype(jnp.bfloat16),
        value_rows.astype(jnp.bfloat16),
    )


def allowed_mask(segment):
    spots = jnp.arange(segment.shape[0])
    return (spots[:, None] >= spots[None, :]) & (segment[:, None] == segment[None, :])


def score_block(query_block, key_rows, segment):
    scores = jnp.einsum(
        "qhgd,khd->hgqk", query_block, key_rows, preferred_element_type=jnp.float32
    ) * query_block.shape[-1] ** (-0.5)
    return jnp.where(allowed_mask(segment)[None, None], scores, -1e30)


def attend(query_block, key_rows, value_rows, segment):
    scores = score_block(query_block, key_rows, segment)
    highest = jnp.max(scores, -1, keepdims=True)
    logsum = highest + jnp.log(jnp.sum(jnp.exp(scores - highest), -1, keepdims=True))
    probs = jnp.exp(scores - logsum).astype(jnp.bfloat16)
    attended = jnp.einsum("hgqk,khd->qhgd", probs, value_rows, preferred_element_type=jnp.float32)
    return (attended.astype(jnp.bfloat16), logsum)


def attend_back(query_block, key_rows, value_rows, segment, logsum, attended_gradient):
    factor = query_block.shape[-1] ** (-0.5)
    probs = jnp.exp(score_block(query_block, key_rows, segment) - logsum)
    grad_probs = jnp.einsum(
        "qhgd,khd->hgqk", attended_gradient, value_rows, preferred_element_type=jnp.float32
    )
    inner_sum = jnp.sum(probs * grad_probs, -1, keepdims=True)
    grad_scores = (probs * (grad_probs - inner_sum) * factor).astype(jnp.bfloat16)
    grad_values = jnp.einsum(
        "hgqk,qhgd->khd",
        probs.astype(jnp.bfloat16),
        attended_gradient,
        preferred_element_type=jnp.float32,
    )
    grad_query = jnp.einsum(
        "hgqk,khd->qhgd", grad_scores, key_rows, preferred_element_type=jnp.float32
    )
    grad_keys = jnp.einsum(
        "hgqk,qhgd->khd", grad_scores, query_block, preferred_element_type=jnp.float32
    )
    return (grad_query, grad_keys, grad_values)


def join_grads(grad_query, grad_keys, grad_values, cosine_table, sine_table):
    sequence_length = grad_query.shape[0]
    grad_query = apply_rotary(grad_query, cosine_table, -sine_table, 2).reshape(sequence_length, -1)
    grad_keys = apply_rotary(grad_keys, cosine_table, -sine_table, 1).reshape(sequence_length, -1)
    return jnp.concatenate(
        [grad_query, grad_keys, grad_values.reshape(sequence_length, -1)], -1
    ).astype(jnp.bfloat16)


def adam_step(weight, grad, first, second, step_rate, shrink):
    first = beta_one * first + (1.0 - beta_one) * grad
    second = beta_two * second + (1.0 - beta_two) * grad * grad
    update = first / correct_one / (jnp.sqrt(second / correct_two) + adam_eps)
    return (weight - step_rate * (update + shrink * weight), first, second)


NARROW = jnp.bfloat16
WIDE = jnp.float32
DISTANCE = (0, 1, -1, 2)
HOP_CORE, HOP_X, HOP_Y = 1, 2, 4


def swap(rows, pick):
    count = lax.axis_size("dp")
    return lax.ppermute(rows, "dp", [(i, i ^ pick(i)) for i in range(count)])


def first_hop(i):
    return HOP_X if i & 1 else HOP_Y


def second_hop(i):
    return HOP_Y if i & 1 else HOP_X


def swap_core(rows):
    return swap(rows, lambda i: HOP_CORE)


def swap_first(rows):
    return swap(rows, first_hop)


def swap_second(rows):
    return swap(rows, second_hop)


def turn(rows, step):
    count = lax.axis_size("expert")
    return lax.ppermute(rows, "expert", [(i, (i + step) % count) for i in range(count)])


def gather_plane_last(block):
    ahead, behind = turn(block, 1), turn(block, -1)
    found = []
    for part in (block, ahead, behind, turn(ahead, 1)):
        pair = jnp.concatenate([part, swap_first(part)], 0)
        found.append((pair, swap_second(pair)))
    return found


def gather_ring_middle(block):
    pair = jnp.concatenate([block, swap_first(block)], 0)
    ahead, behind = turn(pair, 1), turn(pair, -1)
    return [(part, swap_second(part)) for part in (pair, ahead, behind, turn(ahead, 1))]


def ring_sum(parts):
    far = turn(parts[3].astype(NARROW), -1)
    ahead = turn((parts[1] + far.astype(WIDE)).astype(NARROW), -1)
    behind = turn(parts[2].astype(NARROW), 1)
    return parts[0] + ahead.astype(WIDE) + behind.astype(WIDE)


def scatter_plane_first(parts):
    found = [None] * 4
    for spot in (3, 1, 2, 0):
        near, away = parts[spot]
        near = near + swap_second(away).astype(WIDE)
        half = near.shape[0] // 2
        found[spot] = near[:half] + swap_first(near[half:].astype(NARROW)).astype(WIDE)
    return ring_sum(found)


def scatter_ring_middle(parts):
    found = [None] * 4
    for spot in (3, 1, 2, 0):
        near, away = parts[spot]
        found[spot] = near + swap_second(away).astype(WIDE)
    total = ring_sum(found)
    half = total.shape[0] // 2
    return total[:half] + swap_first(total[half:].astype(NARROW)).astype(WIDE)


def gathered_sources(count_dp, count_expert):
    table = np.zeros((count_dp, count_expert, 4, 2, 2, 2), np.int32)
    for i in range(count_dp):
        for z in range(count_expert):
            for spot, distance in enumerate(DISTANCE):
                for second in range(2):
                    for first in range(2):
                        plane = i ^ (first_hop(i) * first) ^ (second_hop(i) * second)
                        table[i, z, spot, second, first] = plane, (z - distance) % count_expert
    return table.reshape(count_dp, count_expert, 16, 2)


def split_three(values):
    high = values.astype(NARROW)
    left = values - high.astype(WIDE)
    middle = left.astype(NARROW)
    return [high, middle, (left - middle.astype(WIDE)).astype(NARROW)]


def select_columns(values, chosen):
    rows = values.shape[0]
    parts = jnp.dot(
        jnp.concatenate(split_three(values), 0), chosen, preferred_element_type=jnp.float32
    )
    return parts[:rows] + parts[rows : 2 * rows] + parts[2 * rows :]


def parity_columns(rows, parity):
    count = rows.shape[0]
    query_total_width = QUERY_HEADS * HEAD_SIZE
    key_columns_width = KEY_VALUE_HEADS * HEAD_SIZE
    bounds = (
        (0, query_total_width),
        (query_total_width, query_total_width + key_columns_width),
        (query_total_width + key_columns_width, query_total_width + 2 * key_columns_width),
    )
    return jnp.concatenate(
        [
            rows[:, low:high].reshape(count, KEY_VALUE_HEADS // 2, 2, -1)[:, :, parity]
            .reshape(count, -1)
            for low, high in bounds
        ],
        1,
    )


def join_parities(even, odd):
    count = even.shape[0]
    query_half = QUERY_HEADS * HEAD_SIZE // 2
    key_half = KEY_VALUE_HEADS * HEAD_SIZE // 2
    bounds = (
        (0, query_half),
        (query_half, query_half + key_half),
        (query_half + key_half, query_half + 2 * key_half),
    )
    heads = KEY_VALUE_HEADS // 2
    return jnp.concatenate(
        [
            jnp.stack(
                [
                    even[:, low:high].reshape(count, heads, -1),
                    odd[:, low:high].reshape(count, heads, -1),
                ],
                2,
            ).reshape(count, -1)
            for low, high in bounds
        ],
        1,
    )


def split_head_group(projected_rows, cosine_table, sine_table):
    sequences, length = projected_rows.shape[:2]
    heads = KEY_VALUE_HEADS // 2
    group = QUERY_HEADS // KEY_VALUE_HEADS
    query_width = heads * group * HEAD_SIZE
    key_width = heads * HEAD_SIZE
    query_block = projected_rows[..., :query_width].reshape(
        sequences, length, heads, group, HEAD_SIZE
    )
    key_rows = projected_rows[..., query_width : query_width + key_width].reshape(
        sequences, length, heads, HEAD_SIZE
    )
    value_rows = projected_rows[..., query_width + key_width :].reshape(
        sequences, length, heads, HEAD_SIZE
    )
    query_block = jax.vmap(lambda a: apply_rotary(a, cosine_table, sine_table, 2))(query_block)
    key_rows = jax.vmap(lambda a: apply_rotary(a, cosine_table, sine_table, 1))(key_rows)
    return (
        query_block.astype(jnp.bfloat16),
        key_rows.astype(jnp.bfloat16),
        value_rows.astype(jnp.bfloat16),
    )


def expert_kernel(
    near_ref,
    away_ref,
    near_grad_ref,
    away_grad_ref,
    route_ref,
    gate_ref,
    upper_ref,
    down_ref,
    near_out_ref,
    away_out_ref,
    near_back_ref,
    away_back_ref,
    hidden_ref,
    grad_gate_ref,
    grad_upper_ref,
    rows_ref,
    grads_ref,
    out_ref,
    back_ref,
    *,
    per_step,
):
    step = pl.program_id(0)
    half = near_ref.shape[0]
    width = near_ref.shape[1]

    @pl.when(step == 0)
    def _():
        rows_ref[:half, :] = near_ref[...]
        rows_ref[half:, :] = away_ref[...]
        grads_ref[:half, :] = near_grad_ref[:, :width]
        grads_ref[half:, :] = away_grad_ref[:, :width]
        out_ref[...] = jnp.zeros_like(out_ref)
        back_ref[...] = jnp.zeros_like(back_ref)

    rows = rows_ref[...]
    grads = grads_ref[...]
    contract_last = (((1,), (1,)), ((), ()))
    gate = jnp.dot(rows, gate_ref[...], preferred_element_type=jnp.float32)
    upper = jnp.dot(rows, upper_ref[...], preferred_element_type=jnp.float32)
    grad_hidden = lax.dot_general(
        grads, down_ref[...], contract_last, preferred_element_type=jnp.float32
    )
    route = route_ref[...]
    lanes = lax.broadcasted_iota(jnp.int32, route.shape, 1)
    columns = gate.shape[1] // per_step
    spread = []
    for i in range(per_step):
        one = jnp.sum(jnp.where(lanes == step * per_step + i, route, 0.0), 1, keepdims=True)
        spread.append(jnp.broadcast_to(one, (route.shape[0], columns)))
    weight = jnp.concatenate(spread, 1)
    sigma = 1.0 / (1.0 + jnp.exp(-gate))
    active = gate * sigma
    hidden = (weight * active * upper).astype(jnp.bfloat16)
    weighted = weight * grad_hidden
    grad_gate = (weighted * upper * sigma * (1.0 + gate * (1.0 - sigma))).astype(jnp.bfloat16)
    grad_upper = (weighted * active).astype(jnp.bfloat16)
    hidden_ref[...] = hidden
    grad_gate_ref[...] = grad_gate
    grad_upper_ref[...] = grad_upper
    out_ref[...] += jnp.dot(hidden, down_ref[...], preferred_element_type=jnp.float32)
    back_ref[...] += lax.dot_general(
        grad_gate, gate_ref[...], contract_last, preferred_element_type=jnp.float32
    ) + lax.dot_general(
        grad_upper, upper_ref[...], contract_last, preferred_element_type=jnp.float32
    )

    @pl.when(step == pl.num_programs(0) - 1)
    def _():
        near_out_ref[...] = out_ref[:half, :]
        away_out_ref[...] = out_ref[half:, :].astype(jnp.bfloat16)
        near_back_ref[...] = back_ref[:half, :]
        away_back_ref[...] = back_ref[half:, :].astype(jnp.bfloat16)


def expert_block(near, away, near_grad, away_grad, route, gate_w, upper_w, down_w, experts):
    half, width = near.shape
    total = gate_w.shape[1]
    per_step = 2
    steps = experts // per_step
    columns = total // steps
    whole = lambda a: pl.BlockSpec(a.shape, lambda i: (0, 0))
    rows = 2 * half
    f32 = lambda r, c: jax.ShapeDtypeStruct((r, c), jnp.float32)
    b16 = lambda r, c: jax.ShapeDtypeStruct((r, c), jnp.bfloat16)
    fixed = pl.BlockSpec((half, width), lambda i: (0, 0))
    part = pl.BlockSpec((rows, columns), lambda i: (0, i))
    flops = 2 * rows * width * total * 6
    return pl.pallas_call(
        functools.partial(expert_kernel, per_step=per_step),
        grid=(steps,),
        in_specs=[
            whole(near),
            whole(away),
            whole(near_grad),
            whole(away_grad),
            whole(route),
            pl.BlockSpec((width, columns), lambda i: (0, i)),
            pl.BlockSpec((width, columns), lambda i: (0, i)),
            pl.BlockSpec((columns, width), lambda i: (i, 0)),
        ],
        out_specs=[fixed] * 4 + [part] * 3,
        out_shape=[f32(half, width), b16(half, width)] * 2 + [b16(rows, total)] * 3,
        scratch_shapes=[
            pltpu.VMEM((rows, width), jnp.bfloat16),
            pltpu.VMEM((rows, width), jnp.bfloat16),
            pltpu.VMEM((rows, width), jnp.float32),
            pltpu.VMEM((rows, width), jnp.float32),
        ],
        compiler_params=pltpu.CompilerParams(vmem_limit_bytes=44 * 1024 * 1024),
        cost_estimate=pl.CostEstimate(
            flops=flops,
            bytes_accessed=2 * (3 * width * total + 3 * rows * total + 10 * rows * width),
            transcendentals=rows * total,
        ),
    )(near, away, near_grad, away_grad, route, gate_w, upper_w, down_w)


def shards_moved(
    tokens,
    cotangent,
    segments,
    expert_ids,
    route_weights,
    w_qkv,
    w_out,
    gains,
    w_gate_up,
    w_down,
    first_moment_projection,
    first_out,
    first_gains,
    first_gate_up,
    first_down,
    second_moment_projection,
    second_out,
    second_gains,
    second_gate_up,
    second_down,
):
    sequence_length = segments.shape[1]
    count_dp, count_expert = lax.axis_size("dp"), lax.axis_size("expert")
    place_dp, place_expert = lax.axis_index("dp"), lax.axis_index("expert")
    core = place_dp % 2
    chip = place_dp // 2
    chips = count_dp // 2
    local_experts = EXPERTS // count_expert
    owned = w_qkv.shape[0]
    half_columns = w_qkv.shape[1] // 2
    half_width = MODEL_WIDTH // 2
    lane_pad = 128

    narrow_qkv = w_qkv.astype(NARROW)
    even_columns, odd_columns = parity_columns(narrow_qkv, 0), parity_columns(narrow_qkv, 1)
    gain_columns = jnp.pad(gains.astype(NARROW).T, ((0, 0), (0, lane_pad - 2)))
    kept = jnp.where(core == 0, even_columns, odd_columns)
    given = jnp.where(core == 0, odd_columns, even_columns)
    taken = swap_core(jnp.concatenate([given, gain_columns], 1))
    narrow_out = w_out.astype(NARROW)
    block = jnp.concatenate(
        [
            jnp.concatenate([jnp.concatenate([kept, gain_columns], 1), taken], 0),
            jnp.concatenate([narrow_out[:, :half_width], narrow_out[:, half_width:]], 0),
        ],
        1,
    )
    attention_blocks = gather_ring_middle(block)

    sources = jnp.asarray(gathered_sources(count_dp, count_expert))[place_dp, place_expert]
    from_dp, from_expert = sources[:, 0], sources[:, 1]
    row_in = jnp.arange(owned, dtype=jnp.int32)
    feature = (
        ((from_dp[:, None] ^ jnp.arange(2, dtype=jnp.int32)[None, :]) * count_expert
         + from_expert[:, None])[:, :, None] * owned + row_in
    ).reshape(-1)
    head_feature = (
        ((from_dp // 2 * count_expert + from_expert) * owned)[:, None] + row_in
    ).reshape(-1)
    places = jnp.arange(MODEL_WIDTH, dtype=jnp.int32)
    to_gathered = (places[:, None] == feature[None, :]).astype(NARROW)
    from_gathered = (feature[:, None] == places[None, :]).astype(NARROW)
    head_places = places[: half_width]
    heads_to_gathered = (head_places[:, None] == head_feature[None, :]).astype(NARROW)
    heads_from_gathered = (head_feature[:, None] == head_places[None, :]).astype(NARROW)

    ff_columns = FF // chips

    def columns_of(which):
        gate = lax.dynamic_slice_in_dim(w_gate_up, which * ff_columns, ff_columns, 2)
        upper = lax.dynamic_slice_in_dim(w_gate_up, FF + which * ff_columns, ff_columns, 2)
        return jnp.stack(
            [
                jnp.concatenate([a[e] for e in range(local_experts)], 1).astype(NARROW)
                for a in (gate, upper)
            ]
        )

    plane_rows = w_gate_up.shape[1]
    share = local_experts * ff_columns
    mine = jnp.zeros((chips, 2, plane_rows, share), NARROW)
    for other in range(chips):
        piece = columns_of(chip ^ other)
        if other:
            piece = swap(piece, lambda i, other=other: 2 * other)
        mine = lax.dynamic_update_slice(mine, piece[None], (chip ^ other, 0, 0, 0))
    theirs = swap_core(mine)
    both = jnp.where(
        core == 0, jnp.stack([mine, theirs], 1), jnp.stack([theirs, mine], 1)
    )
    gate_w = both[:, :, 0].reshape(MODEL_WIDTH, share)
    upper_w = both[:, :, 1].reshape(MODEL_WIDTH, share)
    down_mine = w_down.astype(NARROW)
    down_theirs = swap_core(down_mine)
    down_w = jnp.where(
        core == 0,
        jnp.concatenate([down_mine, down_theirs], 1),
        jnp.concatenate([down_theirs, down_mine], 1),
    ).reshape(share, MODEL_WIDTH)

    routes = jnp.concatenate([expert_ids.astype(NARROW)] + split_three(route_weights), 1)
    cotangent_blocks = gather_plane_last(
        jnp.concatenate(
            [
                cotangent.astype(NARROW),
                jnp.pad(routes, ((0, 0), (0, lane_pad - routes.shape[1]))),
            ],
            1,
        )
    )

    def dense_route(rows):
        ids = rows[:, :TOP].astype(jnp.int32)
        parts = rows[:, TOP : 4 * TOP].astype(WIDE)
        weights = parts[:, :TOP] + parts[:, TOP : 2 * TOP] + parts[:, 2 * TOP :]
        local = place_expert * local_experts + jnp.arange(lane_pad, dtype=jnp.int32)
        match = (ids[:, :, None] == local) & (jnp.arange(lane_pad) < local_experts)
        return jnp.sum(jnp.where(match, weights[:, :, None], 0.0), 1)

    cosine_table, sine_table = rotary_tables(sequence_length, HEAD_SIZE // 2)
    inputs = tokens.astype(WIDE)
    pair_tokens = jnp.concatenate([tokens, swap_core(tokens)], 0)
    pair_segments = jnp.concatenate([segments, swap_core(segments)], 0)
    scale_pair = norm_scale(pair_tokens.astype(WIDE))
    scale_one = scale_pair[:sequence_length]
    pair_gathered = jnp.dot(pair_tokens, to_gathered, preferred_element_type=jnp.float32)
    blocks = [half for pair in attention_blocks for half in pair]
    qkv_here = jnp.concatenate([b[:, :half_columns] for b in blocks], 0)
    gain_here = jnp.concatenate(
        [b[:, half_columns : half_columns + 2] for b in blocks], 0
    ).T
    out_here = jnp.concatenate(
        [
            b[:, half_columns + lane_pad :]
            .reshape(2, 2, owned, half_width)
            .transpose(0, 2, 1, 3)
            .reshape(2 * owned, MODEL_WIDTH)
            for b in blocks
        ],
        0,
    )
    gain_attn = gain_here[0].astype(WIDE)
    gains_placed = jnp.dot(gain_here, from_gathered, preferred_element_type=jnp.float32)
    gain_moe = gains_placed[1]
    normed_one = (pair_gathered * scale_pair * gain_attn).astype(NARROW)
    projected = jnp.dot(normed_one, qkv_here, preferred_element_type=jnp.float32)
    query_block, key_rows, value_rows = split_head_group(
        projected.reshape(2, sequence_length, -1), cosine_table, sine_table
    )
    attended, logsums = jax.vmap(attend)(query_block, key_rows, value_rows, pair_segments)
    attended = attended.reshape(2 * sequence_length, half_width)
    attended = jnp.dot(attended, heads_to_gathered, preferred_element_type=jnp.float32).astype(
        NARROW
    )
    resid_parts = jnp.dot(attended, out_here, preferred_element_type=jnp.float32)
    resid = inputs + resid_parts[:sequence_length] + swap_core(resid_parts[sequence_length:])
    scale_two = norm_scale(resid)
    normed_two = (resid * scale_two * gain_moe).astype(NARROW)

    normed_blocks = gather_plane_last(normed_two)
    out_parts, back_parts, hidden, grad_gate, grad_upper = [], [], [], [], []
    for (near, away), (near_grad, away_grad) in zip(normed_blocks, cotangent_blocks):
        route = jnp.concatenate(
            [dense_route(g[:, MODEL_WIDTH:]) for g in (near_grad, away_grad)], 0
        )
        done = expert_block(
            near, away, near_grad, away_grad, route, gate_w, upper_w, down_w, local_experts
        )
        out_parts.append((done[0], done[1]))
        back_parts.append((done[2], done[3]))
        hidden.append(done[4])
        grad_gate.append(done[5])
        grad_upper.append(done[6])
    grad_normed_two = scatter_plane_first(back_parts)
    out_tokens = resid + scatter_plane_first(out_parts)

    rows_all = jnp.concatenate([half for pair in normed_blocks for half in pair], 0)
    grads_all = jnp.concatenate(
        [half[:, :MODEL_WIDTH] for pair in cotangent_blocks for half in pair], 0
    )
    over_rows = (((0,), (0,)), ((), ()))
    grad_down_parts = lax.dot_general(
        jnp.concatenate(hidden, 0), grads_all, over_rows, preferred_element_type=jnp.float32
    ).reshape(local_experts, 2, ff_columns // 2, MODEL_WIDTH)
    part_down = lax.dynamic_index_in_dim(grad_down_parts, core, 1, False) + swap_core(
        lax.dynamic_index_in_dim(grad_down_parts, 1 - core, 1, False)
    )
    sums = []
    for grads in (grad_gate, grad_upper):
        full = lax.dot_general(
            rows_all, jnp.concatenate(grads, 0), over_rows, preferred_element_type=jnp.float32
        ).reshape(chips, 2, plane_rows, share)
        theirs = swap_core(lax.dynamic_index_in_dim(full, 1 - core, 1, False).astype(NARROW))
        sums.append(lax.dynamic_index_in_dim(full, core, 1, False) + theirs.astype(WIDE))
    sums = jnp.stack(sums, 1).astype(NARROW)
    collected = jnp.zeros((chips, 2, plane_rows, share), NARROW)
    for other in range(chips):
        piece = lax.dynamic_index_in_dim(sums, chip ^ other, 0, False)
        if other:
            piece = swap(piece, lambda i, other=other: 2 * other)
        collected = lax.dynamic_update_slice(collected, piece[None], (chip ^ other, 0, 0, 0))
    part_gate_up = (
        collected.reshape(chips, 2, plane_rows, local_experts, ff_columns)
        .transpose(3, 2, 1, 0, 4)
        .reshape(local_experts, plane_rows, 2 * FF)
        .astype(WIDE)
    )

    hat_two = grad_normed_two * gain_moe
    grad_gain_moe = jnp.sum(grad_normed_two * resid * scale_two, 0)
    grad_resid = cotangent + scale_two * (
        hat_two - resid * scale_two**2 * jnp.mean(hat_two * resid, -1, keepdims=True)
    )
    grad_resid_half = grad_resid.astype(NARROW)
    pair_grads = jnp.concatenate([grad_resid_half, swap_core(grad_resid_half)], 0)
    grad_out = lax.dot_general(attended, pair_grads, over_rows, preferred_element_type=jnp.float32)
    attended_gradient = lax.dot_general(
        pair_grads, out_here, (((1,), (1,)), ((), ())), preferred_element_type=jnp.float32
    ).astype(NARROW)
    attended_gradient = (
        jnp.dot(attended_gradient, heads_from_gathered, preferred_element_type=jnp.float32)
        .astype(NARROW)
        .reshape(query_block.shape)
    )
    grad_query, grad_keys, grad_values = jax.vmap(attend_back)(
        query_block, key_rows, value_rows, pair_segments, logsums, attended_gradient
    )
    joined = jax.vmap(lambda a, b, c: join_grads(a, b, c, cosine_table, sine_table))(
        grad_query, grad_keys, grad_values
    ).reshape(2 * sequence_length, -1)
    grad_qkv = lax.dot_general(normed_one, joined, over_rows, preferred_element_type=jnp.float32)
    grad_normed_parts = lax.dot_general(
        joined, qkv_here, (((1,), (1,)), ((), ())), preferred_element_type=jnp.float32
    )
    grad_gain_attn = jnp.sum(grad_normed_parts * pair_gathered * scale_pair, 0)
    gain_parts = jnp.stack(
        [grad_gain_attn, select_columns(grad_gain_moe[None], to_gathered)[0]], 1
    )
    attention_parts = jnp.concatenate(
        [
            grad_qkv,
            jnp.pad(gain_parts, ((0, 0), (0, lane_pad - 2))),
            grad_out.reshape(-1, owned, 2, half_width)
            .transpose(0, 2, 1, 3)
            .reshape(MODEL_WIDTH, half_width),
        ],
        1,
    ).reshape(4, 2, 4 * owned, -1)
    summed = scatter_ring_middle(
        [(attention_parts[i, 0], attention_parts[i, 1].astype(NARROW)) for i in range(4)]
    )
    here, there = summed[:owned], summed[owned:]
    part_out = jnp.concatenate(
        [here[:, half_columns + lane_pad :], there[:, half_columns + lane_pad :]], 1
    )
    there = swap_core(there[:, : half_columns + lane_pad])
    part_gains = (
        here[:, half_columns : half_columns + 2] + there[:, half_columns : half_columns + 2]
    ).T
    here, there = here[:, :half_columns], there[:, :half_columns]
    part_qkv = join_parities(
        jnp.where(core == 0, here, there), jnp.where(core == 0, there, here)
    )

    grad_normed_parts = select_columns(grad_normed_parts, from_gathered)
    grad_normed_one = grad_normed_parts[:sequence_length] + swap_core(
        grad_normed_parts[sequence_length:]
    )
    hat_one = grad_normed_one * gains_placed[0]
    grad_tokens = grad_resid + scale_one * (
        hat_one - inputs * scale_one**2 * jnp.mean(hat_one * inputs, -1, keepdims=True)
    )

    new_qkv, new_first_qkv, new_second_qkv = adam_step(
        w_qkv, part_qkv, first_moment_projection, second_moment_projection, learn_rate, weight_decay
    )
    new_out, new_first_out, new_second_out = adam_step(
        w_out, part_out, first_out, second_out, out_rate, weight_decay
    )
    new_gains, new_first_gains, new_second_gains = adam_step(
        gains, part_gains, first_gains, second_gains, gain_rate, 0.0
    )
    new_gate_up, new_first_gate_up, new_second_gate_up = adam_step(
        w_gate_up, part_gate_up, first_gate_up, second_gate_up, learn_rate, weight_decay
    )
    new_down, new_first_down, new_second_down = adam_step(
        w_down, part_down, first_down, second_down, learn_rate, weight_decay
    )
    return (
        out_tokens,
        grad_tokens,
        part_qkv,
        part_out,
        part_gains,
        part_gate_up,
        part_down,
        new_qkv,
        new_out,
        new_gains,
        new_gate_up,
        new_down,
        new_first_qkv,
        new_first_out,
        new_first_gains,
        new_first_gate_up,
        new_first_down,
        new_second_qkv,
        new_second_out,
        new_second_gains,
        new_second_gate_up,
        new_second_down,
    )


def shards_plain(
    tokens,
    cotangent,
    segments,
    expert_ids,
    route_weights,
    w_qkv,
    w_out,
    gains,
    w_gate_up,
    w_down,
    first_moment_projection,
    first_out,
    first_gains,
    first_gate_up,
    first_down,
    second_moment_projection,
    second_out,
    second_gains,
    second_gate_up,
    second_down,
):
    sequence_count = segments.shape[0]
    sequence_length = segments.shape[1]
    groups_expert = lax.axis_size("expert")
    local_experts = EXPERTS // groups_expert
    slot_rows = groups_expert * CAP
    qkv_full, out_full, gain_full = (
        lax.all_gather(w_qkv.astype(jnp.bfloat16), ("dp", "expert"), axis=0, tiled=True),
        lax.all_gather(w_out.astype(jnp.bfloat16), ("dp", "expert"), axis=0, tiled=True),
        lax.all_gather(gains.astype(jnp.bfloat16), ("dp", "expert"), axis=1, tiled=True),
    )
    gate_up_full, down_full = (
        lax.all_gather(w_gate_up.astype(jnp.bfloat16), "dp", axis=1, tiled=True),
        lax.all_gather(w_down.astype(jnp.bfloat16), "dp", axis=1, tiled=True),
    )
    gain_attn = gain_full[0].astype(jnp.float32)
    gain_moe = gain_full[1].astype(jnp.float32)
    cosine_table, sine_table = rotary_tables(sequence_length, HEAD_SIZE // 2)
    inputs = tokens.astype(jnp.float32)
    scale_one = norm_scale(inputs)
    normed_one = (inputs * scale_one * gain_attn).astype(jnp.bfloat16)
    projected_rows = jnp.dot(normed_one, qkv_full, preferred_element_type=jnp.float32)
    query_block, key_rows, value_rows = split_heads(
        projected_rows, sequence_count, sequence_length, cosine_table, sine_table
    )
    index = 0
    attended_seq, logsum = attend(
        query_block[index], key_rows[index], value_rows[index], segments[index]
    )
    pieces = attended_seq.reshape(sequence_length, QUERY_HEADS * HEAD_SIZE)
    logsums = [logsum]
    resid = inputs + jnp.dot(pieces, out_full, preferred_element_type=jnp.float32)
    scale_two = norm_scale(resid)
    normed_two = (resid * scale_two * gain_moe).astype(jnp.bfloat16)
    flat_ids = expert_ids.reshape(-1)
    pair_count = flat_ids.shape[0]
    one_hot = (flat_ids[:, None] == jnp.arange(EXPERTS, dtype=jnp.int32)[None, :]).astype(jnp.int32)
    ranking = jnp.sum(jnp.cumsum(one_hot, 0) * one_hot, 1) - 1
    target = flat_ids * CAP + ranking
    owners = (
        jnp.full((EXPERTS * CAP,), -1, jnp.int32)
        .at[target]
        .set(jnp.arange(pair_count, dtype=jnp.int32))
    )
    filled = (owners >= 0)[:, None]
    safe_owner = jnp.maximum(owners, 0)
    send_rows = jnp.where(filled, normed_two[safe_owner // TOP], jnp.zeros((), jnp.bfloat16))
    received = lax.all_to_all(
        send_rows.reshape(groups_expert, local_experts, CAP, MODEL_WIDTH),
        "expert",
        split_axis=0,
        concat_axis=2,
        tiled=True,
    )
    received = received.reshape(local_experts, slot_rows, MODEL_WIDTH)
    mixed = jnp.einsum("erd,edf->erf", received, gate_up_full, preferred_element_type=jnp.float32)
    gate = mixed[..., :FF]
    upper = mixed[..., FF:]
    hidden = (jax.nn.silu(gate) * upper).astype(jnp.bfloat16)
    expert_out = jnp.einsum(
        "erf,efd->erd", hidden, down_full, preferred_element_type=jnp.float32
    ).astype(jnp.bfloat16)
    returned = lax.all_to_all(
        expert_out.reshape(1, local_experts, slot_rows, MODEL_WIDTH),
        "expert",
        split_axis=2,
        concat_axis=0,
        tiled=True,
    )
    picked = returned.reshape(EXPERTS * CAP, MODEL_WIDTH)[target].reshape(-1, TOP, MODEL_WIDTH)
    out_tokens = resid + jnp.sum(route_weights[..., None] * picked.astype(jnp.float32), 1)
    gate_up_back, down_back = (
        lax.all_gather(w_gate_up.astype(jnp.bfloat16), "dp", axis=1, tiled=True),
        lax.all_gather(w_down.astype(jnp.bfloat16), "dp", axis=1, tiled=True),
    )
    grad_routed = (
        (route_weights[..., None] * cotangent[:, None, :])
        .astype(jnp.bfloat16)
        .reshape(pair_count, MODEL_WIDTH)
    )
    send_grads = jnp.where(filled, grad_routed[safe_owner], jnp.zeros((), jnp.bfloat16))
    grad_expert = lax.all_to_all(
        send_grads.reshape(groups_expert, local_experts, CAP, MODEL_WIDTH),
        "expert",
        split_axis=0,
        concat_axis=2,
        tiled=True,
    )
    grad_expert = grad_expert.reshape(local_experts, slot_rows, MODEL_WIDTH)
    grad_hidden = jnp.einsum(
        "erd,efd->erf", grad_expert, down_back, preferred_element_type=jnp.float32
    )
    grad_down = jnp.einsum("erf,erd->efd", hidden, grad_expert, preferred_element_type=jnp.float32)
    sigma = jax.nn.sigmoid(gate)
    grad_mixed = jnp.concatenate(
        [grad_hidden * upper * sigma * (1.0 + gate * (1.0 - sigma)), grad_hidden * gate * sigma], -1
    ).astype(jnp.bfloat16)
    grad_gate_up = jnp.einsum(
        "erd,erf->edf", received, grad_mixed, preferred_element_type=jnp.float32
    )
    grad_received = jnp.einsum(
        "erf,edf->erd", grad_mixed, gate_up_back, preferred_element_type=jnp.float32
    ).astype(jnp.bfloat16)
    grad_back = lax.all_to_all(
        grad_received.reshape(1, local_experts, slot_rows, MODEL_WIDTH),
        "expert",
        split_axis=2,
        concat_axis=0,
        tiled=True,
    )
    grad_normed_two = jnp.sum(
        grad_back.reshape(EXPERTS * CAP, MODEL_WIDTH)[target]
        .reshape(-1, TOP, MODEL_WIDTH)
        .astype(jnp.float32),
        1,
    )
    hat_two = grad_normed_two * gain_moe
    grad_gain_moe = jnp.sum(grad_normed_two * resid * scale_two, 0)
    grad_resid = cotangent + scale_two * (
        hat_two - resid * scale_two**2 * jnp.mean(hat_two * resid, -1, keepdims=True)
    )
    grad_resid_half = grad_resid.astype(jnp.bfloat16)
    qkv_back, out_back = (
        lax.all_gather(w_qkv.astype(jnp.bfloat16), ("dp", "expert"), axis=0, tiled=True),
        lax.all_gather(w_out.astype(jnp.bfloat16), ("dp", "expert"), axis=0, tiled=True),
    )
    grad_out = jnp.dot(pieces.T, grad_resid_half, preferred_element_type=jnp.float32)
    attended_gradient = jnp.dot(
        grad_resid_half, out_back.T, preferred_element_type=jnp.float32
    ).astype(jnp.bfloat16)
    attended_gradient = attended_gradient.reshape(
        sequence_count, sequence_length, KEY_VALUE_HEADS, QUERY_HEADS // KEY_VALUE_HEADS, HEAD_SIZE
    )
    index = 0
    grad_query, grad_keys, grad_values = attend_back(
        query_block[index],
        key_rows[index],
        value_rows[index],
        segments[index],
        logsums[index],
        attended_gradient[index],
    )
    joined = join_grads(grad_query, grad_keys, grad_values, cosine_table, sine_table)
    grad_qkv = jnp.dot(normed_one.T, joined, preferred_element_type=jnp.float32)
    grad_normed_one = jnp.dot(joined, qkv_back.T, preferred_element_type=jnp.float32)
    hat_one = grad_normed_one * gain_attn
    grad_gain_attn = jnp.sum(grad_normed_one * inputs * scale_one, 0)
    grad_tokens = grad_resid + scale_one * (
        hat_one - inputs * scale_one**2 * jnp.mean(hat_one * inputs, -1, keepdims=True)
    )
    grad_gains = jnp.stack([grad_gain_attn, grad_gain_moe])
    part_qkv, part_out, part_gains = (
        lax.psum_scatter(grad_qkv, ("dp", "expert"), scatter_dimension=0, tiled=True),
        lax.psum_scatter(grad_out, ("dp", "expert"), scatter_dimension=0, tiled=True),
        lax.psum_scatter(grad_gains, ("dp", "expert"), scatter_dimension=1, tiled=True),
    )
    part_gate_up, part_down = (
        lax.psum_scatter(grad_gate_up, "dp", scatter_dimension=1, tiled=True),
        lax.psum_scatter(grad_down, "dp", scatter_dimension=1, tiled=True),
    )
    new_qkv, new_first_qkv, new_second_qkv = adam_step(
        w_qkv, part_qkv, first_moment_projection, second_moment_projection, learn_rate, weight_decay
    )
    new_out, new_first_out, new_second_out = adam_step(
        w_out, part_out, first_out, second_out, out_rate, weight_decay
    )
    new_gains, new_first_gains, new_second_gains = adam_step(
        gains, part_gains, first_gains, second_gains, gain_rate, 0.0
    )
    new_gate_up, new_first_gate_up, new_second_gate_up = adam_step(
        w_gate_up, part_gate_up, first_gate_up, second_gate_up, learn_rate, weight_decay
    )
    new_down, new_first_down, new_second_down = adam_step(
        w_down, part_down, first_down, second_down, learn_rate, weight_decay
    )
    return (
        out_tokens,
        grad_tokens,
        part_qkv,
        part_out,
        part_gains,
        part_gate_up,
        part_down,
        new_qkv,
        new_out,
        new_gains,
        new_gate_up,
        new_down,
        new_first_qkv,
        new_first_out,
        new_first_gains,
        new_first_gate_up,
        new_first_down,
        new_second_qkv,
        new_second_out,
        new_second_gains,
        new_second_gate_up,
        new_second_down,
    )


def solution(mesh):
    by_heads = mesh.shape["dp"] == KEY_VALUE_HEADS and mesh.shape["expert"] == 4
    return jax.shard_map(
        shards_moved if by_heads else shards_plain,
        mesh=mesh,
        in_specs=(
            P(("dp", "expert"), None),
            P(("dp", "expert"), None),
            P(("dp", "expert"), None),
            P(("dp", "expert"), None),
            P(("dp", "expert"), None),
            P(("dp", "expert"), None),
            P(("dp", "expert"), None),
            P(None, ("dp", "expert")),
            P("expert", "dp", None),
            P("expert", "dp", None),
            P(("dp", "expert"), None),
            P(("dp", "expert"), None),
            P(None, ("dp", "expert")),
            P("expert", "dp", None),
            P("expert", "dp", None),
            P(("dp", "expert"), None),
            P(("dp", "expert"), None),
            P(None, ("dp", "expert")),
            P("expert", "dp", None),
            P("expert", "dp", None),
        ),
        out_specs=(
            P(("dp", "expert"), None),
            P(("dp", "expert"), None),
            P(("dp", "expert"), None),
            P(("dp", "expert"), None),
            P(None, ("dp", "expert")),
            P("expert", "dp", None),
            P("expert", "dp", None),
            P(("dp", "expert"), None),
            P(("dp", "expert"), None),
            P(None, ("dp", "expert")),
            P("expert", "dp", None),
            P("expert", "dp", None),
            P(("dp", "expert"), None),
            P(("dp", "expert"), None),
            P(None, ("dp", "expert")),
            P("expert", "dp", None),
            P("expert", "dp", None),
            P(("dp", "expert"), None),
            P(("dp", "expert"), None),
            P(None, ("dp", "expert")),
            P("expert", "dp", None),
            P("expert", "dp", None),
        ),
        check_vma=False,
    )
```

```python
import functools

import jax
import jax.numpy as jnp
import numpy as np
from jax import lax
from jax.experimental import pallas as pl
from jax.experimental.pallas import tpu as pltpu
from jax.sharding import PartitionSpec as P

MODEL_WIDTH = 1536
QUERY_HEADS = 24
KEY_VALUE_HEADS = 8
HEAD_SIZE = 64
FF = 512
EXPERTS = 40
TOP = 8
CAP = 32


eps_norm = 1e-05
beta_one = 0.9
beta_two = 0.95
adam_eps = 1e-08
learn_rate = 0.01
out_rate = 0.04
gain_rate = 0.2
weight_decay = 0.1
correct_one = 1.0 - beta_one**3
correct_two = 1.0 - beta_two**3


def norm_scale(rows):
    return lax.rsqrt(jnp.mean(rows * rows, -1, keepdims=True) + eps_norm)


def rotary_tables(sequence_length, half_dim):
    position = jnp.arange(sequence_length, dtype=jnp.float32)[:, None]
    frequency = 10000.0 ** (-jnp.arange(half_dim, dtype=jnp.float32) / half_dim)
    angles = position * frequency[None, :]
    return (jnp.cos(angles), jnp.sin(angles))


def apply_rotary(value_rows, cosine_table, sine_table, middle):
    half_dim = value_rows.shape[-1] // 2
    shape = (cosine_table.shape[0],) + (1,) * middle + (half_dim,)
    cosine_table = cosine_table.reshape(shape)
    sine_table = sine_table.reshape(shape)
    first = value_rows[..., :half_dim]
    second = value_rows[..., half_dim:]
    return jnp.concatenate(
        [first * cosine_table - second * sine_table, second * cosine_table + first * sine_table], -1
    )


def split_heads(projected_rows, sequence_count, sequence_length, cosine_table, sine_table):
    query_total_width = QUERY_HEADS * HEAD_SIZE
    key_columns_width = KEY_VALUE_HEADS * HEAD_SIZE
    reshaped_rows = projected_rows.reshape(sequence_count, sequence_length, -1)
    query_block = apply_rotary(
        reshaped_rows[..., :query_total_width].reshape(
            sequence_count,
            sequence_length,
            KEY_VALUE_HEADS,
            QUERY_HEADS // KEY_VALUE_HEADS,
            HEAD_SIZE,
        ),
        cosine_table,
        sine_table,
        2,
    )
    key_rows = apply_rotary(
        reshaped_rows[..., query_total_width : query_total_width + key_columns_width].reshape(
            sequence_count, sequence_length, KEY_VALUE_HEADS, HEAD_SIZE
        ),
        cosine_table,
        sine_table,
        1,
    )
    value_rows = reshaped_rows[..., query_total_width + key_columns_width :].reshape(
        sequence_count, sequence_length, KEY_VALUE_HEADS, HEAD_SIZE
    )
    return (
        query_block.astype(jnp.bfloat16),
        key_rows.astype(jnp.bfloat16),
        value_rows.astype(jnp.bfloat16),
    )


def allowed_mask(segment):
    spots = jnp.arange(segment.shape[0])
    return (spots[:, None] >= spots[None, :]) & (segment[:, None] == segment[None, :])


def score_block(query_block, key_rows, segment):
    scores = jnp.einsum(
        "qhgd,khd->hgqk", query_block, key_rows, preferred_element_type=jnp.float32
    ) * query_block.shape[-1] ** (-0.5)
    return jnp.where(allowed_mask(segment)[None, None], scores, -1e30)


def attend(query_block, key_rows, value_rows, segment):
    scores = score_block(query_block, key_rows, segment)
    highest = jnp.max(scores, -1, keepdims=True)
    logsum = highest + jnp.log(jnp.sum(jnp.exp(scores - highest), -1, keepdims=True))
    probs = jnp.exp(scores - logsum).astype(jnp.bfloat16)
    attended = jnp.einsum("hgqk,khd->qhgd", probs, value_rows, preferred_element_type=jnp.float32)
    return (attended.astype(jnp.bfloat16), logsum)


def attend_back(query_block, key_rows, value_rows, segment, logsum, attended_gradient):
    factor = query_block.shape[-1] ** (-0.5)
    probs = jnp.exp(score_block(query_block, key_rows, segment) - logsum)
    grad_probs = jnp.einsum(
        "qhgd,khd->hgqk", attended_gradient, value_rows, preferred_element_type=jnp.float32
    )
    inner_sum = jnp.sum(probs * grad_probs, -1, keepdims=True)
    grad_scores = (probs * (grad_probs - inner_sum) * factor).astype(jnp.bfloat16)
    grad_values = jnp.einsum(
        "hgqk,qhgd->khd",
        probs.astype(jnp.bfloat16),
        attended_gradient,
        preferred_element_type=jnp.float32,
    )
    grad_query = jnp.einsum(
        "hgqk,khd->qhgd", grad_scores, key_rows, preferred_element_type=jnp.float32
    )
    grad_keys = jnp.einsum(
        "hgqk,qhgd->khd", grad_scores, query_block, preferred_element_type=jnp.float32
    )
    return (grad_query, grad_keys, grad_values)


def join_grads(grad_query, grad_keys, grad_values, cosine_table, sine_table):
    sequence_length = grad_query.shape[0]
    grad_query = apply_rotary(grad_query, cosine_table, -sine_table, 2).reshape(sequence_length, -1)
    grad_keys = apply_rotary(grad_keys, cosine_table, -sine_table, 1).reshape(sequence_length, -1)
    return jnp.concatenate(
        [grad_query, grad_keys, grad_values.reshape(sequence_length, -1)], -1
    ).astype(jnp.bfloat16)


def adam_step(weight, grad, first, second, step_rate, shrink):
    first = beta_one * first + (1.0 - beta_one) * grad
    second = beta_two * second + (1.0 - beta_two) * grad * grad
    update = first / correct_one / (jnp.sqrt(second / correct_two) + adam_eps)
    return (weight - step_rate * (update + shrink * weight), first, second)


NARROW = jnp.bfloat16
WIDE = jnp.float32
DISTANCE = (0, 1, -1, 2)
HOP_CORE, HOP_X, HOP_Y = 1, 2, 4


def swap(rows, pick):
    count = lax.axis_size("dp")
    return lax.ppermute(rows, "dp", [(i, i ^ pick(i)) for i in range(count)])


def first_hop(i):
    return HOP_X if i & 1 else HOP_Y


def second_hop(i):
    return HOP_Y if i & 1 else HOP_X


def swap_core(rows):
    return swap(rows, lambda i: HOP_CORE)


def swap_first(rows):
    return swap(rows, first_hop)


def swap_second(rows):
    return swap(rows, second_hop)


def turn(rows, step):
    count = lax.axis_size("expert")
    return lax.ppermute(rows, "expert", [(i, (i + step) % count) for i in range(count)])


def gather_plane_last(block):
    ahead, behind = turn(block, 1), turn(block, -1)
    found = []
    for part in (block, ahead, behind, turn(ahead, 1)):
        pair = jnp.concatenate([part, swap_first(part)], 0)
        found.append((pair, swap_second(pair)))
    return found


def gather_ring_middle(block):
    pair = jnp.concatenate([block, swap_first(block)], 0)
    ahead, behind = turn(pair, 1), turn(pair, -1)
    return [(part, swap_second(part)) for part in (pair, ahead, behind, turn(ahead, 1))]


def ring_sum(parts):
    far = turn(parts[3].astype(NARROW), -1)
    ahead = turn((parts[1] + far.astype(WIDE)).astype(NARROW), -1)
    behind = turn(parts[2].astype(NARROW), 1)
    return parts[0] + ahead.astype(WIDE) + behind.astype(WIDE)


def scatter_plane_first(parts):
    found = [None] * 4
    for spot in (3, 1, 2, 0):
        near, away = parts[spot]
        near = near + swap_second(away).astype(WIDE)
        half = near.shape[0] // 2
        found[spot] = near[:half] + swap_first(near[half:].astype(NARROW)).astype(WIDE)
    return ring_sum(found)


def scatter_ring_middle(parts):
    found = [None] * 4
    for spot in (3, 1, 2, 0):
        near, away = parts[spot]
        found[spot] = near + swap_second(away).astype(WIDE)
    total = ring_sum(found)
    half = total.shape[0] // 2
    return total[:half] + swap_first(total[half:].astype(NARROW)).astype(WIDE)


def gathered_sources(count_dp, count_expert):
    table = np.zeros((count_dp, count_expert, 4, 2, 2, 2), np.int32)
    for i in range(count_dp):
        for z in range(count_expert):
            for spot, distance in enumerate(DISTANCE):
                for second in range(2):
                    for first in range(2):
                        plane = i ^ (first_hop(i) * first) ^ (second_hop(i) * second)
                        table[i, z, spot, second, first] = plane, (z - distance) % count_expert
    return table.reshape(count_dp, count_expert, 16, 2)


def split_three(values):
    high = values.astype(NARROW)
    left = values - high.astype(WIDE)
    middle = left.astype(NARROW)
    return [high, middle, (left - middle.astype(WIDE)).astype(NARROW)]


def select_columns(values, chosen):
    rows = values.shape[0]
    parts = jnp.dot(
        jnp.concatenate(split_three(values), 0), chosen, preferred_element_type=jnp.float32
    )
    return parts[:rows] + parts[rows : 2 * rows] + parts[2 * rows :]


def parity_columns(rows, parity):
    count = rows.shape[0]
    query_total_width = QUERY_HEADS * HEAD_SIZE
    key_columns_width = KEY_VALUE_HEADS * HEAD_SIZE
    bounds = (
        (0, query_total_width),
        (query_total_width, query_total_width + key_columns_width),
        (query_total_width + key_columns_width, query_total_width + 2 * key_columns_width),
    )
    return jnp.concatenate(
        [
            rows[:, low:high].reshape(count, KEY_VALUE_HEADS // 2, 2, -1)[:, :, parity]
            .reshape(count, -1)
            for low, high in bounds
        ],
        1,
    )


def join_parities(even, odd):
    count = even.shape[0]
    query_half = QUERY_HEADS * HEAD_SIZE // 2
    key_half = KEY_VALUE_HEADS * HEAD_SIZE // 2
    bounds = (
        (0, query_half),
        (query_half, query_half + key_half),
        (query_half + key_half, query_half + 2 * key_half),
    )
    heads = KEY_VALUE_HEADS // 2
    return jnp.concatenate(
        [
            jnp.stack(
                [
                    even[:, low:high].reshape(count, heads, -1),
                    odd[:, low:high].reshape(count, heads, -1),
                ],
                2,
            ).reshape(count, -1)
            for low, high in bounds
        ],
        1,
    )


def split_head_group(projected_rows, cosine_table, sine_table):
    sequences, length = projected_rows.shape[:2]
    heads = KEY_VALUE_HEADS // 2
    group = QUERY_HEADS // KEY_VALUE_HEADS
    query_width = heads * group * HEAD_SIZE
    key_width = heads * HEAD_SIZE
    query_block = projected_rows[..., :query_width].reshape(
        sequences, length, heads, group, HEAD_SIZE
    )
    key_rows = projected_rows[..., query_width : query_width + key_width].reshape(
        sequences, length, heads, HEAD_SIZE
    )
    value_rows = projected_rows[..., query_width + key_width :].reshape(
        sequences, length, heads, HEAD_SIZE
    )
    query_block = jax.vmap(lambda a: apply_rotary(a, cosine_table, sine_table, 2))(query_block)
    key_rows = jax.vmap(lambda a: apply_rotary(a, cosine_table, sine_table, 1))(key_rows)
    return (
        query_block.astype(jnp.bfloat16),
        key_rows.astype(jnp.bfloat16),
        value_rows.astype(jnp.bfloat16),
    )


def spread_columns_kernel(place_ref, weight_ref, *out_refs):
    lanes = out_refs[0].shape[2]
    for other, out_ref in enumerate(out_refs):
        start = pl.multiple_of((place_ref[0] ^ other) * lanes, lanes)
        for part in range(2):
            out_ref[part] = weight_ref[0, :, pl.ds(part * FF + start, lanes)].astype(out_ref.dtype)


def spread_columns(place, weight, chips):
    experts, rows, both = weight.shape
    lanes = both // 2 // chips
    return pl.pallas_call(
        spread_columns_kernel,
        grid_spec=pltpu.PrefetchScalarGridSpec(
            num_scalar_prefetch=1,
            grid=(experts,),
            in_specs=[pl.BlockSpec((1, rows, both), lambda e, place: (e, 0, 0))],
            out_specs=[pl.BlockSpec((2, rows, lanes), lambda e, place: (0, 0, e))] * chips,
        ),
        out_shape=[jax.ShapeDtypeStruct((2, rows, experts * lanes), jnp.bfloat16)] * chips,
        cost_estimate=pl.CostEstimate(
            flops=0, bytes_accessed=6 * experts * rows * both, transcendentals=0
        ),
    )(place, weight)


def stack_rows_kernel(place_ref, *refs):
    pieces, (gate_ref, upper_ref, sems) = refs[:-3], refs[-3:]
    chip, core = place_ref[0], place_ref[1]
    chips = len(pieces) // 2
    rows = pieces[0].shape[1]
    copies = []
    for other in range(chips):
        for mate in range(2):
            start = pl.multiple_of(((chip ^ other) * 2 + (core ^ mate)) * rows, rows)
            for part, out_ref in enumerate((gate_ref, upper_ref)):
                copies.append(
                    pltpu.make_async_copy(
                        pieces[mate * chips + other].at[part],
                        out_ref.at[pl.ds(start, rows), :],
                        sems.at[len(copies)],
                    )
                )
    for copy in copies:
        copy.start()
    for copy in copies:
        copy.wait()


def stack_rows(place, pieces):
    _, rows, columns = pieces[0].shape
    shape = jax.ShapeDtypeStruct((rows * len(pieces), columns), jnp.bfloat16)
    return pl.pallas_call(
        stack_rows_kernel,
        in_specs=[pl.BlockSpec(memory_space=pltpu.SMEM)]
        + [pl.BlockSpec(memory_space=pl.ANY)] * len(pieces),
        out_specs=[pl.BlockSpec(memory_space=pl.ANY)] * 2,
        out_shape=[shape] * 2,
        scratch_shapes=[pltpu.SemaphoreType.DMA((2 * len(pieces),))],
        cost_estimate=pl.CostEstimate(
            flops=0, bytes_accessed=8 * len(pieces) * rows * columns, transcendentals=0
        ),
    )(place, *pieces)


def stack_attention_kernel(*refs):
    blocks, (qkv_ref, gain_ref, out_ref, sems) = refs[:-4], refs[-4:]
    wide, lanes = qkv_ref.shape[1], gain_ref.shape[1]
    owned = out_ref.shape[0] // (2 * len(blocks))
    copies = []
    for i, block in enumerate(blocks):
        for j in range(2):
            top, spot = 3 * owned * j, 2 * i + j
            pairs = (
                (
                    block.at[pl.ds(top, 2 * owned), pl.ds(0, wide)],
                    qkv_ref.at[pl.ds(2 * owned * spot, 2 * owned), :],
                ),
                (
                    block.at[pl.ds(top, 2 * owned), pl.ds(wide, lanes)],
                    gain_ref.at[pl.ds(2 * owned * spot, 2 * owned), :],
                ),
                (
                    block.at[pl.ds(top + 2 * owned, owned), :],
                    out_ref.at[pl.ds(owned * spot, owned), :],
                ),
            )
            for source, target in pairs:
                copies.append(pltpu.make_async_copy(source, target, sems.at[len(copies)]))
    for copy in copies:
        copy.start()
    for copy in copies:
        copy.wait()


def stack_attention(blocks, wide, lanes):
    owned = blocks[0].shape[0] // 6
    count = 2 * len(blocks)
    b16 = lambda r, c: jax.ShapeDtypeStruct((r, c), jnp.bfloat16)
    return pl.pallas_call(
        stack_attention_kernel,
        in_specs=[pl.BlockSpec(memory_space=pl.ANY)] * len(blocks),
        out_specs=[pl.BlockSpec(memory_space=pl.ANY)] * 3,
        out_shape=[
            b16(2 * owned * count, wide),
            b16(2 * owned * count, lanes),
            b16(owned * count, blocks[0].shape[1]),
        ],
        scratch_shapes=[pltpu.SemaphoreType.DMA((3 * count,))],
        cost_estimate=pl.CostEstimate(
            flops=0, bytes_accessed=4 * 3 * owned * count * MODEL_WIDTH, transcendentals=0
        ),
    )(*blocks)


def attention_grads_kernel(
    normed_ref, joined_ref, attended_ref, grads_ref, gain_ref, near_ref, away_ref
):
    contract = (((0,), (0,)), ((), ()))
    wide, lanes = joined_ref.shape[1], gain_ref.shape[1]
    spots = near_ref.shape[0]
    owned = near_ref.shape[1] // 6
    joined, grads = joined_ref[...], grads_ref[...]

    def place(spot, second, first, row, columns, values):
        rows = pl.ds(3 * owned * first + row, values.shape[0])
        if second:
            away_ref[spot, rows, columns] = values.astype(away_ref.dtype)
        else:
            near_ref[spot, rows, columns] = values

    for spot in range(spots):
        rows = 8 * owned
        qkv = lax.dot_general(
            normed_ref[:, rows * spot : rows * (spot + 1)],
            joined,
            contract,
            preferred_element_type=jnp.float32,
        )
        for i in range(4):
            part = slice(2 * owned * i, 2 * owned * (i + 1))
            place(spot, i // 2, i % 2, 0, pl.ds(0, wide), qkv[part])
            gain = gain_ref[pl.ds(rows * spot + 2 * owned * i, 2 * owned), :]
            place(spot, i // 2, i % 2, 0, pl.ds(wide, lanes), gain)
            place(spot, i // 2, i % 2, 0, pl.ds(wide + lanes, lanes), jnp.zeros_like(gain))
        if spot % 2 == 0:
            out = lax.dot_general(
                attended_ref[:, 4 * owned * spot : 4 * owned * (spot + 2)],
                grads,
                contract,
                preferred_element_type=jnp.float32,
            )
            for i in range(8):
                part = slice(owned * i, owned * (i + 1))
                place(
                    spot + i // 4,
                    i // 2 % 2,
                    i % 2,
                    2 * owned,
                    pl.ds(0, out.shape[1]),
                    out[part],
                )


def attention_grads(normed, joined, attended, grads, gain, owned):
    spots = len(DISTANCE)
    shape = (spots, 6 * owned, grads.shape[1])
    return pl.pallas_call(
        attention_grads_kernel,
        out_shape=[
            jax.ShapeDtypeStruct(shape, jnp.float32),
            jax.ShapeDtypeStruct(shape, jnp.bfloat16),
        ],
        compiler_params=pltpu.CompilerParams(vmem_limit_bytes=44 * 1024 * 1024),
        cost_estimate=pl.CostEstimate(
            flops=2 * normed.shape[0] * normed.shape[1] * (joined.shape[1] + grads.shape[1] // 2),
            bytes_accessed=20 * 1024 * 1024,
            transcendentals=0,
        ),
    )(normed, joined, attended, grads, gain)


def expert_kernel(
    near_ref,
    away_ref,
    near_grad_ref,
    away_grad_ref,
    route_ref,
    gate_ref,
    upper_ref,
    down_ref,
    *refs,
    per_step,
):
    near_out_ref, away_out_ref, near_back_ref, away_back_ref = refs[-13:-9]
    hidden_ref, grad_gate_ref, grad_upper_ref, rows_all_ref, grads_all_ref = refs[-9:-4]
    rows_ref, grads_ref, out_ref, back_ref = refs[-4:]
    step = pl.program_id(0)
    half = near_ref.shape[0]
    width = near_ref.shape[1]

    @pl.when(step == 0)
    def _():
        rows_ref[:half, :] = near_ref[...]
        rows_ref[half:, :] = away_ref[...]
        grads_ref[:half, :] = near_grad_ref[:, :width]
        grads_ref[half:, :] = away_grad_ref[:, :width]
        rows_all_ref[...] = rows_ref[...]
        grads_all_ref[...] = grads_ref[...]
        out_ref[...] = jnp.zeros_like(out_ref)
        back_ref[...] = jnp.zeros_like(back_ref)

    rows = rows_ref[...]
    grads = grads_ref[...]
    contract_last = (((1,), (1,)), ((), ()))
    gate = jnp.dot(rows, gate_ref[...], preferred_element_type=jnp.float32)
    upper = jnp.dot(rows, upper_ref[...], preferred_element_type=jnp.float32)
    grad_hidden = lax.dot_general(
        grads, down_ref[...], contract_last, preferred_element_type=jnp.float32
    )
    route = route_ref[...]
    lanes = lax.broadcasted_iota(jnp.int32, route.shape, 1)
    columns = gate.shape[1] // per_step
    spread = []
    for i in range(per_step):
        one = jnp.sum(jnp.where(lanes == step * per_step + i, route, 0.0), 1, keepdims=True)
        spread.append(jnp.broadcast_to(one, (route.shape[0], columns)))
    weight = jnp.concatenate(spread, 1)
    sigma = 1.0 / (1.0 + jnp.exp(-gate))
    active = gate * sigma
    hidden = (weight * active * upper).astype(jnp.bfloat16)
    weighted = weight * grad_hidden
    grad_gate = (weighted * upper * sigma * (1.0 + gate * (1.0 - sigma))).astype(jnp.bfloat16)
    grad_upper = (weighted * active).astype(jnp.bfloat16)
    hidden_ref[...] = hidden
    grad_gate_ref[...] = grad_gate
    grad_upper_ref[...] = grad_upper
    out_ref[...] += jnp.dot(hidden, down_ref[...], preferred_element_type=jnp.float32)
    back_ref[...] += lax.dot_general(
        grad_gate, gate_ref[...], contract_last, preferred_element_type=jnp.float32
    ) + lax.dot_general(
        grad_upper, upper_ref[...], contract_last, preferred_element_type=jnp.float32
    )

    @pl.when(step == pl.num_programs(0) - 1)
    def _():
        near_out_ref[...] = out_ref[:half, :]
        away_out_ref[...] = out_ref[half:, :].astype(jnp.bfloat16)
        near_back_ref[...] = back_ref[:half, :]
        away_back_ref[...] = back_ref[half:, :].astype(jnp.bfloat16)


def expert_block(spot, near, away, near_grad, away_grad, route, weights, experts, filled):
    gate_w, upper_w, down_w = weights
    half, width = near.shape
    total = gate_w.shape[1]
    per_step = 2
    steps = experts // per_step
    columns = total // steps
    whole = lambda a: pl.BlockSpec(a.shape, lambda i: (0, 0))
    rows = 2 * half
    every = rows * len(DISTANCE)
    f32 = lambda r, c: jax.ShapeDtypeStruct((r, c), jnp.float32)
    b16 = lambda r, c: jax.ShapeDtypeStruct((r, c), jnp.bfloat16)
    fixed = pl.BlockSpec((half, width), lambda i: (0, 0))
    part = pl.BlockSpec((rows, columns), lambda i: (spot, i))
    kept = pl.BlockSpec((rows, width), lambda i: (spot, 0))
    flops = 2 * rows * width * total * 6
    inputs = (near, away, near_grad, away_grad, route, gate_w, upper_w, down_w)
    return pl.pallas_call(
        functools.partial(expert_kernel, per_step=per_step),
        grid=(steps,),
        in_specs=[
            whole(near),
            whole(away),
            whole(near_grad),
            whole(away_grad),
            whole(route),
            pl.BlockSpec((width, columns), lambda i: (0, i)),
            pl.BlockSpec((width, columns), lambda i: (0, i)),
            pl.BlockSpec((columns, width), lambda i: (i, 0)),
        ]
        + [pl.BlockSpec(memory_space=pl.ANY)] * len(filled),
        out_specs=[fixed] * 4 + [part] * 3 + [kept] * 2,
        out_shape=[f32(half, width), b16(half, width)] * 2
        + [b16(every, total)] * 3
        + [b16(every, width)] * 2,
        input_output_aliases={len(inputs) + i: 4 + i for i in range(len(filled))},
        scratch_shapes=[
            pltpu.VMEM((rows, width), jnp.bfloat16),
            pltpu.VMEM((rows, width), jnp.bfloat16),
            pltpu.VMEM((rows, width), jnp.float32),
            pltpu.VMEM((rows, width), jnp.float32),
        ],
        compiler_params=pltpu.CompilerParams(vmem_limit_bytes=48 * 1024 * 1024),
        cost_estimate=pl.CostEstimate(
            flops=flops,
            bytes_accessed=2 * (3 * width * total + 3 * rows * total + 12 * rows * width),
            transcendentals=rows * total,
        ),
    )(*inputs, *filled)


def expert_grads_kernel(
    place_ref,
    rows_ref,
    grads_ref,
    hidden_ref,
    grad_gate_ref,
    grad_upper_ref,
    keep_ref,
    give_ref,
    keep_down_ref,
    give_down_ref,
    full_ref,
    full_down_ref,
):
    core = place_ref[1]
    contract = (((0,), (0,)), ((), ()))
    chips, _, plane_rows, _ = keep_ref.shape
    for part, ref in enumerate((grad_gate_ref, grad_upper_ref)):
        full_ref[...] = lax.dot_general(
            rows_ref[...], ref[...], contract, preferred_element_type=jnp.float32
        )
        for chip in range(chips):
            mine = pl.multiple_of((2 * chip + core) * plane_rows, plane_rows)
            theirs = pl.multiple_of((2 * chip + 1 - core) * plane_rows, plane_rows)
            keep_ref[chip, part] = full_ref[pl.ds(mine, plane_rows), :]
            give_ref[chip, part] = full_ref[pl.ds(theirs, plane_rows), :].astype(give_ref.dtype)
    full_down_ref[...] = lax.dot_general(
        hidden_ref[...], grads_ref[...], contract, preferred_element_type=jnp.float32
    )
    experts, down_rows, _ = keep_down_ref.shape
    for e in range(experts):
        mine = pl.multiple_of((2 * e + core) * down_rows, down_rows)
        theirs = pl.multiple_of((2 * e + 1 - core) * down_rows, down_rows)
        keep_down_ref[e] = full_down_ref[pl.ds(mine, down_rows), :]
        give_down_ref[e] = full_down_ref[pl.ds(theirs, down_rows), :]


def expert_grads(place, rows_all, grads_all, hidden, grad_gate, grad_upper, experts, chips):
    tokens, width = rows_all.shape
    total = hidden.shape[1]
    per_step = 2
    steps = experts // per_step
    columns = total // steps
    plane_rows = width // (2 * chips)
    down_rows = total // experts // 2
    whole = pl.BlockSpec((tokens, width), lambda i, p: (0, 0), pipeline_mode=pl.Buffered(1))
    part = pl.BlockSpec((tokens, columns), lambda i, p: (0, i))
    wide = pl.BlockSpec((chips, 2, plane_rows, columns), lambda i, p: (0, 0, 0, i))
    down = pl.BlockSpec((per_step, down_rows, width), lambda i, p: (i, 0, 0))
    return pl.pallas_call(
        expert_grads_kernel,
        grid_spec=pltpu.PrefetchScalarGridSpec(
            num_scalar_prefetch=1,
            grid=(steps,),
            in_specs=[whole, whole, part, part, part],
            out_specs=[wide, wide, down, down],
            scratch_shapes=[
                pltpu.VMEM((width, columns), jnp.float32),
                pltpu.VMEM((columns, width), jnp.float32),
            ],
        ),
        out_shape=[
            jax.ShapeDtypeStruct((chips, 2, plane_rows, total), jnp.float32),
            jax.ShapeDtypeStruct((chips, 2, plane_rows, total), jnp.bfloat16),
            jax.ShapeDtypeStruct((experts, down_rows, width), jnp.float32),
            jax.ShapeDtypeStruct((experts, down_rows, width), jnp.float32),
        ],
        compiler_params=pltpu.CompilerParams(vmem_limit_bytes=52 * 1024 * 1024),
        cost_estimate=pl.CostEstimate(
            flops=6 * tokens * width * total,
            bytes_accessed=2 * tokens * (2 * width + 3 * total) + 20 * width * total,
            transcendentals=0,
        ),
    )(place, rows_all, grads_all, hidden, grad_gate, grad_upper)


def adam_columns_kernel(place_ref, w_ref, first_ref, second_ref, *refs):
    pieces, outs = refs[:-4], refs[-4:]
    lanes = pieces[0].shape[2]
    for other, piece in enumerate(pieces):
        start = pl.multiple_of((place_ref[0] ^ other) * lanes, lanes)
        for part in range(2):
            columns = pl.ds(part * FF + start, lanes)
            grad = piece[part].astype(jnp.float32)
            found = adam_step(
                w_ref[0, :, columns],
                grad,
                first_ref[0, :, columns],
                second_ref[0, :, columns],
                learn_rate,
                weight_decay,
            )
            for out_ref, value in zip(outs, (grad,) + found):
                out_ref[0, :, columns] = value


def adam_columns(place, weight, first, second, pieces):
    experts, rows, both = weight.shape
    lanes = pieces[0].shape[2] // experts
    block = pl.BlockSpec((1, rows, both), lambda e, p: (e, 0, 0))
    return pl.pallas_call(
        adam_columns_kernel,
        grid_spec=pltpu.PrefetchScalarGridSpec(
            num_scalar_prefetch=1,
            grid=(experts,),
            in_specs=[block] * 3
            + [pl.BlockSpec((2, rows, lanes), lambda e, p: (0, 0, e))] * len(pieces),
            out_specs=[block] * 4,
        ),
        out_shape=[jax.ShapeDtypeStruct(weight.shape, jnp.float32)] * 4,
        compiler_params=pltpu.CompilerParams(vmem_limit_bytes=32 * 1024 * 1024),
        cost_estimate=pl.CostEstimate(
            flops=20 * experts * rows * both,
            bytes_accessed=30 * experts * rows * both,
            transcendentals=experts * rows * both,
        ),
    )(place, weight, first, second, *pieces)


def shards_moved(
    tokens,
    cotangent,
    segments,
    expert_ids,
    route_weights,
    w_qkv,
    w_out,
    gains,
    w_gate_up,
    w_down,
    first_moment_projection,
    first_out,
    first_gains,
    first_gate_up,
    first_down,
    second_moment_projection,
    second_out,
    second_gains,
    second_gate_up,
    second_down,
):
    sequence_length = segments.shape[1]
    count_dp, count_expert = lax.axis_size("dp"), lax.axis_size("expert")
    place_dp, place_expert = lax.axis_index("dp"), lax.axis_index("expert")
    core = place_dp % 2
    chip = place_dp // 2
    chips = count_dp // 2
    local_experts = EXPERTS // count_expert
    owned = w_qkv.shape[0]
    half_columns = w_qkv.shape[1] // 2
    half_width = MODEL_WIDTH // 2
    lane_pad = 128

    narrow_qkv = w_qkv.astype(NARROW)
    even_columns, odd_columns = parity_columns(narrow_qkv, 0), parity_columns(narrow_qkv, 1)
    gain_columns = jnp.pad(gains.astype(NARROW).T, ((0, 0), (0, lane_pad - 2)))
    kept = jnp.where(core == 0, even_columns, odd_columns)
    given = jnp.where(core == 0, odd_columns, even_columns)
    rest = jnp.zeros((owned, MODEL_WIDTH - half_columns - lane_pad), NARROW)
    taken = swap_core(jnp.concatenate([given, gain_columns], 1))
    block = jnp.concatenate(
        [
            jnp.concatenate([kept, gain_columns, rest], 1),
            jnp.concatenate([taken, rest], 1),
            w_out.astype(NARROW),
        ],
        0,
    )
    attention_blocks = gather_ring_middle(block)

    sources = jnp.asarray(gathered_sources(count_dp, count_expert))[place_dp, place_expert]
    from_dp, from_expert = sources[:, 0], sources[:, 1]
    row_in = jnp.arange(owned, dtype=jnp.int32)
    feature = (
        ((from_dp[:, None] ^ jnp.arange(2, dtype=jnp.int32)[None, :]) * count_expert
         + from_expert[:, None])[:, :, None] * owned + row_in
    ).reshape(-1)
    head_feature = (
        ((from_dp // 2 * count_expert + from_expert) * owned)[:, None] + row_in
    ).reshape(-1)
    places = jnp.arange(MODEL_WIDTH, dtype=jnp.int32)
    to_gathered = (places[:, None] == feature[None, :]).astype(NARROW)
    from_gathered = (feature[:, None] == places[None, :]).astype(NARROW)
    head_places = places[: half_width]
    heads_to_gathered = (head_places[:, None] == head_feature[None, :]).astype(NARROW)
    heads_from_gathered = (head_feature[:, None] == head_places[None, :]).astype(NARROW)

    ff_columns = FF // chips

    share = local_experts * ff_columns
    place = jnp.stack([chip, core]).astype(jnp.int32)
    pieces = spread_columns(place, w_gate_up, chips)
    pieces = [
        swap(piece, lambda i, other=other: 2 * other) if other else piece
        for other, piece in enumerate(pieces)
    ]
    gate_w, upper_w = stack_rows(place, pieces + [swap_core(piece) for piece in pieces])
    down_mine = w_down.astype(NARROW)
    down_theirs = swap_core(down_mine)
    down_w = jnp.where(
        core == 0,
        jnp.concatenate([down_mine, down_theirs], 1),
        jnp.concatenate([down_theirs, down_mine], 1),
    ).reshape(share, MODEL_WIDTH)

    routes = jnp.concatenate([expert_ids.astype(NARROW)] + split_three(route_weights), 1)
    cotangent_blocks = gather_plane_last(
        jnp.concatenate(
            [
                cotangent.astype(NARROW),
                jnp.pad(routes, ((0, 0), (0, lane_pad - routes.shape[1]))),
            ],
            1,
        )
    )

    def dense_route(rows):
        ids = rows[:, :TOP].astype(jnp.int32)
        parts = rows[:, TOP : 4 * TOP].astype(WIDE)
        weights = parts[:, :TOP] + parts[:, TOP : 2 * TOP] + parts[:, 2 * TOP :]
        local = place_expert * local_experts + jnp.arange(lane_pad, dtype=jnp.int32)
        match = (ids[:, :, None] == local) & (jnp.arange(lane_pad) < local_experts)
        return jnp.sum(jnp.where(match, weights[:, :, None], 0.0), 1)

    cosine_table, sine_table = rotary_tables(sequence_length, HEAD_SIZE // 2)
    inputs = tokens.astype(WIDE)
    pair_tokens = jnp.concatenate([tokens, swap_core(tokens)], 0)
    pair_segments = jnp.concatenate([segments, swap_core(segments)], 0)
    scale_pair = norm_scale(pair_tokens.astype(WIDE))
    scale_one = scale_pair[:sequence_length]
    pair_gathered = jnp.dot(pair_tokens, to_gathered, preferred_element_type=jnp.float32)
    blocks = [half for pair in attention_blocks for half in pair]
    qkv_here, gain_here, out_here = stack_attention(blocks, half_columns, lane_pad)
    gain_here = gain_here[:, :2].T
    gain_attn = gain_here[0].astype(WIDE)
    gains_placed = jnp.dot(gain_here, from_gathered, preferred_element_type=jnp.float32)
    gain_moe = gains_placed[1]
    normed_one = (pair_gathered * scale_pair * gain_attn).astype(NARROW)
    projected = jnp.dot(normed_one, qkv_here, preferred_element_type=jnp.float32)
    query_block, key_rows, value_rows = split_head_group(
        projected.reshape(2, sequence_length, -1), cosine_table, sine_table
    )
    attended, logsums = jax.vmap(attend)(query_block, key_rows, value_rows, pair_segments)
    attended = attended.reshape(2 * sequence_length, half_width)
    attended = jnp.dot(attended, heads_to_gathered, preferred_element_type=jnp.float32).astype(
        NARROW
    )
    resid_parts = jnp.dot(attended, out_here, preferred_element_type=jnp.float32)
    resid = inputs + resid_parts[:sequence_length] + swap_core(resid_parts[sequence_length:])
    scale_two = norm_scale(resid)
    normed_two = (resid * scale_two * gain_moe).astype(NARROW)

    normed_blocks = gather_plane_last(normed_two)
    out_parts, back_parts, filled = [], [], []
    for spot, ((near, away), (near_grad, away_grad)) in enumerate(
        zip(normed_blocks, cotangent_blocks)
    ):
        route = jnp.concatenate(
            [dense_route(g[:, MODEL_WIDTH:]) for g in (near_grad, away_grad)], 0
        )
        done = expert_block(
            spot,
            near,
            away,
            near_grad,
            away_grad,
            route,
            (gate_w, upper_w, down_w),
            local_experts,
            filled,
        )
        out_parts.append((done[0], done[1]))
        back_parts.append((done[2], done[3]))
        filled = done[4:]
    grad_normed_two = scatter_plane_first(back_parts)
    out_tokens = resid + scatter_plane_first(out_parts)

    hidden, grad_gate, grad_upper, rows_all, grads_all = filled
    keep, give, keep_down, give_down = expert_grads(
        place, rows_all, grads_all, hidden, grad_gate, grad_upper, local_experts, chips
    )
    part_down = keep_down + swap_core(give_down)
    taken = swap_core(give)
    collected = []
    for other in range(chips):
        piece = (
            lax.dynamic_index_in_dim(keep, chip ^ other, 0, False)
            + lax.dynamic_index_in_dim(taken, chip ^ other, 0, False).astype(WIDE)
        ).astype(NARROW)
        if other:
            piece = swap(piece, lambda i, other=other: 2 * other)
        collected.append(piece)
    part_gate_up, new_gate_up, new_first_gate_up, new_second_gate_up = adam_columns(
        place, w_gate_up, first_gate_up, second_gate_up, collected
    )

    hat_two = grad_normed_two * gain_moe
    grad_gain_moe = jnp.sum(grad_normed_two * resid * scale_two, 0)
    grad_resid = cotangent + scale_two * (
        hat_two - resid * scale_two**2 * jnp.mean(hat_two * resid, -1, keepdims=True)
    )
    grad_resid_half = grad_resid.astype(NARROW)
    pair_grads = jnp.concatenate([grad_resid_half, swap_core(grad_resid_half)], 0)
    attended_gradient = lax.dot_general(
        pair_grads, out_here, (((1,), (1,)), ((), ())), preferred_element_type=jnp.float32
    ).astype(NARROW)
    attended_gradient = (
        jnp.dot(attended_gradient, heads_from_gathered, preferred_element_type=jnp.float32)
        .astype(NARROW)
        .reshape(query_block.shape)
    )
    grad_query, grad_keys, grad_values = jax.vmap(attend_back)(
        query_block, key_rows, value_rows, pair_segments, logsums, attended_gradient
    )
    joined = jax.vmap(lambda a, b, c: join_grads(a, b, c, cosine_table, sine_table))(
        grad_query, grad_keys, grad_values
    ).reshape(2 * sequence_length, -1)
    grad_normed_parts = lax.dot_general(
        joined, qkv_here, (((1,), (1,)), ((), ())), preferred_element_type=jnp.float32
    )
    grad_gain_attn = jnp.sum(grad_normed_parts * pair_gathered * scale_pair, 0)
    gain_parts = jnp.stack(
        [grad_gain_attn, select_columns(grad_gain_moe[None], to_gathered)[0]], 1
    )
    near_parts, away_parts = attention_grads(
        normed_one,
        joined,
        attended,
        pair_grads,
        jnp.pad(gain_parts, ((0, 0), (0, lane_pad - 2))),
        owned,
    )
    summed = scatter_ring_middle([(near_parts[i], away_parts[i]) for i in range(len(DISTANCE))])
    here, there, part_out = summed[:owned], summed[owned : 2 * owned], summed[2 * owned :]
    there = swap_core(there[:, : half_columns + lane_pad])
    part_gains = (
        here[:, half_columns : half_columns + 2] + there[:, half_columns : half_columns + 2]
    ).T
    here, there = here[:, :half_columns], there[:, :half_columns]
    part_qkv = join_parities(
        jnp.where(core == 0, here, there), jnp.where(core == 0, there, here)
    )

    grad_normed_parts = select_columns(grad_normed_parts, from_gathered)
    grad_normed_one = grad_normed_parts[:sequence_length] + swap_core(
        grad_normed_parts[sequence_length:]
    )
    hat_one = grad_normed_one * gains_placed[0]
    grad_tokens = grad_resid + scale_one * (
        hat_one - inputs * scale_one**2 * jnp.mean(hat_one * inputs, -1, keepdims=True)
    )

    new_qkv, new_first_qkv, new_second_qkv = adam_step(
        w_qkv, part_qkv, first_moment_projection, second_moment_projection, learn_rate, weight_decay
    )
    new_out, new_first_out, new_second_out = adam_step(
        w_out, part_out, first_out, second_out, out_rate, weight_decay
    )
    new_gains, new_first_gains, new_second_gains = adam_step(
        gains, part_gains, first_gains, second_gains, gain_rate, 0.0
    )
    new_down, new_first_down, new_second_down = adam_step(
        w_down, part_down, first_down, second_down, learn_rate, weight_decay
    )
    return (
        out_tokens,
        grad_tokens,
        part_qkv,
        part_out,
        part_gains,
        part_gate_up,
        part_down,
        new_qkv,
        new_out,
        new_gains,
        new_gate_up,
        new_down,
        new_first_qkv,
        new_first_out,
        new_first_gains,
        new_first_gate_up,
        new_first_down,
        new_second_qkv,
        new_second_out,
        new_second_gains,
        new_second_gate_up,
        new_second_down,
    )


def shards_plain(
    tokens,
    cotangent,
    segments,
    expert_ids,
    route_weights,
    w_qkv,
    w_out,
    gains,
    w_gate_up,
    w_down,
    first_moment_projection,
    first_out,
    first_gains,
    first_gate_up,
    first_down,
    second_moment_projection,
    second_out,
    second_gains,
    second_gate_up,
    second_down,
):
    sequence_count = segments.shape[0]
    sequence_length = segments.shape[1]
    groups_expert = lax.axis_size("expert")
    local_experts = EXPERTS // groups_expert
    slot_rows = groups_expert * CAP
    qkv_full, out_full, gain_full = (
        lax.all_gather(w_qkv.astype(jnp.bfloat16), ("dp", "expert"), axis=0, tiled=True),
        lax.all_gather(w_out.astype(jnp.bfloat16), ("dp", "expert"), axis=0, tiled=True),
        lax.all_gather(gains.astype(jnp.bfloat16), ("dp", "expert"), axis=1, tiled=True),
    )
    gate_up_full, down_full = (
        lax.all_gather(w_gate_up.astype(jnp.bfloat16), "dp", axis=1, tiled=True),
        lax.all_gather(w_down.astype(jnp.bfloat16), "dp", axis=1, tiled=True),
    )
    gain_attn = gain_full[0].astype(jnp.float32)
    gain_moe = gain_full[1].astype(jnp.float32)
    cosine_table, sine_table = rotary_tables(sequence_length, HEAD_SIZE // 2)
    inputs = tokens.astype(jnp.float32)
    scale_one = norm_scale(inputs)
    normed_one = (inputs * scale_one * gain_attn).astype(jnp.bfloat16)
    projected_rows = jnp.dot(normed_one, qkv_full, preferred_element_type=jnp.float32)
    query_block, key_rows, value_rows = split_heads(
        projected_rows, sequence_count, sequence_length, cosine_table, sine_table
    )
    index = 0
    attended_seq, logsum = attend(
        query_block[index], key_rows[index], value_rows[index], segments[index]
    )
    pieces = attended_seq.reshape(sequence_length, QUERY_HEADS * HEAD_SIZE)
    logsums = [logsum]
    resid = inputs + jnp.dot(pieces, out_full, preferred_element_type=jnp.float32)
    scale_two = norm_scale(resid)
    normed_two = (resid * scale_two * gain_moe).astype(jnp.bfloat16)
    flat_ids = expert_ids.reshape(-1)
    pair_count = flat_ids.shape[0]
    one_hot = (flat_ids[:, None] == jnp.arange(EXPERTS, dtype=jnp.int32)[None, :]).astype(jnp.int32)
    ranking = jnp.sum(jnp.cumsum(one_hot, 0) * one_hot, 1) - 1
    target = flat_ids * CAP + ranking
    owners = (
        jnp.full((EXPERTS * CAP,), -1, jnp.int32)
        .at[target]
        .set(jnp.arange(pair_count, dtype=jnp.int32))
    )
    filled = (owners >= 0)[:, None]
    safe_owner = jnp.maximum(owners, 0)
    send_rows = jnp.where(filled, normed_two[safe_owner // TOP], jnp.zeros((), jnp.bfloat16))
    received = lax.all_to_all(
        send_rows.reshape(groups_expert, local_experts, CAP, MODEL_WIDTH),
        "expert",
        split_axis=0,
        concat_axis=2,
        tiled=True,
    )
    received = received.reshape(local_experts, slot_rows, MODEL_WIDTH)
    mixed = jnp.einsum("erd,edf->erf", received, gate_up_full, preferred_element_type=jnp.float32)
    gate = mixed[..., :FF]
    upper = mixed[..., FF:]
    hidden = (jax.nn.silu(gate) * upper).astype(jnp.bfloat16)
    expert_out = jnp.einsum(
        "erf,efd->erd", hidden, down_full, preferred_element_type=jnp.float32
    ).astype(jnp.bfloat16)
    returned = lax.all_to_all(
        expert_out.reshape(1, local_experts, slot_rows, MODEL_WIDTH),
        "expert",
        split_axis=2,
        concat_axis=0,
        tiled=True,
    )
    picked = returned.reshape(EXPERTS * CAP, MODEL_WIDTH)[target].reshape(-1, TOP, MODEL_WIDTH)
    out_tokens = resid + jnp.sum(route_weights[..., None] * picked.astype(jnp.float32), 1)
    gate_up_back, down_back = (
        lax.all_gather(w_gate_up.astype(jnp.bfloat16), "dp", axis=1, tiled=True),
        lax.all_gather(w_down.astype(jnp.bfloat16), "dp", axis=1, tiled=True),
    )
    grad_routed = (
        (route_weights[..., None] * cotangent[:, None, :])
        .astype(jnp.bfloat16)
        .reshape(pair_count, MODEL_WIDTH)
    )
    send_grads = jnp.where(filled, grad_routed[safe_owner], jnp.zeros((), jnp.bfloat16))
    grad_expert = lax.all_to_all(
        send_grads.reshape(groups_expert, local_experts, CAP, MODEL_WIDTH),
        "expert",
        split_axis=0,
        concat_axis=2,
        tiled=True,
    )
    grad_expert = grad_expert.reshape(local_experts, slot_rows, MODEL_WIDTH)
    grad_hidden = jnp.einsum(
        "erd,efd->erf", grad_expert, down_back, preferred_element_type=jnp.float32
    )
    grad_down = jnp.einsum("erf,erd->efd", hidden, grad_expert, preferred_element_type=jnp.float32)
    sigma = jax.nn.sigmoid(gate)
    grad_mixed = jnp.concatenate(
        [grad_hidden * upper * sigma * (1.0 + gate * (1.0 - sigma)), grad_hidden * gate * sigma], -1
    ).astype(jnp.bfloat16)
    grad_gate_up = jnp.einsum(
        "erd,erf->edf", received, grad_mixed, preferred_element_type=jnp.float32
    )
    grad_received = jnp.einsum(
        "erf,edf->erd", grad_mixed, gate_up_back, preferred_element_type=jnp.float32
    ).astype(jnp.bfloat16)
    grad_back = lax.all_to_all(
        grad_received.reshape(1, local_experts, slot_rows, MODEL_WIDTH),
        "expert",
        split_axis=2,
        concat_axis=0,
        tiled=True,
    )
    grad_normed_two = jnp.sum(
        grad_back.reshape(EXPERTS * CAP, MODEL_WIDTH)[target]
        .reshape(-1, TOP, MODEL_WIDTH)
        .astype(jnp.float32),
        1,
    )
    hat_two = grad_normed_two * gain_moe
    grad_gain_moe = jnp.sum(grad_normed_two * resid * scale_two, 0)
    grad_resid = cotangent + scale_two * (
        hat_two - resid * scale_two**2 * jnp.mean(hat_two * resid, -1, keepdims=True)
    )
    grad_resid_half = grad_resid.astype(jnp.bfloat16)
    qkv_back, out_back = (
        lax.all_gather(w_qkv.astype(jnp.bfloat16), ("dp", "expert"), axis=0, tiled=True),
        lax.all_gather(w_out.astype(jnp.bfloat16), ("dp", "expert"), axis=0, tiled=True),
    )
    grad_out = jnp.dot(pieces.T, grad_resid_half, preferred_element_type=jnp.float32)
    attended_gradient = jnp.dot(
        grad_resid_half, out_back.T, preferred_element_type=jnp.float32
    ).astype(jnp.bfloat16)
    attended_gradient = attended_gradient.reshape(
        sequence_count, sequence_length, KEY_VALUE_HEADS, QUERY_HEADS // KEY_VALUE_HEADS, HEAD_SIZE
    )
    index = 0
    grad_query, grad_keys, grad_values = attend_back(
        query_block[index],
        key_rows[index],
        value_rows[index],
        segments[index],
        logsums[index],
        attended_gradient[index],
    )
    joined = join_grads(grad_query, grad_keys, grad_values, cosine_table, sine_table)
    grad_qkv = jnp.dot(normed_one.T, joined, preferred_element_type=jnp.float32)
    grad_normed_one = jnp.dot(joined, qkv_back.T, preferred_element_type=jnp.float32)
    hat_one = grad_normed_one * gain_attn
    grad_gain_attn = jnp.sum(grad_normed_one * inputs * scale_one, 0)
    grad_tokens = grad_resid + scale_one * (
        hat_one - inputs * scale_one**2 * jnp.mean(hat_one * inputs, -1, keepdims=True)
    )
    grad_gains = jnp.stack([grad_gain_attn, grad_gain_moe])
    part_qkv, part_out, part_gains = (
        lax.psum_scatter(grad_qkv, ("dp", "expert"), scatter_dimension=0, tiled=True),
        lax.psum_scatter(grad_out, ("dp", "expert"), scatter_dimension=0, tiled=True),
        lax.psum_scatter(grad_gains, ("dp", "expert"), scatter_dimension=1, tiled=True),
    )
    part_gate_up, part_down = (
        lax.psum_scatter(grad_gate_up, "dp", scatter_dimension=1, tiled=True),
        lax.psum_scatter(grad_down, "dp", scatter_dimension=1, tiled=True),
    )
    new_qkv, new_first_qkv, new_second_qkv = adam_step(
        w_qkv, part_qkv, first_moment_projection, second_moment_projection, learn_rate, weight_decay
    )
    new_out, new_first_out, new_second_out = adam_step(
        w_out, part_out, first_out, second_out, out_rate, weight_decay
    )
    new_gains, new_first_gains, new_second_gains = adam_step(
        gains, part_gains, first_gains, second_gains, gain_rate, 0.0
    )
    new_gate_up, new_first_gate_up, new_second_gate_up = adam_step(
        w_gate_up, part_gate_up, first_gate_up, second_gate_up, learn_rate, weight_decay
    )
    new_down, new_first_down, new_second_down = adam_step(
        w_down, part_down, first_down, second_down, learn_rate, weight_decay
    )
    return (
        out_tokens,
        grad_tokens,
        part_qkv,
        part_out,
        part_gains,
        part_gate_up,
        part_down,
        new_qkv,
        new_out,
        new_gains,
        new_gate_up,
        new_down,
        new_first_qkv,
        new_first_out,
        new_first_gains,
        new_first_gate_up,
        new_first_down,
        new_second_qkv,
        new_second_out,
        new_second_gains,
        new_second_gate_up,
        new_second_down,
    )


def solution(mesh):
    by_heads = mesh.shape["dp"] == KEY_VALUE_HEADS and mesh.shape["expert"] == 4
    return jax.shard_map(
        shards_moved if by_heads else shards_plain,
        mesh=mesh,
        in_specs=(
            P(("dp", "expert"), None),
            P(("dp", "expert"), None),
            P(("dp", "expert"), None),
            P(("dp", "expert"), None),
            P(("dp", "expert"), None),
            P(("dp", "expert"), None),
            P(("dp", "expert"), None),
            P(None, ("dp", "expert")),
            P("expert", "dp", None),
            P("expert", "dp", None),
            P(("dp", "expert"), None),
            P(("dp", "expert"), None),
            P(None, ("dp", "expert")),
            P("expert", "dp", None),
            P("expert", "dp", None),
            P(("dp", "expert"), None),
            P(("dp", "expert"), None),
            P(None, ("dp", "expert")),
            P("expert", "dp", None),
            P("expert", "dp", None),
        ),
        out_specs=(
            P(("dp", "expert"), None),
            P(("dp", "expert"), None),
            P(("dp", "expert"), None),
            P(("dp", "expert"), None),
            P(None, ("dp", "expert")),
            P("expert", "dp", None),
            P("expert", "dp", None),
            P(("dp", "expert"), None),
            P(("dp", "expert"), None),
            P(None, ("dp", "expert")),
            P("expert", "dp", None),
            P("expert", "dp", None),
            P(("dp", "expert"), None),
            P(("dp", "expert"), None),
            P(None, ("dp", "expert")),
            P("expert", "dp", None),
            P("expert", "dp", None),
            P(("dp", "expert"), None),
            P(("dp", "expert"), None),
            P(None, ("dp", "expert")),
            P("expert", "dp", None),
            P("expert", "dp", None),
        ),
        check_vma=False,
    )
```

```python
import functools

import jax
import jax.numpy as jnp
import numpy as np
from jax import lax
from jax.experimental import pallas as pl
from jax.experimental.pallas import tpu as pltpu
from jax.sharding import PartitionSpec as P

MODEL_WIDTH = 1536
QUERY_HEADS = 24
KEY_VALUE_HEADS = 8
HEAD_SIZE = 64
FF = 512
EXPERTS = 40
TOP = 8
CAP = 32


eps_norm = 1e-05
beta_one = 0.9
beta_two = 0.95
adam_eps = 1e-08
learn_rate = 0.01
out_rate = 0.04
gain_rate = 0.2
weight_decay = 0.1
correct_one = 1.0 - beta_one**3
correct_two = 1.0 - beta_two**3


def norm_scale(rows):
    return lax.rsqrt(jnp.mean(rows * rows, -1, keepdims=True) + eps_norm)


def rotary_tables(sequence_length, half_dim):
    position = jnp.arange(sequence_length, dtype=jnp.float32)[:, None]
    frequency = 10000.0 ** (-jnp.arange(half_dim, dtype=jnp.float32) / half_dim)
    angles = position * frequency[None, :]
    return (jnp.cos(angles), jnp.sin(angles))


def apply_rotary(value_rows, cosine_table, sine_table, middle):
    half_dim = value_rows.shape[-1] // 2
    shape = (cosine_table.shape[0],) + (1,) * middle + (half_dim,)
    cosine_table = cosine_table.reshape(shape)
    sine_table = sine_table.reshape(shape)
    first = value_rows[..., :half_dim]
    second = value_rows[..., half_dim:]
    return jnp.concatenate(
        [first * cosine_table - second * sine_table, second * cosine_table + first * sine_table], -1
    )


def split_heads(projected_rows, sequence_count, sequence_length, cosine_table, sine_table):
    query_total_width = QUERY_HEADS * HEAD_SIZE
    key_columns_width = KEY_VALUE_HEADS * HEAD_SIZE
    reshaped_rows = projected_rows.reshape(sequence_count, sequence_length, -1)
    query_block = apply_rotary(
        reshaped_rows[..., :query_total_width].reshape(
            sequence_count,
            sequence_length,
            KEY_VALUE_HEADS,
            QUERY_HEADS // KEY_VALUE_HEADS,
            HEAD_SIZE,
        ),
        cosine_table,
        sine_table,
        2,
    )
    key_rows = apply_rotary(
        reshaped_rows[..., query_total_width : query_total_width + key_columns_width].reshape(
            sequence_count, sequence_length, KEY_VALUE_HEADS, HEAD_SIZE
        ),
        cosine_table,
        sine_table,
        1,
    )
    value_rows = reshaped_rows[..., query_total_width + key_columns_width :].reshape(
        sequence_count, sequence_length, KEY_VALUE_HEADS, HEAD_SIZE
    )
    return (
        query_block.astype(jnp.bfloat16),
        key_rows.astype(jnp.bfloat16),
        value_rows.astype(jnp.bfloat16),
    )


def allowed_mask(segment):
    spots = jnp.arange(segment.shape[0])
    return (spots[:, None] >= spots[None, :]) & (segment[:, None] == segment[None, :])


def score_block(query_block, key_rows, segment):
    scores = jnp.einsum(
        "qhgd,khd->hgqk", query_block, key_rows, preferred_element_type=jnp.float32
    ) * query_block.shape[-1] ** (-0.5)
    return jnp.where(allowed_mask(segment)[None, None], scores, -1e30)


def attend(query_block, key_rows, value_rows, segment):
    scores = score_block(query_block, key_rows, segment)
    highest = jnp.max(scores, -1, keepdims=True)
    logsum = highest + jnp.log(jnp.sum(jnp.exp(scores - highest), -1, keepdims=True))
    probs = jnp.exp(scores - logsum).astype(jnp.bfloat16)
    attended = jnp.einsum("hgqk,khd->qhgd", probs, value_rows, preferred_element_type=jnp.float32)
    return (attended.astype(jnp.bfloat16), logsum)


def attend_back(query_block, key_rows, value_rows, segment, logsum, attended_gradient):
    factor = query_block.shape[-1] ** (-0.5)
    probs = jnp.exp(score_block(query_block, key_rows, segment) - logsum)
    grad_probs = jnp.einsum(
        "qhgd,khd->hgqk", attended_gradient, value_rows, preferred_element_type=jnp.float32
    )
    inner_sum = jnp.sum(probs * grad_probs, -1, keepdims=True)
    grad_scores = (probs * (grad_probs - inner_sum) * factor).astype(jnp.bfloat16)
    grad_values = jnp.einsum(
        "hgqk,qhgd->khd",
        probs.astype(jnp.bfloat16),
        attended_gradient,
        preferred_element_type=jnp.float32,
    )
    grad_query = jnp.einsum(
        "hgqk,khd->qhgd", grad_scores, key_rows, preferred_element_type=jnp.float32
    )
    grad_keys = jnp.einsum(
        "hgqk,qhgd->khd", grad_scores, query_block, preferred_element_type=jnp.float32
    )
    return (grad_query, grad_keys, grad_values)


def join_grads(grad_query, grad_keys, grad_values, cosine_table, sine_table):
    sequence_length = grad_query.shape[0]
    grad_query = apply_rotary(grad_query, cosine_table, -sine_table, 2).reshape(sequence_length, -1)
    grad_keys = apply_rotary(grad_keys, cosine_table, -sine_table, 1).reshape(sequence_length, -1)
    return jnp.concatenate(
        [grad_query, grad_keys, grad_values.reshape(sequence_length, -1)], -1
    ).astype(jnp.bfloat16)


def adam_step(weight, grad, first, second, step_rate, shrink):
    first = beta_one * first + (1.0 - beta_one) * grad
    second = beta_two * second + (1.0 - beta_two) * grad * grad
    update = first / correct_one / (jnp.sqrt(second / correct_two) + adam_eps)
    return (weight - step_rate * (update + shrink * weight), first, second)


NARROW = jnp.bfloat16
WIDE = jnp.float32
DISTANCE = (0, 1, -1, 2)
HOP_CORE, HOP_X, HOP_Y = 1, 2, 4


def swap(rows, pick):
    count = lax.axis_size("dp")
    return lax.ppermute(rows, "dp", [(i, i ^ pick(i)) for i in range(count)])


def first_hop(i):
    return HOP_X if i & 1 else HOP_Y


def second_hop(i):
    return HOP_Y if i & 1 else HOP_X


def swap_core(rows):
    return swap(rows, lambda i: HOP_CORE)


def swap_first(rows):
    return swap(rows, first_hop)


def swap_second(rows):
    return swap(rows, second_hop)


def turn(rows, step):
    count = lax.axis_size("expert")
    return lax.ppermute(rows, "expert", [(i, (i + step) % count) for i in range(count)])


def after(values, *others):
    return lax.optimization_barrier((values, others))[0]


def along_first(part):
    return jnp.concatenate([part, swap_first(part)], 0)


def gather_plane_last(block):
    ahead, behind = turn(block, 1), turn(block, -1)
    far = turn(ahead, 1)
    found = []
    for part in (block, ahead, behind, far):
        pair = jnp.concatenate([part, swap_first(part)], 0)
        found.append((pair, swap_second(pair)))
    return found, far


def gather_ring(block):
    pair = jnp.concatenate([block, swap_first(block)], 0)
    ahead, behind = turn(pair, 1), turn(pair, -1)
    return pair, ahead, behind, turn(ahead, 1)


def ring_sum(parts, gate=()):
    behind = turn(parts[2].astype(NARROW), 1)
    far = turn(parts[3].astype(NARROW), -1)
    ahead = turn((parts[1] + far.astype(WIDE)).astype(NARROW), -1)
    behind, ahead = after((behind, ahead), gate)
    return parts[0] + behind.astype(WIDE) + ahead.astype(WIDE)


def add_second(near, away, gate=()):
    return near + after(swap_second(away.astype(NARROW)), gate).astype(WIDE)


def add_first(rows, gate=()):
    half = rows.shape[0] // 2
    return rows[:half] + after(swap_first(rows[half:].astype(NARROW)), gate).astype(WIDE)


def gathered_sources(count_dp, count_expert):
    table = np.zeros((count_dp, count_expert, 4, 2, 2, 2), np.int32)
    for i in range(count_dp):
        for z in range(count_expert):
            for spot, distance in enumerate(DISTANCE):
                for second in range(2):
                    for first in range(2):
                        plane = i ^ (first_hop(i) * first) ^ (second_hop(i) * second)
                        table[i, z, spot, second, first] = plane, (z - distance) % count_expert
    return table.reshape(count_dp, count_expert, 16, 2)


def split_three(values):
    high = values.astype(NARROW)
    left = values - high.astype(WIDE)
    middle = left.astype(NARROW)
    return [high, middle, (left - middle.astype(WIDE)).astype(NARROW)]


def select_columns(values, chosen):
    rows = values.shape[0]
    parts = jnp.dot(
        jnp.concatenate(split_three(values), 0), chosen, preferred_element_type=jnp.float32
    )
    return parts[:rows] + parts[rows : 2 * rows] + parts[2 * rows :]


def parity_columns(rows, parity):
    count = rows.shape[0]
    query_total_width = QUERY_HEADS * HEAD_SIZE
    key_columns_width = KEY_VALUE_HEADS * HEAD_SIZE
    bounds = (
        (0, query_total_width),
        (query_total_width, query_total_width + key_columns_width),
        (query_total_width + key_columns_width, query_total_width + 2 * key_columns_width),
    )
    return jnp.concatenate(
        [
            rows[:, low:high].reshape(count, KEY_VALUE_HEADS // 2, 2, -1)[:, :, parity]
            .reshape(count, -1)
            for low, high in bounds
        ],
        1,
    )


def join_parities(even, odd):
    count = even.shape[0]
    query_half = QUERY_HEADS * HEAD_SIZE // 2
    key_half = KEY_VALUE_HEADS * HEAD_SIZE // 2
    bounds = (
        (0, query_half),
        (query_half, query_half + key_half),
        (query_half + key_half, query_half + 2 * key_half),
    )
    heads = KEY_VALUE_HEADS // 2
    return jnp.concatenate(
        [
            jnp.stack(
                [
                    even[:, low:high].reshape(count, heads, -1),
                    odd[:, low:high].reshape(count, heads, -1),
                ],
                2,
            ).reshape(count, -1)
            for low, high in bounds
        ],
        1,
    )


def split_head_group(projected_rows, cosine_table, sine_table):
    sequences, length = projected_rows.shape[:2]
    heads = KEY_VALUE_HEADS // 2
    group = QUERY_HEADS // KEY_VALUE_HEADS
    query_width = heads * group * HEAD_SIZE
    key_width = heads * HEAD_SIZE
    query_block = projected_rows[..., :query_width].reshape(
        sequences, length, heads, group, HEAD_SIZE
    )
    key_rows = projected_rows[..., query_width : query_width + key_width].reshape(
        sequences, length, heads, HEAD_SIZE
    )
    value_rows = projected_rows[..., query_width + key_width :].reshape(
        sequences, length, heads, HEAD_SIZE
    )
    query_block = jax.vmap(lambda a: apply_rotary(a, cosine_table, sine_table, 2))(query_block)
    key_rows = jax.vmap(lambda a: apply_rotary(a, cosine_table, sine_table, 1))(key_rows)
    return (
        query_block.astype(jnp.bfloat16),
        key_rows.astype(jnp.bfloat16),
        value_rows.astype(jnp.bfloat16),
    )


def spread_columns_kernel(weight_ref, out_ref):
    chips, _, _, lanes = out_ref.shape
    for chip in range(chips):
        for part in range(2):
            columns = slice(part * FF + chip * lanes, part * FF + (chip + 1) * lanes)
            out_ref[chip, part] = weight_ref[0, :, columns].astype(out_ref.dtype)


def spread_columns(weight, chips):
    experts, rows, both = weight.shape
    lanes = both // 2 // chips
    return pl.pallas_call(
        spread_columns_kernel,
        grid=(experts,),
        in_specs=[pl.BlockSpec((1, rows, both), lambda e: (e, 0, 0))],
        out_specs=pl.BlockSpec((chips, 2, rows, lanes), lambda e: (0, 0, 0, e)),
        out_shape=jax.ShapeDtypeStruct((chips, 2, rows, experts * lanes), jnp.bfloat16),
        cost_estimate=pl.CostEstimate(
            flops=0, bytes_accessed=6 * experts * rows * both, transcendentals=0
        ),
    )(weight)


def stack_rows_kernel(place_ref, mine_ref, theirs_ref, gate_ref, upper_ref, sems):
    core = place_ref[1]
    chips, _, rows, _ = mine_ref.shape
    copies = []
    for chip in range(chips):
        for mate, ref in enumerate((mine_ref, theirs_ref)):
            start = pl.multiple_of((chip * 2 + (core ^ mate)) * rows, rows)
            for part, out_ref in enumerate((gate_ref, upper_ref)):
                copies.append(
                    pltpu.make_async_copy(
                        ref.at[chip, part],
                        out_ref.at[pl.ds(start, rows), :],
                        sems.at[len(copies)],
                    )
                )
    for copy in copies:
        copy.start()
    for copy in copies:
        copy.wait()


def stack_rows(place, mine, theirs):
    chips, _, rows, columns = mine.shape
    shape = jax.ShapeDtypeStruct((2 * chips * rows, columns), jnp.bfloat16)
    return pl.pallas_call(
        stack_rows_kernel,
        in_specs=[pl.BlockSpec(memory_space=pltpu.SMEM)]
        + [pl.BlockSpec(memory_space=pltpu.VMEM)] * 2,
        out_specs=[pl.BlockSpec(memory_space=pl.ANY)] * 2,
        out_shape=[shape] * 2,
        scratch_shapes=[pltpu.SemaphoreType.DMA((4 * chips,))],
        cost_estimate=pl.CostEstimate(
            flops=0, bytes_accessed=16 * chips * rows * columns, transcendentals=0
        ),
    )(place, mine, theirs)


def stack_attention_kernel(*refs):
    blocks, (qkv_ref, gain_ref, out_ref, sems) = refs[:-4], refs[-4:]
    wide, lanes = qkv_ref.shape[1], gain_ref.shape[1]
    owned = out_ref.shape[0] // (2 * len(blocks))
    copies = []
    for i, block in enumerate(blocks):
        for j in range(2):
            top, spot = 3 * owned * j, 2 * i + j
            pairs = (
                (
                    block.at[pl.ds(top, 2 * owned), pl.ds(0, wide)],
                    qkv_ref.at[pl.ds(2 * owned * spot, 2 * owned), :],
                ),
                (
                    block.at[pl.ds(top, 2 * owned), pl.ds(wide, lanes)],
                    gain_ref.at[pl.ds(2 * owned * spot, 2 * owned), :],
                ),
                (
                    block.at[pl.ds(top + 2 * owned, owned), :],
                    out_ref.at[pl.ds(owned * spot, owned), :],
                ),
            )
            for source, target in pairs:
                copies.append(pltpu.make_async_copy(source, target, sems.at[len(copies)]))
    for copy in copies:
        copy.start()
    for copy in copies:
        copy.wait()


def stack_attention(blocks, wide, lanes):
    owned = blocks[0].shape[0] // 6
    count = 2 * len(blocks)
    b16 = lambda r, c: jax.ShapeDtypeStruct((r, c), jnp.bfloat16)
    return pl.pallas_call(
        stack_attention_kernel,
        in_specs=[pl.BlockSpec(memory_space=pltpu.VMEM)] * len(blocks),
        out_specs=[pl.BlockSpec(memory_space=pl.ANY)] * 3,
        out_shape=[
            b16(2 * owned * count, wide),
            b16(2 * owned * count, lanes),
            b16(owned * count, blocks[0].shape[1]),
        ],
        scratch_shapes=[pltpu.SemaphoreType.DMA((3 * count,))],
        cost_estimate=pl.CostEstimate(
            flops=0, bytes_accessed=4 * 3 * owned * count * MODEL_WIDTH, transcendentals=0
        ),
    )(*blocks)


def attention_grads_kernel(
    normed_ref, joined_ref, attended_ref, grads_ref, gain_ref, near_ref, away_ref
):
    contract = (((0,), (0,)), ((), ()))
    wide, lanes = joined_ref.shape[1], gain_ref.shape[1]
    spots = near_ref.shape[0]
    owned = near_ref.shape[1] // 6
    joined, grads = joined_ref[...], grads_ref[...]

    def place(spot, second, first, row, columns, values):
        rows = pl.ds(3 * owned * first + row, values.shape[0])
        if second:
            away_ref[spot, rows, columns] = values.astype(away_ref.dtype)
        else:
            near_ref[spot, rows, columns] = values

    for spot in range(spots):
        rows = 8 * owned
        qkv = lax.dot_general(
            normed_ref[:, rows * spot : rows * (spot + 1)],
            joined,
            contract,
            preferred_element_type=jnp.float32,
        )
        for i in range(4):
            part = slice(2 * owned * i, 2 * owned * (i + 1))
            place(spot, i // 2, i % 2, 0, pl.ds(0, wide), qkv[part])
            gain = gain_ref[pl.ds(rows * spot + 2 * owned * i, 2 * owned), :]
            place(spot, i // 2, i % 2, 0, pl.ds(wide, lanes), gain)
            place(spot, i // 2, i % 2, 0, pl.ds(wide + lanes, lanes), jnp.zeros_like(gain))
        if spot % 2 == 0:
            out = lax.dot_general(
                attended_ref[:, 4 * owned * spot : 4 * owned * (spot + 2)],
                grads,
                contract,
                preferred_element_type=jnp.float32,
            )
            for i in range(8):
                part = slice(owned * i, owned * (i + 1))
                place(
                    spot + i // 4,
                    i // 2 % 2,
                    i % 2,
                    2 * owned,
                    pl.ds(0, out.shape[1]),
                    out[part],
                )


def attention_grads(normed, joined, attended, grads, gain, owned):
    spots = len(DISTANCE)
    shape = (spots, 6 * owned, grads.shape[1])
    return pl.pallas_call(
        attention_grads_kernel,
        out_shape=[
            jax.ShapeDtypeStruct(shape, jnp.float32),
            jax.ShapeDtypeStruct(shape, jnp.bfloat16),
        ],
        compiler_params=pltpu.CompilerParams(vmem_limit_bytes=44 * 1024 * 1024),
        cost_estimate=pl.CostEstimate(
            flops=2 * normed.shape[0] * normed.shape[1] * (joined.shape[1] + grads.shape[1] // 2),
            bytes_accessed=20 * 1024 * 1024,
            transcendentals=0,
        ),
    )(normed, joined, attended, grads, gain)


def expert_kernel(place_ref, near_ref, away_ref, *refs, per_step, spot):
    given_ref, gate_ref, upper_ref, down_ref = refs[:4]
    near_back_ref, away_back_ref = refs[-11:-9]
    hidden_ref, grad_gate_ref, grad_upper_ref, rows_ref, grads_ref, narrow_ref = refs[-9:-3]
    route_ref, out_ref, back_ref = refs[-3:]
    step = pl.program_id(0)
    half, width = near_ref.shape

    @pl.when(step == 0)
    def _():
        rows_ref[:half, :] = near_ref[...]
        rows_ref[half:, :] = away_ref[...]
        grads_ref[...] = given_ref[:, :width]
        lanes = lax.broadcasted_iota(jnp.int32, route_ref.shape, 1)
        expert = (lanes + place_ref[2]).astype(jnp.float32)
        routes = given_ref[:, width:].astype(jnp.float32)
        weights = (
            routes[:, TOP : 2 * TOP]
            + routes[:, 2 * TOP : 3 * TOP]
            + routes[:, 3 * TOP : 4 * TOP]
        )
        dense = jnp.zeros_like(expert)
        for k in range(TOP):
            dense += jnp.where(expert == routes[:, k : k + 1], weights[:, k : k + 1], 0.0)
        route_ref[...] = dense
        out_ref[...] = jnp.zeros_like(out_ref)
        back_ref[...] = jnp.zeros_like(back_ref)

    rows = rows_ref[...]
    grads = grads_ref[...]
    contract_last = (((1,), (1,)), ((), ()))
    gate = jnp.dot(rows, gate_ref[...], preferred_element_type=jnp.float32)
    upper = jnp.dot(rows, upper_ref[...], preferred_element_type=jnp.float32)
    grad_hidden = lax.dot_general(
        grads, down_ref[...], contract_last, preferred_element_type=jnp.float32
    )
    route = route_ref[...]
    lanes = lax.broadcasted_iota(jnp.int32, route.shape, 1)
    columns = gate.shape[1] // per_step
    spread = []
    for i in range(per_step):
        one = jnp.sum(jnp.where(lanes == step * per_step + i, route, 0.0), 1, keepdims=True)
        spread.append(jnp.broadcast_to(one, (route.shape[0], columns)))
    weight = jnp.concatenate(spread, 1)
    sigma = 1.0 / (1.0 + jnp.exp(-gate))
    active = gate * sigma
    hidden = (weight * active * upper).astype(jnp.bfloat16)
    weighted = weight * grad_hidden
    grad_gate = (weighted * upper * sigma * (1.0 + gate * (1.0 - sigma))).astype(jnp.bfloat16)
    grad_upper = (weighted * active).astype(jnp.bfloat16)
    hidden_ref[...] = hidden
    grad_gate_ref[...] = grad_gate
    grad_upper_ref[...] = grad_upper
    out_ref[...] += jnp.dot(hidden, down_ref[...], preferred_element_type=jnp.float32)
    back_ref[...] += lax.dot_general(
        grad_gate, gate_ref[...], contract_last, preferred_element_type=jnp.float32
    ) + lax.dot_general(
        grad_upper, upper_ref[...], contract_last, preferred_element_type=jnp.float32
    )

    @pl.when(step == pl.num_programs(0) - 1)
    def _():
        narrow_ref[...] = out_ref[...].astype(jnp.bfloat16)
        near_back_ref[...] = back_ref[:half, :]
        away_back_ref[...] = back_ref[half:, :].astype(jnp.bfloat16)


def expert_block(place, spot, near, away, given, weights, experts, filled):
    gate_w, upper_w, down_w = weights
    half, width = near.shape
    block = half // 2
    total = gate_w.shape[1]
    per_step = 2
    steps = experts // per_step
    columns = total // steps
    whole = lambda a: pl.BlockSpec(a.shape, lambda i, p: (0, 0))
    rows = 2 * half
    every = rows * len(DISTANCE)
    b16 = lambda r, c: jax.ShapeDtypeStruct((r, c), jnp.bfloat16)
    fixed = pl.BlockSpec((half, width), lambda i, p: (0, 0))
    part = pl.BlockSpec((rows, columns), lambda i, p: (spot, i))
    kept = pl.BlockSpec((rows, width), lambda i, p: (spot, 0))
    wide = given.shape[1]
    inputs = (place, near, away, given, gate_w, upper_w, down_w)
    return pl.pallas_call(
        functools.partial(expert_kernel, per_step=per_step, spot=spot),
        grid_spec=pltpu.PrefetchScalarGridSpec(
            num_scalar_prefetch=1,
            grid=(steps,),
            in_specs=[
                whole(near),
                whole(away),
                pl.BlockSpec((rows, wide), lambda i, p: (p[3 + spot], 0)),
            ]
            + [
                pl.BlockSpec((width, columns), lambda i, p: (0, i)),
                pl.BlockSpec((width, columns), lambda i, p: (0, i)),
                pl.BlockSpec((columns, width), lambda i, p: (i, 0)),
            ]
            + [pl.BlockSpec(memory_space=pl.ANY)] * len(filled),
            out_specs=[fixed] * 2
            + [part] * 3
            + [kept] * 2
            + [pl.BlockSpec((rows, width), lambda i, p: (p[3 + spot], 0))],
            scratch_shapes=[
                pltpu.VMEM((rows, wide - width), jnp.float32),
                pltpu.VMEM((rows, width), jnp.float32),
                pltpu.VMEM((rows, width), jnp.float32),
            ],
        ),
        out_shape=[
            jax.ShapeDtypeStruct((half, width), jnp.float32),
            b16(half, width),
        ]
        + [b16(every, total)] * 3
        + [b16(every, width)] * 3,
        input_output_aliases={len(inputs) + i: 2 + i for i in range(len(filled))},
        compiler_params=pltpu.CompilerParams(vmem_limit_bytes=48 * 1024 * 1024),
        cost_estimate=pl.CostEstimate(
            flops=2 * rows * width * total * 6,
            bytes_accessed=2 * (3 * width * total + 3 * rows * total + 12 * rows * width),
            transcendentals=rows * total,
        ),
    )(*inputs, *filled)


def column_grads_kernel(
    place_ref, rows_ref, grad_gate_ref, grad_upper_ref, *refs
):
    keep_ref, give_ref, full_ref = refs[-3:]
    core = place_ref[1]
    contract = (((0,), (0,)), ((), ()))
    chips, _, plane_rows, _ = keep_ref.shape
    for part, ref in enumerate((grad_gate_ref, grad_upper_ref)):
        full_ref[...] = lax.dot_general(
            rows_ref[...], ref[...], contract, preferred_element_type=jnp.float32
        )
        for chip in range(chips):
            mine = pl.multiple_of((2 * chip + core) * plane_rows, plane_rows)
            theirs = pl.multiple_of((2 * chip + 1 - core) * plane_rows, plane_rows)
            keep_ref[chip, part] = full_ref[pl.ds(mine, plane_rows), :]
            give_ref[chip, part] = full_ref[pl.ds(theirs, plane_rows), :].astype(give_ref.dtype)


def column_grads(place, step, steps, rows_all, grad_gate, grad_upper, chips, filled):
    tokens, width = rows_all.shape
    total = grad_gate.shape[1]
    columns = total // steps
    plane_rows = width // (2 * chips)
    part = pl.BlockSpec((tokens, columns), lambda i, p: (0, step))
    wide = pl.BlockSpec((chips, 2, plane_rows, columns), lambda i, p: (0, 0, 0, step))
    shape = (chips, 2, plane_rows, total)
    return pl.pallas_call(
        column_grads_kernel,
        grid_spec=pltpu.PrefetchScalarGridSpec(
            num_scalar_prefetch=1,
            grid=(1,),
            in_specs=[pl.BlockSpec((tokens, width), lambda i, p: (0, 0)), part, part]
            + [pl.BlockSpec(memory_space=pl.ANY)] * len(filled),
            out_specs=[wide, wide],
            scratch_shapes=[pltpu.VMEM((width, columns), jnp.float32)],
        ),
        out_shape=[
            jax.ShapeDtypeStruct(shape, jnp.float32),
            jax.ShapeDtypeStruct(shape, jnp.bfloat16),
        ],
        input_output_aliases={4 + i: i for i in range(len(filled))},
        compiler_params=pltpu.CompilerParams(vmem_limit_bytes=36 * 1024 * 1024),
        cost_estimate=pl.CostEstimate(
            flops=4 * tokens * width * columns,
            bytes_accessed=2 * tokens * (width + 2 * columns) + 6 * 2 * width * columns,
            transcendentals=0,
        ),
    )(place, rows_all, grad_gate, grad_upper, *filled)


def down_grads_kernel(place_ref, grads_ref, hidden_ref, keep_ref, give_ref, full_ref):
    core = place_ref[1]
    full_ref[...] = lax.dot_general(
        hidden_ref[...],
        grads_ref[...],
        (((0,), (0,)), ((), ())),
        preferred_element_type=jnp.float32,
    )
    experts, down_rows, _ = keep_ref.shape
    for e in range(experts):
        mine = pl.multiple_of((2 * e + core) * down_rows, down_rows)
        theirs = pl.multiple_of((2 * e + 1 - core) * down_rows, down_rows)
        keep_ref[e] = full_ref[pl.ds(mine, down_rows), :]
        give_ref[e] = full_ref[pl.ds(theirs, down_rows), :]


def down_grads(place, steps, grads_all, hidden, experts):
    tokens, width = grads_all.shape
    total = hidden.shape[1]
    columns = total // steps
    per_step = experts // steps
    down_rows = total // experts // 2
    down = pl.BlockSpec((per_step, down_rows, width), lambda i, p: (i, 0, 0))
    return pl.pallas_call(
        down_grads_kernel,
        grid_spec=pltpu.PrefetchScalarGridSpec(
            num_scalar_prefetch=1,
            grid=(steps,),
            in_specs=[
                pl.BlockSpec((tokens, width), lambda i, p: (0, 0)),
                pl.BlockSpec((tokens, columns), lambda i, p: (0, i)),
            ],
            out_specs=[down, down],
            scratch_shapes=[pltpu.VMEM((columns, width), jnp.float32)],
        ),
        out_shape=[jax.ShapeDtypeStruct((experts, down_rows, width), jnp.float32)] * 2,
        compiler_params=pltpu.CompilerParams(vmem_limit_bytes=36 * 1024 * 1024),
        cost_estimate=pl.CostEstimate(
            flops=2 * tokens * width * total,
            bytes_accessed=2 * tokens * (width + total) + 4 * width * total,
            transcendentals=0,
        ),
    )(place, grads_all, hidden)


def adam_columns_kernel(w_ref, first_ref, second_ref, grad_ref, *outs):
    chips, _, _, lanes = grad_ref.shape
    for chip in range(chips):
        for part in range(2):
            columns = slice(part * FF + chip * lanes, part * FF + (chip + 1) * lanes)
            grad = grad_ref[chip, part].astype(jnp.float32)
            found = adam_step(
                w_ref[0, :, columns],
                grad,
                first_ref[0, :, columns],
                second_ref[0, :, columns],
                learn_rate,
                weight_decay,
            )
            for out_ref, value in zip(outs, (grad,) + found):
                out_ref[0, :, columns] = value


def adam_columns(weight, first, second, grads):
    experts, rows, both = weight.shape
    chips = grads.shape[0]
    lanes = grads.shape[3] // experts
    block = pl.BlockSpec((1, rows, both), lambda e: (e, 0, 0))
    return pl.pallas_call(
        adam_columns_kernel,
        grid=(experts,),
        in_specs=[block] * 3 + [pl.BlockSpec((chips, 2, rows, lanes), lambda e: (0, 0, 0, e))],
        out_specs=[block] * 4,
        out_shape=[jax.ShapeDtypeStruct(weight.shape, jnp.float32)] * 4,
        compiler_params=pltpu.CompilerParams(vmem_limit_bytes=56 * 1024 * 1024),
        cost_estimate=pl.CostEstimate(
            flops=20 * experts * rows * both,
            bytes_accessed=30 * experts * rows * both,
            transcendentals=experts * rows * both,
        ),
    )(weight, first, second, grads)


def shards_moved(
    tokens,
    cotangent,
    segments,
    expert_ids,
    route_weights,
    w_qkv,
    w_out,
    gains,
    w_gate_up,
    w_down,
    first_moment_projection,
    first_out,
    first_gains,
    first_gate_up,
    first_down,
    second_moment_projection,
    second_out,
    second_gains,
    second_gate_up,
    second_down,
):
    sequence_length = segments.shape[1]
    count_dp, count_expert = lax.axis_size("dp"), lax.axis_size("expert")
    place_dp, place_expert = lax.axis_index("dp"), lax.axis_index("expert")
    core = place_dp % 2
    chip = place_dp // 2
    chips = count_dp // 2
    local_experts = EXPERTS // count_expert
    owned = w_qkv.shape[0]
    half_columns = w_qkv.shape[1] // 2
    half_width = MODEL_WIDTH // 2
    lane_pad = 128

    narrow_qkv = w_qkv.astype(NARROW)
    even_columns, odd_columns = parity_columns(narrow_qkv, 0), parity_columns(narrow_qkv, 1)
    gain_columns = jnp.pad(gains.astype(NARROW).T, ((0, 0), (0, lane_pad - 2)))
    kept = jnp.where(core == 0, even_columns, odd_columns)
    given = jnp.where(core == 0, odd_columns, even_columns)
    rest = jnp.zeros((owned, MODEL_WIDTH - half_columns - lane_pad), NARROW)
    taken = swap_core(jnp.concatenate([given, gain_columns], 1))
    block = jnp.concatenate(
        [
            jnp.concatenate([kept, gain_columns, rest], 1),
            jnp.concatenate([taken, rest], 1),
            w_out.astype(NARROW),
        ],
        0,
    )
    share = local_experts * (FF // chips)
    attention_ring = [block] + [turn(block, distance) for distance in DISTANCE[1:]]
    attention_pairs = [along_first(part) for part in attention_ring[:2]]
    pieces = spread_columns(after(w_gate_up, attention_pairs[0]), chips)
    routes = jnp.concatenate([expert_ids.astype(NARROW)] + split_three(route_weights), 1)
    cotangent_rows = jnp.concatenate(
        [
            cotangent.astype(NARROW),
            jnp.pad(routes, ((0, 0), (0, lane_pad - routes.shape[1]))),
        ],
        1,
    )
    cotangent_pair = along_first(cotangent_rows)
    cotangent_here = jnp.concatenate([cotangent_pair, swap_second(cotangent_pair)], 0)
    cotangent_all = lax.all_gather(
        after(cotangent_here, attention_ring), "expert", axis=0, tiled=True
    )
    attention_ring = attention_ring[:2] + after(attention_ring[2:], (pieces, cotangent_pair))
    attention_pairs.append(along_first(attention_ring[2]))
    attention_pairs.append(along_first(after(attention_ring[3], cotangent_here)))
    attention_blocks = [(pair, swap_second(pair)) for pair in attention_pairs]

    sources = jnp.asarray(gathered_sources(count_dp, count_expert))[place_dp, place_expert]
    from_dp, from_expert = sources[:, 0], sources[:, 1]
    row_in = jnp.arange(owned, dtype=jnp.int32)
    feature = (
        ((from_dp[:, None] ^ jnp.arange(2, dtype=jnp.int32)[None, :]) * count_expert
         + from_expert[:, None])[:, :, None] * owned + row_in
    ).reshape(-1)
    head_feature = (
        ((from_dp // 2 * count_expert + from_expert) * owned)[:, None] + row_in
    ).reshape(-1)
    places = jnp.arange(MODEL_WIDTH, dtype=jnp.int32)
    to_gathered = (places[:, None] == feature[None, :]).astype(NARROW)
    from_gathered = (feature[:, None] == places[None, :]).astype(NARROW)
    head_places = places[: half_width]
    heads_to_gathered = (head_places[:, None] == head_feature[None, :]).astype(NARROW)
    heads_from_gathered = (head_feature[:, None] == head_places[None, :]).astype(NARROW)

    found_at = (place_expert - jnp.asarray(DISTANCE, jnp.int32)) % count_expert
    place = jnp.concatenate(
        [jnp.stack([chip, core, place_expert * local_experts]).astype(jnp.int32), found_at]
    )
    parities = [list(range(i, count_dp, 2)) for i in range(2)]
    pieces = lax.all_to_all(
        after(pieces, attention_blocks[1][1]), "dp", 0, 0, axis_index_groups=parities, tiled=True
    )
    down_mine = after(w_down, attention_pairs[0]).astype(NARROW)
    down_theirs = swap_core(down_mine)
    down_w = jnp.where(
        core == 0,
        jnp.concatenate([down_mine, down_theirs], 1),
        jnp.concatenate([down_theirs, down_mine], 1),
    ).reshape(share, MODEL_WIDTH)

    cosine_table, sine_table = rotary_tables(sequence_length, HEAD_SIZE // 2)
    inputs = tokens.astype(WIDE)
    pair_tokens = jnp.concatenate([tokens, swap_core(tokens)], 0)
    pair_segments = jnp.concatenate([segments, swap_core(segments)], 0)
    scale_pair = norm_scale(pair_tokens.astype(WIDE))
    scale_one = scale_pair[:sequence_length]
    pair_gathered = jnp.dot(pair_tokens, to_gathered, preferred_element_type=jnp.float32)
    blocks = [half for pair in attention_blocks for half in pair]
    qkv_here, gain_here, out_here = stack_attention(blocks, half_columns, lane_pad)
    gain_here = gain_here[:, :2].T
    gain_attn = gain_here[0].astype(WIDE)
    gains_placed = jnp.dot(gain_here, from_gathered, preferred_element_type=jnp.float32)
    gain_moe = gains_placed[1]
    normed_one = (pair_gathered * scale_pair * gain_attn).astype(NARROW)
    projected = jnp.dot(normed_one, qkv_here, preferred_element_type=jnp.float32)
    query_block, key_rows, value_rows = split_head_group(
        projected.reshape(2, sequence_length, -1), cosine_table, sine_table
    )
    attended, logsums = jax.vmap(attend)(query_block, key_rows, value_rows, pair_segments)
    attended = attended.reshape(2 * sequence_length, half_width)
    attended = jnp.dot(attended, heads_to_gathered, preferred_element_type=jnp.float32).astype(
        NARROW
    )
    resid_parts = jnp.dot(attended, out_here, preferred_element_type=jnp.float32)
    resid = inputs + resid_parts[:sequence_length] + swap_core(resid_parts[sequence_length:])
    scale_two = norm_scale(resid)
    normed_two = (resid * scale_two * gain_moe).astype(NARROW)
    normed_two = after(normed_two, pieces)

    normed_blocks, _ = gather_plane_last(normed_two)
    gate_w, upper_w = stack_rows(place, pieces, after(swap_core(pieces), normed_two))
    back_parts, filled = [], []
    second_parts = []
    for spot, (near, away) in enumerate(normed_blocks):
        if spot >= 2:
            near = after(near, (second_parts[spot - 2], back_parts[: spot - 2]))
        done = expert_block(
            place,
            spot,
            near,
            away,
            cotangent_all,
            (gate_w, upper_w, down_w),
            local_experts,
            filled,
        )
        filled = done[2:]
        if spot < len(DISTANCE) - 1:
            second_parts.append(add_second(done[0], done[1]))
            back_parts.append(add_first(second_parts[-1]))
    hidden, grad_gate, grad_upper, rows_all, grads_all, out_all = filled
    steps = local_experts // 2
    kept_grads = []
    for step in range(steps):
        kept_grads = column_grads(
            place, step, steps, rows_all, grad_gate, grad_upper, chips, kept_grads
        )
        if step == 0:
            last = add_second(done[0], done[1], kept_grads)
        elif step == 1:
            back_parts.append(add_first(last, kept_grads))
        elif step == 2:
            found = [
                turn(part.astype(NARROW), -distance)
                for part, distance in zip(back_parts[1:], DISTANCE[1:])
            ]
            grad_normed_two = back_parts[0] + sum(
                part.astype(WIDE) for part in after(found, kept_grads)
            )
            rows_all = after(rows_all, grad_normed_two)
    keep, give = kept_grads
    taken = swap_core(give)
    expert_sums = (keep + taken.astype(WIDE)).astype(NARROW)
    parities = [list(range(i, count_dp, 2)) for i in range(2)]
    collected = lax.all_to_all(
        expert_sums, "dp", 0, 0, axis_index_groups=parities, tiled=True
    )
    out_sums = lax.psum_scatter(
        after(out_all, grad_normed_two), "expert", scatter_dimension=0, tiled=True
    )

    hat_two = grad_normed_two * gain_moe
    grad_gain_moe = jnp.sum(grad_normed_two * resid * scale_two, 0)
    grad_resid = cotangent + scale_two * (
        hat_two - resid * scale_two**2 * jnp.mean(hat_two * resid, -1, keepdims=True)
    )
    grad_resid_half = grad_resid.astype(NARROW)
    pair_grads = jnp.concatenate([grad_resid_half, swap_core(grad_resid_half)], 0)
    attended_gradient = lax.dot_general(
        pair_grads, out_here, (((1,), (1,)), ((), ())), preferred_element_type=jnp.float32
    ).astype(NARROW)
    attended_gradient = (
        jnp.dot(attended_gradient, heads_from_gathered, preferred_element_type=jnp.float32)
        .astype(NARROW)
        .reshape(query_block.shape)
    )
    grad_query, grad_keys, grad_values = jax.vmap(attend_back)(
        query_block, key_rows, value_rows, pair_segments, logsums, attended_gradient
    )
    joined = jax.vmap(lambda a, b, c: join_grads(a, b, c, cosine_table, sine_table))(
        grad_query, grad_keys, grad_values
    ).reshape(2 * sequence_length, -1)
    joined = after(joined, expert_sums)
    grad_normed_parts = lax.dot_general(
        joined, qkv_here, (((1,), (1,)), ((), ())), preferred_element_type=jnp.float32
    )
    grad_gain_attn = jnp.sum(grad_normed_parts * pair_gathered * scale_pair, 0)
    gain_parts = jnp.stack(
        [grad_gain_attn, select_columns(grad_gain_moe[None], to_gathered)[0]], 1
    )
    near_parts, away_parts = attention_grads(
        normed_one,
        joined,
        attended,
        pair_grads,
        jnp.pad(gain_parts, ((0, 0), (0, lane_pad - 2))),
        owned,
    )
    keep_down, give_down = down_grads(
        place, steps, after(grads_all, near_parts), hidden, local_experts
    )
    part_down = keep_down + swap_core(give_down)
    new_down, new_first_down, new_second_down = adam_step(
        w_down, part_down, first_down, second_down, learn_rate, weight_decay
    )
    part_gate_up, new_gate_up, new_first_gate_up, new_second_gate_up = adam_columns(
        w_gate_up, first_gate_up, second_gate_up, after(collected, near_parts)
    )
    in_plane = [None] * len(DISTANCE)
    for i in (3, 1, 2, 0):
        in_plane[i] = add_second(near_parts[i], away_parts[i], new_gate_up if i in (2, 0) else ())
    for i in (3, 1, 2, 0):
        in_plane[i] = add_first(in_plane[i])
    out_sums = after(out_sums, in_plane[3]).astype(WIDE)
    out_half = out_sums.shape[0] // 2
    out_sums = add_second(out_sums[:out_half], out_sums[out_half:])
    summed = ring_sum(in_plane, (new_down, out_sums))
    out_tokens = resid + add_first(out_sums, summed)
    here, there, part_out = summed[:owned], summed[owned : 2 * owned], summed[2 * owned :]
    there = swap_core(there[:, : half_columns + lane_pad])
    part_gains = (
        here[:, half_columns : half_columns + 2] + there[:, half_columns : half_columns + 2]
    ).T
    here, there = here[:, :half_columns], there[:, :half_columns]
    part_qkv = join_parities(
        jnp.where(core == 0, here, there), jnp.where(core == 0, there, here)
    )

    grad_normed_parts = select_columns(grad_normed_parts, from_gathered)
    grad_normed_one = grad_normed_parts[:sequence_length] + swap_core(
        grad_normed_parts[sequence_length:]
    )
    hat_one = grad_normed_one * gains_placed[0]
    grad_tokens = grad_resid + scale_one * (
        hat_one - inputs * scale_one**2 * jnp.mean(hat_one * inputs, -1, keepdims=True)
    )

    new_qkv, new_first_qkv, new_second_qkv = adam_step(
        w_qkv, part_qkv, first_moment_projection, second_moment_projection, learn_rate, weight_decay
    )
    new_out, new_first_out, new_second_out = adam_step(
        w_out, part_out, first_out, second_out, out_rate, weight_decay
    )
    new_gains, new_first_gains, new_second_gains = adam_step(
        gains, part_gains, first_gains, second_gains, gain_rate, 0.0
    )
    return (
        out_tokens,
        grad_tokens,
        part_qkv,
        part_out,
        part_gains,
        part_gate_up,
        part_down,
        new_qkv,
        new_out,
        new_gains,
        new_gate_up,
        new_down,
        new_first_qkv,
        new_first_out,
        new_first_gains,
        new_first_gate_up,
        new_first_down,
        new_second_qkv,
        new_second_out,
        new_second_gains,
        new_second_gate_up,
        new_second_down,
    )


def shards_plain(
    tokens,
    cotangent,
    segments,
    expert_ids,
    route_weights,
    w_qkv,
    w_out,
    gains,
    w_gate_up,
    w_down,
    first_moment_projection,
    first_out,
    first_gains,
    first_gate_up,
    first_down,
    second_moment_projection,
    second_out,
    second_gains,
    second_gate_up,
    second_down,
):
    sequence_count = segments.shape[0]
    sequence_length = segments.shape[1]
    groups_expert = lax.axis_size("expert")
    local_experts = EXPERTS // groups_expert
    slot_rows = groups_expert * CAP
    qkv_full, out_full, gain_full = (
        lax.all_gather(w_qkv.astype(jnp.bfloat16), ("dp", "expert"), axis=0, tiled=True),
        lax.all_gather(w_out.astype(jnp.bfloat16), ("dp", "expert"), axis=0, tiled=True),
        lax.all_gather(gains.astype(jnp.bfloat16), ("dp", "expert"), axis=1, tiled=True),
    )
    gate_up_full, down_full = (
        lax.all_gather(w_gate_up.astype(jnp.bfloat16), "dp", axis=1, tiled=True),
        lax.all_gather(w_down.astype(jnp.bfloat16), "dp", axis=1, tiled=True),
    )
    gain_attn = gain_full[0].astype(jnp.float32)
    gain_moe = gain_full[1].astype(jnp.float32)
    cosine_table, sine_table = rotary_tables(sequence_length, HEAD_SIZE // 2)
    inputs = tokens.astype(jnp.float32)
    scale_one = norm_scale(inputs)
    normed_one = (inputs * scale_one * gain_attn).astype(jnp.bfloat16)
    projected_rows = jnp.dot(normed_one, qkv_full, preferred_element_type=jnp.float32)
    query_block, key_rows, value_rows = split_heads(
        projected_rows, sequence_count, sequence_length, cosine_table, sine_table
    )
    index = 0
    attended_seq, logsum = attend(
        query_block[index], key_rows[index], value_rows[index], segments[index]
    )
    pieces = attended_seq.reshape(sequence_length, QUERY_HEADS * HEAD_SIZE)
    logsums = [logsum]
    resid = inputs + jnp.dot(pieces, out_full, preferred_element_type=jnp.float32)
    scale_two = norm_scale(resid)
    normed_two = (resid * scale_two * gain_moe).astype(jnp.bfloat16)
    flat_ids = expert_ids.reshape(-1)
    pair_count = flat_ids.shape[0]
    one_hot = (flat_ids[:, None] == jnp.arange(EXPERTS, dtype=jnp.int32)[None, :]).astype(jnp.int32)
    ranking = jnp.sum(jnp.cumsum(one_hot, 0) * one_hot, 1) - 1
    target = flat_ids * CAP + ranking
    owners = (
        jnp.full((EXPERTS * CAP,), -1, jnp.int32)
        .at[target]
        .set(jnp.arange(pair_count, dtype=jnp.int32))
    )
    filled = (owners >= 0)[:, None]
    safe_owner = jnp.maximum(owners, 0)
    send_rows = jnp.where(filled, normed_two[safe_owner // TOP], jnp.zeros((), jnp.bfloat16))
    received = lax.all_to_all(
        send_rows.reshape(groups_expert, local_experts, CAP, MODEL_WIDTH),
        "expert",
        split_axis=0,
        concat_axis=2,
        tiled=True,
    )
    received = received.reshape(local_experts, slot_rows, MODEL_WIDTH)
    mixed = jnp.einsum("erd,edf->erf", received, gate_up_full, preferred_element_type=jnp.float32)
    gate = mixed[..., :FF]
    upper = mixed[..., FF:]
    hidden = (jax.nn.silu(gate) * upper).astype(jnp.bfloat16)
    expert_out = jnp.einsum(
        "erf,efd->erd", hidden, down_full, preferred_element_type=jnp.float32
    ).astype(jnp.bfloat16)
    returned = lax.all_to_all(
        expert_out.reshape(1, local_experts, slot_rows, MODEL_WIDTH),
        "expert",
        split_axis=2,
        concat_axis=0,
        tiled=True,
    )
    picked = returned.reshape(EXPERTS * CAP, MODEL_WIDTH)[target].reshape(-1, TOP, MODEL_WIDTH)
    out_tokens = resid + jnp.sum(route_weights[..., None] * picked.astype(jnp.float32), 1)
    gate_up_back, down_back = (
        lax.all_gather(w_gate_up.astype(jnp.bfloat16), "dp", axis=1, tiled=True),
        lax.all_gather(w_down.astype(jnp.bfloat16), "dp", axis=1, tiled=True),
    )
    grad_routed = (
        (route_weights[..., None] * cotangent[:, None, :])
        .astype(jnp.bfloat16)
        .reshape(pair_count, MODEL_WIDTH)
    )
    send_grads = jnp.where(filled, grad_routed[safe_owner], jnp.zeros((), jnp.bfloat16))
    grad_expert = lax.all_to_all(
        send_grads.reshape(groups_expert, local_experts, CAP, MODEL_WIDTH),
        "expert",
        split_axis=0,
        concat_axis=2,
        tiled=True,
    )
    grad_expert = grad_expert.reshape(local_experts, slot_rows, MODEL_WIDTH)
    grad_hidden = jnp.einsum(
        "erd,efd->erf", grad_expert, down_back, preferred_element_type=jnp.float32
    )
    grad_down = jnp.einsum("erf,erd->efd", hidden, grad_expert, preferred_element_type=jnp.float32)
    sigma = jax.nn.sigmoid(gate)
    grad_mixed = jnp.concatenate(
        [grad_hidden * upper * sigma * (1.0 + gate * (1.0 - sigma)), grad_hidden * gate * sigma], -1
    ).astype(jnp.bfloat16)
    grad_gate_up = jnp.einsum(
        "erd,erf->edf", received, grad_mixed, preferred_element_type=jnp.float32
    )
    grad_received = jnp.einsum(
        "erf,edf->erd", grad_mixed, gate_up_back, preferred_element_type=jnp.float32
    ).astype(jnp.bfloat16)
    grad_back = lax.all_to_all(
        grad_received.reshape(1, local_experts, slot_rows, MODEL_WIDTH),
        "expert",
        split_axis=2,
        concat_axis=0,
        tiled=True,
    )
    grad_normed_two = jnp.sum(
        grad_back.reshape(EXPERTS * CAP, MODEL_WIDTH)[target]
        .reshape(-1, TOP, MODEL_WIDTH)
        .astype(jnp.float32),
        1,
    )
    hat_two = grad_normed_two * gain_moe
    grad_gain_moe = jnp.sum(grad_normed_two * resid * scale_two, 0)
    grad_resid = cotangent + scale_two * (
        hat_two - resid * scale_two**2 * jnp.mean(hat_two * resid, -1, keepdims=True)
    )
    grad_resid_half = grad_resid.astype(jnp.bfloat16)
    qkv_back, out_back = (
        lax.all_gather(w_qkv.astype(jnp.bfloat16), ("dp", "expert"), axis=0, tiled=True),
        lax.all_gather(w_out.astype(jnp.bfloat16), ("dp", "expert"), axis=0, tiled=True),
    )
    grad_out = jnp.dot(pieces.T, grad_resid_half, preferred_element_type=jnp.float32)
    attended_gradient = jnp.dot(
        grad_resid_half, out_back.T, preferred_element_type=jnp.float32
    ).astype(jnp.bfloat16)
    attended_gradient = attended_gradient.reshape(
        sequence_count, sequence_length, KEY_VALUE_HEADS, QUERY_HEADS // KEY_VALUE_HEADS, HEAD_SIZE
    )
    index = 0
    grad_query, grad_keys, grad_values = attend_back(
        query_block[index],
        key_rows[index],
        value_rows[index],
        segments[index],
        logsums[index],
        attended_gradient[index],
    )
    joined = join_grads(grad_query, grad_keys, grad_values, cosine_table, sine_table)
    grad_qkv = jnp.dot(normed_one.T, joined, preferred_element_type=jnp.float32)
    grad_normed_one = jnp.dot(joined, qkv_back.T, preferred_element_type=jnp.float32)
    hat_one = grad_normed_one * gain_attn
    grad_gain_attn = jnp.sum(grad_normed_one * inputs * scale_one, 0)
    grad_tokens = grad_resid + scale_one * (
        hat_one - inputs * scale_one**2 * jnp.mean(hat_one * inputs, -1, keepdims=True)
    )
    grad_gains = jnp.stack([grad_gain_attn, grad_gain_moe])
    part_qkv, part_out, part_gains = (
        lax.psum_scatter(grad_qkv, ("dp", "expert"), scatter_dimension=0, tiled=True),
        lax.psum_scatter(grad_out, ("dp", "expert"), scatter_dimension=0, tiled=True),
        lax.psum_scatter(grad_gains, ("dp", "expert"), scatter_dimension=1, tiled=True),
    )
    part_gate_up, part_down = (
        lax.psum_scatter(grad_gate_up, "dp", scatter_dimension=1, tiled=True),
        lax.psum_scatter(grad_down, "dp", scatter_dimension=1, tiled=True),
    )
    new_qkv, new_first_qkv, new_second_qkv = adam_step(
        w_qkv, part_qkv, first_moment_projection, second_moment_projection, learn_rate, weight_decay
    )
    new_out, new_first_out, new_second_out = adam_step(
        w_out, part_out, first_out, second_out, out_rate, weight_decay
    )
    new_gains, new_first_gains, new_second_gains = adam_step(
        gains, part_gains, first_gains, second_gains, gain_rate, 0.0
    )
    new_gate_up, new_first_gate_up, new_second_gate_up = adam_step(
        w_gate_up, part_gate_up, first_gate_up, second_gate_up, learn_rate, weight_decay
    )
    new_down, new_first_down, new_second_down = adam_step(
        w_down, part_down, first_down, second_down, learn_rate, weight_decay
    )
    return (
        out_tokens,
        grad_tokens,
        part_qkv,
        part_out,
        part_gains,
        part_gate_up,
        part_down,
        new_qkv,
        new_out,
        new_gains,
        new_gate_up,
        new_down,
        new_first_qkv,
        new_first_out,
        new_first_gains,
        new_first_gate_up,
        new_first_down,
        new_second_qkv,
        new_second_out,
        new_second_gains,
        new_second_gate_up,
        new_second_down,
    )


def solution(mesh):
    by_heads = mesh.shape["dp"] == KEY_VALUE_HEADS and mesh.shape["expert"] == 4
    return jax.shard_map(
        shards_moved if by_heads else shards_plain,
        mesh=mesh,
        in_specs=(
            P(("dp", "expert"), None),
            P(("dp", "expert"), None),
            P(("dp", "expert"), None),
            P(("dp", "expert"), None),
            P(("dp", "expert"), None),
            P(("dp", "expert"), None),
            P(("dp", "expert"), None),
            P(None, ("dp", "expert")),
            P("expert", "dp", None),
            P("expert", "dp", None),
            P(("dp", "expert"), None),
            P(("dp", "expert"), None),
            P(None, ("dp", "expert")),
            P("expert", "dp", None),
            P("expert", "dp", None),
            P(("dp", "expert"), None),
            P(("dp", "expert"), None),
            P(None, ("dp", "expert")),
            P("expert", "dp", None),
            P("expert", "dp", None),
        ),
        out_specs=(
            P(("dp", "expert"), None),
            P(("dp", "expert"), None),
            P(("dp", "expert"), None),
            P(("dp", "expert"), None),
            P(None, ("dp", "expert")),
            P("expert", "dp", None),
            P("expert", "dp", None),
            P(("dp", "expert"), None),
            P(("dp", "expert"), None),
            P(None, ("dp", "expert")),
            P("expert", "dp", None),
            P("expert", "dp", None),
            P(("dp", "expert"), None),
            P(("dp", "expert"), None),
            P(None, ("dp", "expert")),
            P("expert", "dp", None),
            P("expert", "dp", None),
            P(("dp", "expert"), None),
            P(("dp", "expert"), None),
            P(None, ("dp", "expert")),
            P("expert", "dp", None),
            P("expert", "dp", None),
        ),
        check_vma=False,
    )
```

```python
import functools

import jax
import jax.numpy as jnp
import numpy as np
from jax import lax
from jax.experimental import pallas as pl
from jax.experimental.pallas import tpu as pltpu
from jax.sharding import PartitionSpec as P

MODEL_WIDTH = 1536
QUERY_HEADS = 24
KEY_VALUE_HEADS = 8
HEAD_SIZE = 64
FF = 512
EXPERTS = 40
TOP = 8
CAP = 32


eps_norm = 1e-05
beta_one = 0.9
beta_two = 0.95
adam_eps = 1e-08
learn_rate = 0.01
out_rate = 0.04
gain_rate = 0.2
weight_decay = 0.1
correct_one = 1.0 - beta_one**3
correct_two = 1.0 - beta_two**3


def norm_scale(rows):
    return lax.rsqrt(jnp.mean(rows * rows, -1, keepdims=True) + eps_norm)


def rotary_tables(sequence_length, half_dim):
    position = jnp.arange(sequence_length, dtype=jnp.float32)[:, None]
    frequency = 10000.0 ** (-jnp.arange(half_dim, dtype=jnp.float32) / half_dim)
    angles = position * frequency[None, :]
    return (jnp.cos(angles), jnp.sin(angles))


def apply_rotary(value_rows, cosine_table, sine_table, middle):
    half_dim = value_rows.shape[-1] // 2
    shape = (cosine_table.shape[0],) + (1,) * middle + (half_dim,)
    cosine_table = cosine_table.reshape(shape)
    sine_table = sine_table.reshape(shape)
    first = value_rows[..., :half_dim]
    second = value_rows[..., half_dim:]
    return jnp.concatenate(
        [first * cosine_table - second * sine_table, second * cosine_table + first * sine_table], -1
    )


def split_heads(projected_rows, sequence_count, sequence_length, cosine_table, sine_table):
    query_total_width = QUERY_HEADS * HEAD_SIZE
    key_columns_width = KEY_VALUE_HEADS * HEAD_SIZE
    reshaped_rows = projected_rows.reshape(sequence_count, sequence_length, -1)
    query_block = apply_rotary(
        reshaped_rows[..., :query_total_width].reshape(
            sequence_count,
            sequence_length,
            KEY_VALUE_HEADS,
            QUERY_HEADS // KEY_VALUE_HEADS,
            HEAD_SIZE,
        ),
        cosine_table,
        sine_table,
        2,
    )
    key_rows = apply_rotary(
        reshaped_rows[..., query_total_width : query_total_width + key_columns_width].reshape(
            sequence_count, sequence_length, KEY_VALUE_HEADS, HEAD_SIZE
        ),
        cosine_table,
        sine_table,
        1,
    )
    value_rows = reshaped_rows[..., query_total_width + key_columns_width :].reshape(
        sequence_count, sequence_length, KEY_VALUE_HEADS, HEAD_SIZE
    )
    return (
        query_block.astype(jnp.bfloat16),
        key_rows.astype(jnp.bfloat16),
        value_rows.astype(jnp.bfloat16),
    )


def allowed_mask(segment):
    spots = jnp.arange(segment.shape[0])
    return (spots[:, None] >= spots[None, :]) & (segment[:, None] == segment[None, :])


def score_block(query_block, key_rows, segment):
    scores = jnp.einsum(
        "qhgd,khd->hgqk", query_block, key_rows, preferred_element_type=jnp.float32
    ) * query_block.shape[-1] ** (-0.5)
    return jnp.where(allowed_mask(segment)[None, None], scores, -1e30)


def attend(query_block, key_rows, value_rows, segment):
    scores = score_block(query_block, key_rows, segment)
    highest = jnp.max(scores, -1, keepdims=True)
    logsum = highest + jnp.log(jnp.sum(jnp.exp(scores - highest), -1, keepdims=True))
    probs = jnp.exp(scores - logsum).astype(jnp.bfloat16)
    attended = jnp.einsum("hgqk,khd->qhgd", probs, value_rows, preferred_element_type=jnp.float32)
    return (attended.astype(jnp.bfloat16), logsum)


def attend_back(query_block, key_rows, value_rows, segment, logsum, attended_gradient):
    factor = query_block.shape[-1] ** (-0.5)
    probs = jnp.exp(score_block(query_block, key_rows, segment) - logsum)
    grad_probs = jnp.einsum(
        "qhgd,khd->hgqk", attended_gradient, value_rows, preferred_element_type=jnp.float32
    )
    inner_sum = jnp.sum(probs * grad_probs, -1, keepdims=True)
    grad_scores = (probs * (grad_probs - inner_sum) * factor).astype(jnp.bfloat16)
    grad_values = jnp.einsum(
        "hgqk,qhgd->khd",
        probs.astype(jnp.bfloat16),
        attended_gradient,
        preferred_element_type=jnp.float32,
    )
    grad_query = jnp.einsum(
        "hgqk,khd->qhgd", grad_scores, key_rows, preferred_element_type=jnp.float32
    )
    grad_keys = jnp.einsum(
        "hgqk,qhgd->khd", grad_scores, query_block, preferred_element_type=jnp.float32
    )
    return (grad_query, grad_keys, grad_values)


def join_grads(grad_query, grad_keys, grad_values, cosine_table, sine_table):
    sequence_length = grad_query.shape[0]
    grad_query = apply_rotary(grad_query, cosine_table, -sine_table, 2).reshape(sequence_length, -1)
    grad_keys = apply_rotary(grad_keys, cosine_table, -sine_table, 1).reshape(sequence_length, -1)
    return jnp.concatenate(
        [grad_query, grad_keys, grad_values.reshape(sequence_length, -1)], -1
    ).astype(jnp.bfloat16)


def adam_step(weight, grad, first, second, step_rate, shrink):
    first = beta_one * first + (1.0 - beta_one) * grad
    second = beta_two * second + (1.0 - beta_two) * grad * grad
    update = first / correct_one / (jnp.sqrt(second / correct_two) + adam_eps)
    return (weight - step_rate * (update + shrink * weight), first, second)


NARROW = jnp.bfloat16
WIDE = jnp.float32
DISTANCE = (0, 1, -1, 2)
HOP_CORE, HOP_X, HOP_Y = 1, 2, 4


def swap(rows, pick):
    count = lax.axis_size("dp")
    return lax.ppermute(rows, "dp", [(i, i ^ pick(i)) for i in range(count)])


def first_hop(i):
    return HOP_X if i & 1 else HOP_Y


def second_hop(i):
    return HOP_Y if i & 1 else HOP_X


def swap_core(rows):
    return swap(rows, lambda i: HOP_CORE)


def swap_first(rows):
    return swap(rows, first_hop)


def swap_second(rows):
    return swap(rows, second_hop)


def turn(rows, step):
    count = lax.axis_size("expert")
    return lax.ppermute(rows, "expert", [(i, (i + step) % count) for i in range(count)])


def after(values, *others):
    return lax.optimization_barrier((values, others))[0]


def start_ring(block):
    ahead, behind = turn(block, 1), turn(block, -1)
    return [block, ahead, behind, turn(ahead, 1)]


def along_first(part):
    return jnp.concatenate([part, swap_first(part)], 0)


def gather_plane_last(block):
    ahead, behind = turn(block, 1), turn(block, -1)
    far = turn(ahead, 1)
    found = []
    for part in (block, ahead, behind, far):
        pair = jnp.concatenate([part, swap_first(part)], 0)
        found.append((pair, swap_second(pair)))
    return found, far


def gather_ring(block):
    pair = jnp.concatenate([block, swap_first(block)], 0)
    ahead, behind = turn(pair, 1), turn(pair, -1)
    return pair, ahead, behind, turn(ahead, 1)


def ring_sum(parts, gate=()):
    behind = turn(parts[2].astype(NARROW), 1)
    far = turn(parts[3].astype(NARROW), -1)
    ahead = turn((parts[1] + far.astype(WIDE)).astype(NARROW), -1)
    behind, ahead = after((behind, ahead), gate)
    return parts[0] + behind.astype(WIDE) + ahead.astype(WIDE)


def add_second(near, away, gate=()):
    return near + after(swap_second(away.astype(NARROW)), gate).astype(WIDE)


def add_first(rows, gate=()):
    half = rows.shape[0] // 2
    return rows[:half] + after(swap_first(rows[half:].astype(NARROW)), gate).astype(WIDE)


def gathered_sources(count_dp, count_expert):
    table = np.zeros((count_dp, count_expert, 4, 2, 2, 2), np.int32)
    for i in range(count_dp):
        for z in range(count_expert):
            for spot, distance in enumerate(DISTANCE):
                for second in range(2):
                    for first in range(2):
                        plane = i ^ (first_hop(i) * first) ^ (second_hop(i) * second)
                        table[i, z, spot, second, first] = plane, (z - distance) % count_expert
    return table.reshape(count_dp, count_expert, 16, 2)


def split_three(values):
    high = values.astype(NARROW)
    left = values - high.astype(WIDE)
    middle = left.astype(NARROW)
    return [high, middle, (left - middle.astype(WIDE)).astype(NARROW)]


def select_columns(values, chosen):
    rows = values.shape[0]
    parts = jnp.dot(
        jnp.concatenate(split_three(values), 0), chosen, preferred_element_type=jnp.float32
    )
    return parts[:rows] + parts[rows : 2 * rows] + parts[2 * rows :]


def parity_columns(rows, parity):
    count = rows.shape[0]
    query_total_width = QUERY_HEADS * HEAD_SIZE
    key_columns_width = KEY_VALUE_HEADS * HEAD_SIZE
    bounds = (
        (0, query_total_width),
        (query_total_width, query_total_width + key_columns_width),
        (query_total_width + key_columns_width, query_total_width + 2 * key_columns_width),
    )
    return jnp.concatenate(
        [
            rows[:, low:high].reshape(count, KEY_VALUE_HEADS // 2, 2, -1)[:, :, parity]
            .reshape(count, -1)
            for low, high in bounds
        ],
        1,
    )


def join_parities(even, odd):
    count = even.shape[0]
    query_half = QUERY_HEADS * HEAD_SIZE // 2
    key_half = KEY_VALUE_HEADS * HEAD_SIZE // 2
    bounds = (
        (0, query_half),
        (query_half, query_half + key_half),
        (query_half + key_half, query_half + 2 * key_half),
    )
    heads = KEY_VALUE_HEADS // 2
    return jnp.concatenate(
        [
            jnp.stack(
                [
                    even[:, low:high].reshape(count, heads, -1),
                    odd[:, low:high].reshape(count, heads, -1),
                ],
                2,
            ).reshape(count, -1)
            for low, high in bounds
        ],
        1,
    )


def split_head_group(projected_rows, cosine_table, sine_table):
    sequences, length = projected_rows.shape[:2]
    heads = KEY_VALUE_HEADS // 2
    group = QUERY_HEADS // KEY_VALUE_HEADS
    query_width = heads * group * HEAD_SIZE
    key_width = heads * HEAD_SIZE
    query_block = projected_rows[..., :query_width].reshape(
        sequences, length, heads, group, HEAD_SIZE
    )
    key_rows = projected_rows[..., query_width : query_width + key_width].reshape(
        sequences, length, heads, HEAD_SIZE
    )
    value_rows = projected_rows[..., query_width + key_width :].reshape(
        sequences, length, heads, HEAD_SIZE
    )
    query_block = jax.vmap(lambda a: apply_rotary(a, cosine_table, sine_table, 2))(query_block)
    key_rows = jax.vmap(lambda a: apply_rotary(a, cosine_table, sine_table, 1))(key_rows)
    return (
        query_block.astype(jnp.bfloat16),
        key_rows.astype(jnp.bfloat16),
        value_rows.astype(jnp.bfloat16),
    )


def spread_columns_kernel(weight_ref, out_ref):
    chips, _, _, lanes = out_ref.shape
    for chip in range(chips):
        for part in range(2):
            columns = slice(part * FF + chip * lanes, part * FF + (chip + 1) * lanes)
            out_ref[chip, part] = weight_ref[0, :, columns].astype(out_ref.dtype)


def spread_columns(weight, chips):
    experts, rows, both = weight.shape
    lanes = both // 2 // chips
    return pl.pallas_call(
        spread_columns_kernel,
        grid=(experts,),
        in_specs=[pl.BlockSpec((1, rows, both), lambda e: (e, 0, 0))],
        out_specs=pl.BlockSpec((chips, 2, rows, lanes), lambda e: (0, 0, 0, e)),
        out_shape=jax.ShapeDtypeStruct((chips, 2, rows, experts * lanes), jnp.bfloat16),
        cost_estimate=pl.CostEstimate(
            flops=0, bytes_accessed=6 * experts * rows * both, transcendentals=0
        ),
    )(weight)


def stack_rows_kernel(place_ref, mine_ref, theirs_ref, gate_ref, upper_ref, sems):
    core = place_ref[1]
    chips, _, rows, _ = mine_ref.shape
    copies = []
    for chip in range(chips):
        for mate, ref in enumerate((mine_ref, theirs_ref)):
            start = pl.multiple_of((chip * 2 + (core ^ mate)) * rows, rows)
            for part, out_ref in enumerate((gate_ref, upper_ref)):
                copies.append(
                    pltpu.make_async_copy(
                        ref.at[chip, part],
                        out_ref.at[pl.ds(start, rows), :],
                        sems.at[len(copies)],
                    )
                )
    for copy in copies:
        copy.start()
    for copy in copies:
        copy.wait()


def stack_rows(place, mine, theirs):
    chips, _, rows, columns = mine.shape
    shape = jax.ShapeDtypeStruct((2 * chips * rows, columns), jnp.bfloat16)
    return pl.pallas_call(
        stack_rows_kernel,
        in_specs=[pl.BlockSpec(memory_space=pltpu.SMEM)]
        + [pl.BlockSpec(memory_space=pltpu.VMEM)] * 2,
        out_specs=[pl.BlockSpec(memory_space=pl.ANY)] * 2,
        out_shape=[shape] * 2,
        scratch_shapes=[pltpu.SemaphoreType.DMA((4 * chips,))],
        cost_estimate=pl.CostEstimate(
            flops=0, bytes_accessed=16 * chips * rows * columns, transcendentals=0
        ),
    )(place, mine, theirs)


def stack_attention_kernel(*refs):
    blocks, (qkv_ref, gain_ref, out_ref, sems) = refs[:-4], refs[-4:]
    wide, lanes = qkv_ref.shape[1], gain_ref.shape[1]
    owned = out_ref.shape[0] // (2 * len(blocks))
    copies = []
    for i, block in enumerate(blocks):
        for j in range(2):
            top, spot = 3 * owned * j, 2 * i + j
            pairs = (
                (
                    block.at[pl.ds(top, 2 * owned), pl.ds(0, wide)],
                    qkv_ref.at[pl.ds(2 * owned * spot, 2 * owned), :],
                ),
                (
                    block.at[pl.ds(top, 2 * owned), pl.ds(wide, lanes)],
                    gain_ref.at[pl.ds(2 * owned * spot, 2 * owned), :],
                ),
                (
                    block.at[pl.ds(top + 2 * owned, owned), :],
                    out_ref.at[pl.ds(owned * spot, owned), :],
                ),
            )
            for source, target in pairs:
                copies.append(pltpu.make_async_copy(source, target, sems.at[len(copies)]))
    for copy in copies:
        copy.start()
    for copy in copies:
        copy.wait()


def stack_attention(blocks, wide, lanes):
    owned = blocks[0].shape[0] // 6
    count = 2 * len(blocks)
    b16 = lambda r, c: jax.ShapeDtypeStruct((r, c), jnp.bfloat16)
    return pl.pallas_call(
        stack_attention_kernel,
        in_specs=[pl.BlockSpec(memory_space=pltpu.VMEM)] * len(blocks),
        out_specs=[pl.BlockSpec(memory_space=pl.ANY)] * 3,
        out_shape=[
            b16(2 * owned * count, wide),
            b16(2 * owned * count, lanes),
            b16(owned * count, blocks[0].shape[1]),
        ],
        scratch_shapes=[pltpu.SemaphoreType.DMA((3 * count,))],
        cost_estimate=pl.CostEstimate(
            flops=0, bytes_accessed=4 * 3 * owned * count * MODEL_WIDTH, transcendentals=0
        ),
    )(*blocks)


def attention_grads_kernel(
    normed_ref, joined_ref, attended_ref, grads_ref, gain_ref, near_ref, away_ref
):
    contract = (((0,), (0,)), ((), ()))
    wide, lanes = joined_ref.shape[1], gain_ref.shape[1]
    spots = near_ref.shape[0]
    owned = near_ref.shape[1] // 6
    joined, grads = joined_ref[...], grads_ref[...]

    def place(spot, second, first, row, columns, values):
        rows = pl.ds(3 * owned * first + row, values.shape[0])
        if second:
            away_ref[spot, rows, columns] = values.astype(away_ref.dtype)
        else:
            near_ref[spot, rows, columns] = values

    for spot in range(spots):
        rows = 8 * owned
        qkv = lax.dot_general(
            normed_ref[:, rows * spot : rows * (spot + 1)],
            joined,
            contract,
            preferred_element_type=jnp.float32,
        )
        for i in range(4):
            part = slice(2 * owned * i, 2 * owned * (i + 1))
            place(spot, i // 2, i % 2, 0, pl.ds(0, wide), qkv[part])
            gain = gain_ref[pl.ds(rows * spot + 2 * owned * i, 2 * owned), :]
            place(spot, i // 2, i % 2, 0, pl.ds(wide, lanes), gain)
            place(spot, i // 2, i % 2, 0, pl.ds(wide + lanes, lanes), jnp.zeros_like(gain))
        if spot % 2 == 0:
            out = lax.dot_general(
                attended_ref[:, 4 * owned * spot : 4 * owned * (spot + 2)],
                grads,
                contract,
                preferred_element_type=jnp.float32,
            )
            for i in range(8):
                part = slice(owned * i, owned * (i + 1))
                place(
                    spot + i // 4,
                    i // 2 % 2,
                    i % 2,
                    2 * owned,
                    pl.ds(0, out.shape[1]),
                    out[part],
                )


def attention_grads(normed, joined, attended, grads, gain, owned):
    spots = len(DISTANCE)
    shape = (spots, 6 * owned, grads.shape[1])
    return pl.pallas_call(
        attention_grads_kernel,
        out_shape=[
            jax.ShapeDtypeStruct(shape, jnp.float32),
            jax.ShapeDtypeStruct(shape, jnp.bfloat16),
        ],
        compiler_params=pltpu.CompilerParams(vmem_limit_bytes=44 * 1024 * 1024),
        cost_estimate=pl.CostEstimate(
            flops=2 * normed.shape[0] * normed.shape[1] * (joined.shape[1] + grads.shape[1] // 2),
            bytes_accessed=20 * 1024 * 1024,
            transcendentals=0,
        ),
    )(normed, joined, attended, grads, gain)


def expert_kernel(place_ref, *refs, per_step, count):
    source_refs = refs[:count]
    given_ref, gate_ref, upper_ref, down_ref = refs[count : count + 4]
    back_refs = refs[-9 - count : -9]
    hidden_ref, grad_gate_ref, grad_upper_ref, rows_ref, grads_ref, narrow_ref = refs[-9:-3]
    route_ref, out_ref, back_ref = refs[-3:]
    step = pl.program_id(0)
    half, width = source_refs[0].shape

    @pl.when(step == 0)
    def _():
        for i, ref in enumerate(source_refs):
            rows_ref[half * i : half * (i + 1), :] = ref[...]
        grads_ref[...] = given_ref[:, :width]
        lanes = lax.broadcasted_iota(jnp.int32, route_ref.shape, 1)
        expert = (lanes + place_ref[2]).astype(jnp.float32)
        routes = given_ref[:, width:].astype(jnp.float32)
        weights = (
            routes[:, TOP : 2 * TOP]
            + routes[:, 2 * TOP : 3 * TOP]
            + routes[:, 3 * TOP : 4 * TOP]
        )
        dense = jnp.zeros_like(expert)
        for k in range(TOP):
            dense += jnp.where(expert == routes[:, k : k + 1], weights[:, k : k + 1], 0.0)
        route_ref[...] = dense
        out_ref[...] = jnp.zeros_like(out_ref)
        back_ref[...] = jnp.zeros_like(back_ref)

    rows = rows_ref[...]
    grads = grads_ref[...]
    contract_last = (((1,), (1,)), ((), ()))
    gate = jnp.dot(rows, gate_ref[...], preferred_element_type=jnp.float32)
    upper = jnp.dot(rows, upper_ref[...], preferred_element_type=jnp.float32)
    grad_hidden = lax.dot_general(
        grads, down_ref[...], contract_last, preferred_element_type=jnp.float32
    )
    route = route_ref[...]
    lanes = lax.broadcasted_iota(jnp.int32, route.shape, 1)
    columns = gate.shape[1] // per_step
    spread = []
    for i in range(per_step):
        one = jnp.sum(jnp.where(lanes == step * per_step + i, route, 0.0), 1, keepdims=True)
        spread.append(jnp.broadcast_to(one, (route.shape[0], columns)))
    weight = jnp.concatenate(spread, 1)
    sigma = 1.0 / (1.0 + jnp.exp(-gate))
    active = gate * sigma
    hidden = (weight * active * upper).astype(jnp.bfloat16)
    weighted = weight * grad_hidden
    grad_gate = (weighted * upper * sigma * (1.0 + gate * (1.0 - sigma))).astype(jnp.bfloat16)
    grad_upper = (weighted * active).astype(jnp.bfloat16)
    hidden_ref[...] = hidden
    grad_gate_ref[...] = grad_gate
    grad_upper_ref[...] = grad_upper
    out_ref[...] += jnp.dot(hidden, down_ref[...], preferred_element_type=jnp.float32)
    back_ref[...] += lax.dot_general(
        grad_gate, gate_ref[...], contract_last, preferred_element_type=jnp.float32
    ) + lax.dot_general(
        grad_upper, upper_ref[...], contract_last, preferred_element_type=jnp.float32
    )

    @pl.when(step == pl.num_programs(0) - 1)
    def _():
        narrow_ref[...] = out_ref[...].astype(jnp.bfloat16)
        for i, ref in enumerate(back_refs):
            ref[...] = back_ref[half * i : half * (i + 1), :].astype(ref.dtype)


def expert_block(place, spot, second, sources, given, weights, experts, filled):
    gate_w, upper_w, down_w = weights
    half, width = sources[0].shape
    wide = given.shape[1]
    total = gate_w.shape[1]
    per_step = 2
    steps = experts // per_step
    columns = total // steps
    count = len(sources)
    rows = half * count
    every = 2 * half * len(DISTANCE)
    at = (2 * spot + second) // count
    of = lambda p: p[3 + spot] * (2 // count) + second
    dtypes = (jnp.float32, jnp.bfloat16)[second : second + count]
    b16 = lambda r, c: jax.ShapeDtypeStruct((r, c), jnp.bfloat16)
    fixed = pl.BlockSpec((half, width), lambda i, p: (0, 0))
    part = pl.BlockSpec((rows, columns), lambda i, p: (at, i))
    kept = pl.BlockSpec((rows, width), lambda i, p: (at, 0))
    inputs = (place, *sources, given, gate_w, upper_w, down_w)
    return pl.pallas_call(
        functools.partial(expert_kernel, per_step=per_step, count=count),
        grid_spec=pltpu.PrefetchScalarGridSpec(
            num_scalar_prefetch=1,
            grid=(steps,),
            in_specs=[fixed] * count
            + [
                pl.BlockSpec((rows, wide), lambda i, p: (of(p), 0)),
                pl.BlockSpec((width, columns), lambda i, p: (0, i)),
                pl.BlockSpec((width, columns), lambda i, p: (0, i)),
                pl.BlockSpec((columns, width), lambda i, p: (i, 0)),
            ]
            + [pl.BlockSpec(memory_space=pl.ANY)] * len(filled),
            out_specs=[fixed] * count
            + [part] * 3
            + [kept] * 2
            + [pl.BlockSpec((rows, width), lambda i, p: (of(p), 0))],
            scratch_shapes=[
                pltpu.VMEM((rows, wide - width), jnp.float32),
                pltpu.VMEM((rows, width), jnp.float32),
                pltpu.VMEM((rows, width), jnp.float32),
            ],
        ),
        out_shape=[jax.ShapeDtypeStruct((half, width), dtype) for dtype in dtypes]
        + [b16(every, total)] * 3
        + [b16(every, width)] * 3,
        input_output_aliases={len(inputs) + i: count + i for i in range(len(filled))},
        compiler_params=pltpu.CompilerParams(vmem_limit_bytes=48 * 1024 * 1024),
        cost_estimate=pl.CostEstimate(
            flops=2 * rows * width * total * 6,
            bytes_accessed=2 * (3 * width * total + 3 * rows * total + 12 * rows * width),
            transcendentals=rows * total,
        ),
    )(*inputs, *filled)


def column_grads_kernel(
    place_ref, rows_ref, grad_gate_ref, grad_upper_ref, *refs
):
    keep_ref, give_ref, full_ref = refs[-3:]
    core = place_ref[1]
    contract = (((0,), (0,)), ((), ()))
    chips, _, plane_rows, _ = keep_ref.shape
    for part, ref in enumerate((grad_gate_ref, grad_upper_ref)):
        full_ref[...] = lax.dot_general(
            rows_ref[...], ref[...], contract, preferred_element_type=jnp.float32
        )
        for chip in range(chips):
            mine = pl.multiple_of((2 * chip + core) * plane_rows, plane_rows)
            theirs = pl.multiple_of((2 * chip + 1 - core) * plane_rows, plane_rows)
            keep_ref[chip, part] = full_ref[pl.ds(mine, plane_rows), :]
            give_ref[chip, part] = full_ref[pl.ds(theirs, plane_rows), :].astype(give_ref.dtype)


def column_grads(place, step, steps, rows_all, grad_gate, grad_upper, chips, filled):
    tokens, width = rows_all.shape
    total = grad_gate.shape[1]
    columns = total // steps
    plane_rows = width // (2 * chips)
    part = pl.BlockSpec((tokens, columns), lambda i, p: (0, step))
    wide = pl.BlockSpec((chips, 2, plane_rows, columns), lambda i, p: (0, 0, 0, step))
    shape = (chips, 2, plane_rows, total)
    return pl.pallas_call(
        column_grads_kernel,
        grid_spec=pltpu.PrefetchScalarGridSpec(
            num_scalar_prefetch=1,
            grid=(1,),
            in_specs=[pl.BlockSpec((tokens, width), lambda i, p: (0, 0)), part, part]
            + [pl.BlockSpec(memory_space=pl.ANY)] * len(filled),
            out_specs=[wide, wide],
            scratch_shapes=[pltpu.VMEM((width, columns), jnp.float32)],
        ),
        out_shape=[
            jax.ShapeDtypeStruct(shape, jnp.float32),
            jax.ShapeDtypeStruct(shape, jnp.bfloat16),
        ],
        input_output_aliases={4 + i: i for i in range(len(filled))},
        compiler_params=pltpu.CompilerParams(vmem_limit_bytes=36 * 1024 * 1024),
        cost_estimate=pl.CostEstimate(
            flops=4 * tokens * width * columns,
            bytes_accessed=2 * tokens * (width + 2 * columns) + 6 * 2 * width * columns,
            transcendentals=0,
        ),
    )(place, rows_all, grad_gate, grad_upper, *filled)


def down_grads_kernel(place_ref, grads_ref, hidden_ref, keep_ref, give_ref, full_ref):
    core = place_ref[1]
    full_ref[...] = lax.dot_general(
        hidden_ref[...],
        grads_ref[...],
        (((0,), (0,)), ((), ())),
        preferred_element_type=jnp.float32,
    )
    experts, down_rows, _ = keep_ref.shape
    for e in range(experts):
        mine = pl.multiple_of((2 * e + core) * down_rows, down_rows)
        theirs = pl.multiple_of((2 * e + 1 - core) * down_rows, down_rows)
        keep_ref[e] = full_ref[pl.ds(mine, down_rows), :]
        give_ref[e] = full_ref[pl.ds(theirs, down_rows), :]


def down_grads(place, steps, grads_all, hidden, experts):
    tokens, width = grads_all.shape
    total = hidden.shape[1]
    columns = total // steps
    per_step = experts // steps
    down_rows = total // experts // 2
    down = pl.BlockSpec((per_step, down_rows, width), lambda i, p: (i, 0, 0))
    return pl.pallas_call(
        down_grads_kernel,
        grid_spec=pltpu.PrefetchScalarGridSpec(
            num_scalar_prefetch=1,
            grid=(steps,),
            in_specs=[
                pl.BlockSpec((tokens, width), lambda i, p: (0, 0)),
                pl.BlockSpec((tokens, columns), lambda i, p: (0, i)),
            ],
            out_specs=[down, down],
            scratch_shapes=[pltpu.VMEM((columns, width), jnp.float32)],
        ),
        out_shape=[jax.ShapeDtypeStruct((experts, down_rows, width), jnp.float32)] * 2,
        compiler_params=pltpu.CompilerParams(vmem_limit_bytes=36 * 1024 * 1024),
        cost_estimate=pl.CostEstimate(
            flops=2 * tokens * width * total,
            bytes_accessed=2 * tokens * (width + total) + 4 * width * total,
            transcendentals=0,
        ),
    )(place, grads_all, hidden)


def adam_columns_kernel(w_ref, first_ref, second_ref, grad_ref, *outs):
    chips, _, _, lanes = grad_ref.shape
    for chip in range(chips):
        for part in range(2):
            columns = slice(part * FF + chip * lanes, part * FF + (chip + 1) * lanes)
            grad = grad_ref[chip, part].astype(jnp.float32)
            found = adam_step(
                w_ref[0, :, columns],
                grad,
                first_ref[0, :, columns],
                second_ref[0, :, columns],
                learn_rate,
                weight_decay,
            )
            for out_ref, value in zip(outs, (grad,) + found):
                out_ref[0, :, columns] = value


def adam_columns(weight, first, second, grads):
    experts, rows, both = weight.shape
    chips = grads.shape[0]
    lanes = grads.shape[3] // experts
    block = pl.BlockSpec((1, rows, both), lambda e: (e, 0, 0))
    return pl.pallas_call(
        adam_columns_kernel,
        grid=(experts,),
        in_specs=[block] * 3 + [pl.BlockSpec((chips, 2, rows, lanes), lambda e: (0, 0, 0, e))],
        out_specs=[block] * 4,
        out_shape=[jax.ShapeDtypeStruct(weight.shape, jnp.float32)] * 4,
        compiler_params=pltpu.CompilerParams(vmem_limit_bytes=56 * 1024 * 1024),
        cost_estimate=pl.CostEstimate(
            flops=20 * experts * rows * both,
            bytes_accessed=30 * experts * rows * both,
            transcendentals=experts * rows * both,
        ),
    )(weight, first, second, grads)


def shards_moved(
    tokens,
    cotangent,
    segments,
    expert_ids,
    route_weights,
    w_qkv,
    w_out,
    gains,
    w_gate_up,
    w_down,
    first_moment_projection,
    first_out,
    first_gains,
    first_gate_up,
    first_down,
    second_moment_projection,
    second_out,
    second_gains,
    second_gate_up,
    second_down,
):
    sequence_length = segments.shape[1]
    count_dp, count_expert = lax.axis_size("dp"), lax.axis_size("expert")
    place_dp, place_expert = lax.axis_index("dp"), lax.axis_index("expert")
    core = place_dp % 2
    chip = place_dp // 2
    chips = count_dp // 2
    local_experts = EXPERTS // count_expert
    owned = w_qkv.shape[0]
    half_columns = w_qkv.shape[1] // 2
    half_width = MODEL_WIDTH // 2
    lane_pad = 128

    narrow_qkv = w_qkv.astype(NARROW)
    even_columns, odd_columns = parity_columns(narrow_qkv, 0), parity_columns(narrow_qkv, 1)
    gain_columns = jnp.pad(gains.astype(NARROW).T, ((0, 0), (0, lane_pad - 2)))
    kept = jnp.where(core == 0, even_columns, odd_columns)
    given = jnp.where(core == 0, odd_columns, even_columns)
    rest = jnp.zeros((owned, MODEL_WIDTH - half_columns - lane_pad), NARROW)
    taken = swap_core(jnp.concatenate([given, gain_columns], 1))
    block = jnp.concatenate(
        [
            jnp.concatenate([kept, gain_columns, rest], 1),
            jnp.concatenate([taken, rest], 1),
            w_out.astype(NARROW),
        ],
        0,
    )
    share = local_experts * (FF // chips)
    attention_ring = start_ring(block)
    attention_pairs = [along_first(part) for part in attention_ring[:2]]
    pieces = spread_columns(after(w_gate_up, taken), chips)
    routes = jnp.concatenate([expert_ids.astype(NARROW)] + split_three(route_weights), 1)
    cotangent_rows = jnp.concatenate(
        [
            cotangent.astype(NARROW),
            jnp.pad(routes, ((0, 0), (0, lane_pad - routes.shape[1]))),
        ],
        1,
    )
    cotangent_pair = along_first(cotangent_rows)
    cotangent_here = jnp.concatenate([cotangent_pair, swap_second(cotangent_pair)], 0)
    cotangent_all = lax.all_gather(
        after(cotangent_here, attention_ring), "expert", axis=0, tiled=True
    )
    attention_pairs.append(along_first(attention_ring[2]))
    attention_pairs.append(along_first(after(attention_ring[3], (pieces, cotangent_here))))
    attention_blocks = [(pair, swap_second(pair)) for pair in attention_pairs]

    sources = jnp.asarray(gathered_sources(count_dp, count_expert))[place_dp, place_expert]
    from_dp, from_expert = sources[:, 0], sources[:, 1]
    row_in = jnp.arange(owned, dtype=jnp.int32)
    feature = (
        ((from_dp[:, None] ^ jnp.arange(2, dtype=jnp.int32)[None, :]) * count_expert
         + from_expert[:, None])[:, :, None] * owned + row_in
    ).reshape(-1)
    head_feature = (
        ((from_dp // 2 * count_expert + from_expert) * owned)[:, None] + row_in
    ).reshape(-1)
    places = jnp.arange(MODEL_WIDTH, dtype=jnp.int32)
    to_gathered = (places[:, None] == feature[None, :]).astype(NARROW)
    from_gathered = (feature[:, None] == places[None, :]).astype(NARROW)
    head_places = places[: half_width]
    heads_to_gathered = (head_places[:, None] == head_feature[None, :]).astype(NARROW)
    heads_from_gathered = (head_feature[:, None] == head_places[None, :]).astype(NARROW)

    found_at = (place_expert - jnp.asarray(DISTANCE, jnp.int32)) % count_expert
    place = jnp.concatenate(
        [jnp.stack([chip, core, place_expert * local_experts]).astype(jnp.int32), found_at]
    )
    parities = [list(range(i, count_dp, 2)) for i in range(2)]
    pieces = lax.all_to_all(
        after(pieces, attention_blocks[2][1]), "dp", 0, 0, axis_index_groups=parities, tiled=True
    )
    down_mine = after(w_down, attention_pairs[0]).astype(NARROW)
    down_theirs = swap_core(down_mine)
    down_w = jnp.where(
        core == 0,
        jnp.concatenate([down_mine, down_theirs], 1),
        jnp.concatenate([down_theirs, down_mine], 1),
    ).reshape(share, MODEL_WIDTH)
    attention_blocks = after(attention_blocks, down_w)

    cosine_table, sine_table = rotary_tables(sequence_length, HEAD_SIZE // 2)
    inputs = tokens.astype(WIDE)
    pair_tokens = jnp.concatenate([tokens, swap_core(tokens)], 0)
    pair_segments = jnp.concatenate([segments, swap_core(segments)], 0)
    scale_pair = norm_scale(pair_tokens.astype(WIDE))
    scale_one = scale_pair[:sequence_length]
    pair_gathered = jnp.dot(pair_tokens, to_gathered, preferred_element_type=jnp.float32)
    blocks = [half for pair in attention_blocks for half in pair]
    qkv_here, gain_here, out_here = stack_attention(blocks, half_columns, lane_pad)
    gain_here = gain_here[:, :2].T
    gain_attn = gain_here[0].astype(WIDE)
    gains_placed = jnp.dot(gain_here, from_gathered, preferred_element_type=jnp.float32)
    gain_moe = gains_placed[1]
    normed_one = (pair_gathered * scale_pair * gain_attn).astype(NARROW)
    projected = jnp.dot(normed_one, qkv_here, preferred_element_type=jnp.float32)
    query_block, key_rows, value_rows = split_head_group(
        projected.reshape(2, sequence_length, -1), cosine_table, sine_table
    )
    attended, logsums = jax.vmap(attend)(query_block, key_rows, value_rows, pair_segments)
    attended = attended.reshape(2 * sequence_length, half_width)
    attended = jnp.dot(attended, heads_to_gathered, preferred_element_type=jnp.float32).astype(
        NARROW
    )
    resid_parts = jnp.dot(attended, out_here, preferred_element_type=jnp.float32)
    resid = inputs + resid_parts[:sequence_length] + swap_core(resid_parts[sequence_length:])
    scale_two = norm_scale(resid)
    normed_two = (resid * scale_two * gain_moe).astype(NARROW)
    normed_two = after(normed_two, pieces)

    normed_ring = [normed_two] + [turn(normed_two, distance) for distance in DISTANCE[1:]]
    gate_w, upper_w = stack_rows(place, pieces, after(swap_core(pieces), normed_two))
    back_parts, filled = [], []
    second_parts, begun = [], ()
    for spot, part in enumerate(normed_ring):
        near = along_first(after(part, begun))
        away = swap_second(near)
        if spot >= 2:
            near = after(near, (second_parts[spot - 2], back_parts[: spot - 2]))
        back = []
        for second, sources in ((0, [near]), (1, [away])) if spot < 2 else ((0, [near, away]),):
            done = expert_block(
                place,
                spot,
                second,
                sources,
                cotangent_all,
                (gate_w, upper_w, down_w),
                local_experts,
                filled,
            )
            back += done[: len(sources)]
            filled = done[len(sources) :]
            begun = begun or (back[0],)
        if spot < len(DISTANCE) - 1:
            second_parts.append(add_second(*back))
            back_parts.append(add_first(second_parts[-1]))
    hidden, grad_gate, grad_upper, rows_all, grads_all, out_all = filled
    steps = local_experts // 2
    kept_grads = []
    for step in range(steps):
        kept_grads = column_grads(
            place, step, steps, rows_all, grad_gate, grad_upper, chips, kept_grads
        )
        if step == 0:
            last = add_second(*back, kept_grads)
        elif step == 1:
            back_parts.append(add_first(last, kept_grads))
        elif step == 2:
            found = [
                turn(part.astype(NARROW), -distance)
                for part, distance in zip(back_parts[1:], DISTANCE[1:])
            ]
            grad_normed_two = back_parts[0] + sum(
                part.astype(WIDE) for part in after(found, kept_grads)
            )
            rows_all = after(rows_all, grad_normed_two)
    keep, give = kept_grads
    taken = swap_core(give)
    expert_sums = (keep + taken.astype(WIDE)).astype(NARROW)
    parities = [list(range(i, count_dp, 2)) for i in range(2)]
    collected = lax.all_to_all(
        expert_sums, "dp", 0, 0, axis_index_groups=parities, tiled=True
    )
    out_sums = lax.psum_scatter(
        after(out_all, grad_normed_two), "expert", scatter_dimension=0, tiled=True
    )

    hat_two = grad_normed_two * gain_moe
    grad_gain_moe = jnp.sum(grad_normed_two * resid * scale_two, 0)
    grad_resid = cotangent + scale_two * (
        hat_two - resid * scale_two**2 * jnp.mean(hat_two * resid, -1, keepdims=True)
    )
    grad_resid_half = grad_resid.astype(NARROW)
    pair_grads = jnp.concatenate([grad_resid_half, swap_core(grad_resid_half)], 0)
    attended_gradient = lax.dot_general(
        pair_grads, out_here, (((1,), (1,)), ((), ())), preferred_element_type=jnp.float32
    ).astype(NARROW)
    attended_gradient = (
        jnp.dot(attended_gradient, heads_from_gathered, preferred_element_type=jnp.float32)
        .astype(NARROW)
        .reshape(query_block.shape)
    )
    grad_query, grad_keys, grad_values = jax.vmap(attend_back)(
        query_block, key_rows, value_rows, pair_segments, logsums, attended_gradient
    )
    joined = jax.vmap(lambda a, b, c: join_grads(a, b, c, cosine_table, sine_table))(
        grad_query, grad_keys, grad_values
    ).reshape(2 * sequence_length, -1)
    joined = after(joined, expert_sums)
    grad_normed_parts = lax.dot_general(
        joined, qkv_here, (((1,), (1,)), ((), ())), preferred_element_type=jnp.float32
    )
    grad_gain_attn = jnp.sum(grad_normed_parts * pair_gathered * scale_pair, 0)
    gain_parts = jnp.stack(
        [grad_gain_attn, select_columns(grad_gain_moe[None], to_gathered)[0]], 1
    )
    near_parts, away_parts = attention_grads(
        normed_one,
        joined,
        attended,
        pair_grads,
        jnp.pad(gain_parts, ((0, 0), (0, lane_pad - 2))),
        owned,
    )
    keep_down, give_down = down_grads(
        place, steps, after(grads_all, near_parts), hidden, local_experts
    )
    part_down = keep_down + swap_core(give_down)
    new_down, new_first_down, new_second_down = adam_step(
        w_down, part_down, first_down, second_down, learn_rate, weight_decay
    )
    part_gate_up, new_gate_up, new_first_gate_up, new_second_gate_up = adam_columns(
        w_gate_up, first_gate_up, second_gate_up, after(collected, near_parts)
    )
    in_plane = [None] * len(DISTANCE)
    for i in (3, 1, 2, 0):
        in_plane[i] = add_second(near_parts[i], away_parts[i], new_gate_up)
    for i in (3, 1, 2, 0):
        in_plane[i] = add_first(in_plane[i])
    out_sums = after(out_sums, in_plane[3]).astype(WIDE)
    out_half = out_sums.shape[0] // 2
    out_sums = add_second(out_sums[:out_half], out_sums[out_half:])
    summed = ring_sum(in_plane, (new_down, out_sums))
    out_tokens = resid + add_first(out_sums, summed)
    here, there, part_out = summed[:owned], summed[owned : 2 * owned], summed[2 * owned :]
    there = swap_core(there[:, : half_columns + lane_pad])
    part_gains = (
        here[:, half_columns : half_columns + 2] + there[:, half_columns : half_columns + 2]
    ).T
    here, there = here[:, :half_columns], there[:, :half_columns]
    part_qkv = join_parities(
        jnp.where(core == 0, here, there), jnp.where(core == 0, there, here)
    )

    grad_normed_parts = select_columns(grad_normed_parts, from_gathered)
    grad_normed_one = grad_normed_parts[:sequence_length] + swap_core(
        grad_normed_parts[sequence_length:]
    )
    hat_one = grad_normed_one * gains_placed[0]
    grad_tokens = grad_resid + scale_one * (
        hat_one - inputs * scale_one**2 * jnp.mean(hat_one * inputs, -1, keepdims=True)
    )

    new_qkv, new_first_qkv, new_second_qkv = adam_step(
        w_qkv, part_qkv, first_moment_projection, second_moment_projection, learn_rate, weight_decay
    )
    new_out, new_first_out, new_second_out = adam_step(
        w_out, part_out, first_out, second_out, out_rate, weight_decay
    )
    new_gains, new_first_gains, new_second_gains = adam_step(
        gains, part_gains, first_gains, second_gains, gain_rate, 0.0
    )
    return (
        out_tokens,
        grad_tokens,
        part_qkv,
        part_out,
        part_gains,
        part_gate_up,
        part_down,
        new_qkv,
        new_out,
        new_gains,
        new_gate_up,
        new_down,
        new_first_qkv,
        new_first_out,
        new_first_gains,
        new_first_gate_up,
        new_first_down,
        new_second_qkv,
        new_second_out,
        new_second_gains,
        new_second_gate_up,
        new_second_down,
    )


def shards_plain(
    tokens,
    cotangent,
    segments,
    expert_ids,
    route_weights,
    w_qkv,
    w_out,
    gains,
    w_gate_up,
    w_down,
    first_moment_projection,
    first_out,
    first_gains,
    first_gate_up,
    first_down,
    second_moment_projection,
    second_out,
    second_gains,
    second_gate_up,
    second_down,
):
    sequence_count = segments.shape[0]
    sequence_length = segments.shape[1]
    groups_expert = lax.axis_size("expert")
    local_experts = EXPERTS // groups_expert
    slot_rows = groups_expert * CAP
    qkv_full, out_full, gain_full = (
        lax.all_gather(w_qkv.astype(jnp.bfloat16), ("dp", "expert"), axis=0, tiled=True),
        lax.all_gather(w_out.astype(jnp.bfloat16), ("dp", "expert"), axis=0, tiled=True),
        lax.all_gather(gains.astype(jnp.bfloat16), ("dp", "expert"), axis=1, tiled=True),
    )
    gate_up_full, down_full = (
        lax.all_gather(w_gate_up.astype(jnp.bfloat16), "dp", axis=1, tiled=True),
        lax.all_gather(w_down.astype(jnp.bfloat16), "dp", axis=1, tiled=True),
    )
    gain_attn = gain_full[0].astype(jnp.float32)
    gain_moe = gain_full[1].astype(jnp.float32)
    cosine_table, sine_table = rotary_tables(sequence_length, HEAD_SIZE // 2)
    inputs = tokens.astype(jnp.float32)
    scale_one = norm_scale(inputs)
    normed_one = (inputs * scale_one * gain_attn).astype(jnp.bfloat16)
    projected_rows = jnp.dot(normed_one, qkv_full, preferred_element_type=jnp.float32)
    query_block, key_rows, value_rows = split_heads(
        projected_rows, sequence_count, sequence_length, cosine_table, sine_table
    )
    index = 0
    attended_seq, logsum = attend(
        query_block[index], key_rows[index], value_rows[index], segments[index]
    )
    pieces = attended_seq.reshape(sequence_length, QUERY_HEADS * HEAD_SIZE)
    logsums = [logsum]
    resid = inputs + jnp.dot(pieces, out_full, preferred_element_type=jnp.float32)
    scale_two = norm_scale(resid)
    normed_two = (resid * scale_two * gain_moe).astype(jnp.bfloat16)
    flat_ids = expert_ids.reshape(-1)
    pair_count = flat_ids.shape[0]
    one_hot = (flat_ids[:, None] == jnp.arange(EXPERTS, dtype=jnp.int32)[None, :]).astype(jnp.int32)
    ranking = jnp.sum(jnp.cumsum(one_hot, 0) * one_hot, 1) - 1
    target = flat_ids * CAP + ranking
    owners = (
        jnp.full((EXPERTS * CAP,), -1, jnp.int32)
        .at[target]
        .set(jnp.arange(pair_count, dtype=jnp.int32))
    )
    filled = (owners >= 0)[:, None]
    safe_owner = jnp.maximum(owners, 0)
    send_rows = jnp.where(filled, normed_two[safe_owner // TOP], jnp.zeros((), jnp.bfloat16))
    received = lax.all_to_all(
        send_rows.reshape(groups_expert, local_experts, CAP, MODEL_WIDTH),
        "expert",
        split_axis=0,
        concat_axis=2,
        tiled=True,
    )
    received = received.reshape(local_experts, slot_rows, MODEL_WIDTH)
    mixed = jnp.einsum("erd,edf->erf", received, gate_up_full, preferred_element_type=jnp.float32)
    gate = mixed[..., :FF]
    upper = mixed[..., FF:]
    hidden = (jax.nn.silu(gate) * upper).astype(jnp.bfloat16)
    expert_out = jnp.einsum(
        "erf,efd->erd", hidden, down_full, preferred_element_type=jnp.float32
    ).astype(jnp.bfloat16)
    returned = lax.all_to_all(
        expert_out.reshape(1, local_experts, slot_rows, MODEL_WIDTH),
        "expert",
        split_axis=2,
        concat_axis=0,
        tiled=True,
    )
    picked = returned.reshape(EXPERTS * CAP, MODEL_WIDTH)[target].reshape(-1, TOP, MODEL_WIDTH)
    out_tokens = resid + jnp.sum(route_weights[..., None] * picked.astype(jnp.float32), 1)
    gate_up_back, down_back = (
        lax.all_gather(w_gate_up.astype(jnp.bfloat16), "dp", axis=1, tiled=True),
        lax.all_gather(w_down.astype(jnp.bfloat16), "dp", axis=1, tiled=True),
    )
    grad_routed = (
        (route_weights[..., None] * cotangent[:, None, :])
        .astype(jnp.bfloat16)
        .reshape(pair_count, MODEL_WIDTH)
    )
    send_grads = jnp.where(filled, grad_routed[safe_owner], jnp.zeros((), jnp.bfloat16))
    grad_expert = lax.all_to_all(
        send_grads.reshape(groups_expert, local_experts, CAP, MODEL_WIDTH),
        "expert",
        split_axis=0,
        concat_axis=2,
        tiled=True,
    )
    grad_expert = grad_expert.reshape(local_experts, slot_rows, MODEL_WIDTH)
    grad_hidden = jnp.einsum(
        "erd,efd->erf", grad_expert, down_back, preferred_element_type=jnp.float32
    )
    grad_down = jnp.einsum("erf,erd->efd", hidden, grad_expert, preferred_element_type=jnp.float32)
    sigma = jax.nn.sigmoid(gate)
    grad_mixed = jnp.concatenate(
        [grad_hidden * upper * sigma * (1.0 + gate * (1.0 - sigma)), grad_hidden * gate * sigma], -1
    ).astype(jnp.bfloat16)
    grad_gate_up = jnp.einsum(
        "erd,erf->edf", received, grad_mixed, preferred_element_type=jnp.float32
    )
    grad_received = jnp.einsum(
        "erf,edf->erd", grad_mixed, gate_up_back, preferred_element_type=jnp.float32
    ).astype(jnp.bfloat16)
    grad_back = lax.all_to_all(
        grad_received.reshape(1, local_experts, slot_rows, MODEL_WIDTH),
        "expert",
        split_axis=2,
        concat_axis=0,
        tiled=True,
    )
    grad_normed_two = jnp.sum(
        grad_back.reshape(EXPERTS * CAP, MODEL_WIDTH)[target]
        .reshape(-1, TOP, MODEL_WIDTH)
        .astype(jnp.float32),
        1,
    )
    hat_two = grad_normed_two * gain_moe
    grad_gain_moe = jnp.sum(grad_normed_two * resid * scale_two, 0)
    grad_resid = cotangent + scale_two * (
        hat_two - resid * scale_two**2 * jnp.mean(hat_two * resid, -1, keepdims=True)
    )
    grad_resid_half = grad_resid.astype(jnp.bfloat16)
    qkv_back, out_back = (
        lax.all_gather(w_qkv.astype(jnp.bfloat16), ("dp", "expert"), axis=0, tiled=True),
        lax.all_gather(w_out.astype(jnp.bfloat16), ("dp", "expert"), axis=0, tiled=True),
    )
    grad_out = jnp.dot(pieces.T, grad_resid_half, preferred_element_type=jnp.float32)
    attended_gradient = jnp.dot(
        grad_resid_half, out_back.T, preferred_element_type=jnp.float32
    ).astype(jnp.bfloat16)
    attended_gradient = attended_gradient.reshape(
        sequence_count, sequence_length, KEY_VALUE_HEADS, QUERY_HEADS // KEY_VALUE_HEADS, HEAD_SIZE
    )
    index = 0
    grad_query, grad_keys, grad_values = attend_back(
        query_block[index],
        key_rows[index],
        value_rows[index],
        segments[index],
        logsums[index],
        attended_gradient[index],
    )
    joined = join_grads(grad_query, grad_keys, grad_values, cosine_table, sine_table)
    grad_qkv = jnp.dot(normed_one.T, joined, preferred_element_type=jnp.float32)
    grad_normed_one = jnp.dot(joined, qkv_back.T, preferred_element_type=jnp.float32)
    hat_one = grad_normed_one * gain_attn
    grad_gain_attn = jnp.sum(grad_normed_one * inputs * scale_one, 0)
    grad_tokens = grad_resid + scale_one * (
        hat_one - inputs * scale_one**2 * jnp.mean(hat_one * inputs, -1, keepdims=True)
    )
    grad_gains = jnp.stack([grad_gain_attn, grad_gain_moe])
    part_qkv, part_out, part_gains = (
        lax.psum_scatter(grad_qkv, ("dp", "expert"), scatter_dimension=0, tiled=True),
        lax.psum_scatter(grad_out, ("dp", "expert"), scatter_dimension=0, tiled=True),
        lax.psum_scatter(grad_gains, ("dp", "expert"), scatter_dimension=1, tiled=True),
    )
    part_gate_up, part_down = (
        lax.psum_scatter(grad_gate_up, "dp", scatter_dimension=1, tiled=True),
        lax.psum_scatter(grad_down, "dp", scatter_dimension=1, tiled=True),
    )
    new_qkv, new_first_qkv, new_second_qkv = adam_step(
        w_qkv, part_qkv, first_moment_projection, second_moment_projection, learn_rate, weight_decay
    )
    new_out, new_first_out, new_second_out = adam_step(
        w_out, part_out, first_out, second_out, out_rate, weight_decay
    )
    new_gains, new_first_gains, new_second_gains = adam_step(
        gains, part_gains, first_gains, second_gains, gain_rate, 0.0
    )
    new_gate_up, new_first_gate_up, new_second_gate_up = adam_step(
        w_gate_up, part_gate_up, first_gate_up, second_gate_up, learn_rate, weight_decay
    )
    new_down, new_first_down, new_second_down = adam_step(
        w_down, part_down, first_down, second_down, learn_rate, weight_decay
    )
    return (
        out_tokens,
        grad_tokens,
        part_qkv,
        part_out,
        part_gains,
        part_gate_up,
        part_down,
        new_qkv,
        new_out,
        new_gains,
        new_gate_up,
        new_down,
        new_first_qkv,
        new_first_out,
        new_first_gains,
        new_first_gate_up,
        new_first_down,
        new_second_qkv,
        new_second_out,
        new_second_gains,
        new_second_gate_up,
        new_second_down,
    )


def solution(mesh):
    by_heads = mesh.shape["dp"] == KEY_VALUE_HEADS and mesh.shape["expert"] == 4
    return jax.shard_map(
        shards_moved if by_heads else shards_plain,
        mesh=mesh,
        in_specs=(
            P(("dp", "expert"), None),
            P(("dp", "expert"), None),
            P(("dp", "expert"), None),
            P(("dp", "expert"), None),
            P(("dp", "expert"), None),
            P(("dp", "expert"), None),
            P(("dp", "expert"), None),
            P(None, ("dp", "expert")),
            P("expert", "dp", None),
            P("expert", "dp", None),
            P(("dp", "expert"), None),
            P(("dp", "expert"), None),
            P(None, ("dp", "expert")),
            P("expert", "dp", None),
            P("expert", "dp", None),
            P(("dp", "expert"), None),
            P(("dp", "expert"), None),
            P(None, ("dp", "expert")),
            P("expert", "dp", None),
            P("expert", "dp", None),
        ),
        out_specs=(
            P(("dp", "expert"), None),
            P(("dp", "expert"), None),
            P(("dp", "expert"), None),
            P(("dp", "expert"), None),
            P(None, ("dp", "expert")),
            P("expert", "dp", None),
            P("expert", "dp", None),
            P(("dp", "expert"), None),
            P(("dp", "expert"), None),
            P(None, ("dp", "expert")),
            P("expert", "dp", None),
            P("expert", "dp", None),
            P(("dp", "expert"), None),
            P(("dp", "expert"), None),
            P(None, ("dp", "expert")),
            P("expert", "dp", None),
            P("expert", "dp", None),
            P(("dp", "expert"), None),
            P(("dp", "expert"), None),
            P(None, ("dp", "expert")),
            P("expert", "dp", None),
            P("expert", "dp", None),
        ),
        check_vma=False,
    )
```

```python
import functools

import jax
import jax.numpy as jnp
import numpy as np
from jax import lax
from jax.experimental import pallas as pl
from jax.experimental.pallas import tpu as pltpu
from jax.sharding import PartitionSpec as P

MODEL_WIDTH = 1536
QUERY_HEADS = 24
KEY_VALUE_HEADS = 8
HEAD_SIZE = 64
FF = 512
EXPERTS = 40
TOP = 8
CAP = 32


eps_norm = 1e-05
beta_one = 0.9
beta_two = 0.95
adam_eps = 1e-08
learn_rate = 0.01
out_rate = 0.04
gain_rate = 0.2
weight_decay = 0.1
correct_one = 1.0 - beta_one**3
correct_two = 1.0 - beta_two**3


def norm_scale(rows):
    return lax.rsqrt(jnp.mean(rows * rows, -1, keepdims=True) + eps_norm)


def rotary_tables(sequence_length, half_dim):
    position = jnp.arange(sequence_length, dtype=jnp.float32)[:, None]
    frequency = 10000.0 ** (-jnp.arange(half_dim, dtype=jnp.float32) / half_dim)
    angles = position * frequency[None, :]
    return (jnp.cos(angles), jnp.sin(angles))


def apply_rotary(value_rows, cosine_table, sine_table, middle):
    half_dim = value_rows.shape[-1] // 2
    shape = (cosine_table.shape[0],) + (1,) * middle + (half_dim,)
    cosine_table = cosine_table.reshape(shape)
    sine_table = sine_table.reshape(shape)
    first = value_rows[..., :half_dim]
    second = value_rows[..., half_dim:]
    return jnp.concatenate(
        [first * cosine_table - second * sine_table, second * cosine_table + first * sine_table], -1
    )


def split_heads(projected_rows, sequence_count, sequence_length, cosine_table, sine_table):
    query_total_width = QUERY_HEADS * HEAD_SIZE
    key_columns_width = KEY_VALUE_HEADS * HEAD_SIZE
    reshaped_rows = projected_rows.reshape(sequence_count, sequence_length, -1)
    query_block = apply_rotary(
        reshaped_rows[..., :query_total_width].reshape(
            sequence_count,
            sequence_length,
            KEY_VALUE_HEADS,
            QUERY_HEADS // KEY_VALUE_HEADS,
            HEAD_SIZE,
        ),
        cosine_table,
        sine_table,
        2,
    )
    key_rows = apply_rotary(
        reshaped_rows[..., query_total_width : query_total_width + key_columns_width].reshape(
            sequence_count, sequence_length, KEY_VALUE_HEADS, HEAD_SIZE
        ),
        cosine_table,
        sine_table,
        1,
    )
    value_rows = reshaped_rows[..., query_total_width + key_columns_width :].reshape(
        sequence_count, sequence_length, KEY_VALUE_HEADS, HEAD_SIZE
    )
    return (
        query_block.astype(jnp.bfloat16),
        key_rows.astype(jnp.bfloat16),
        value_rows.astype(jnp.bfloat16),
    )


def allowed_mask(segment):
    spots = jnp.arange(segment.shape[0])
    return (spots[:, None] >= spots[None, :]) & (segment[:, None] == segment[None, :])


def score_block(query_block, key_rows, segment):
    scores = jnp.einsum(
        "qhgd,khd->hgqk", query_block, key_rows, preferred_element_type=jnp.float32
    ) * query_block.shape[-1] ** (-0.5)
    return jnp.where(allowed_mask(segment)[None, None], scores, -1e30)


def attend(query_block, key_rows, value_rows, segment):
    scores = score_block(query_block, key_rows, segment)
    highest = jnp.max(scores, -1, keepdims=True)
    logsum = highest + jnp.log(jnp.sum(jnp.exp(scores - highest), -1, keepdims=True))
    probs = jnp.exp(scores - logsum).astype(jnp.bfloat16)
    attended = jnp.einsum("hgqk,khd->qhgd", probs, value_rows, preferred_element_type=jnp.float32)
    return (attended.astype(jnp.bfloat16), logsum)


def attend_back(query_block, key_rows, value_rows, segment, logsum, attended_gradient):
    factor = query_block.shape[-1] ** (-0.5)
    probs = jnp.exp(score_block(query_block, key_rows, segment) - logsum)
    grad_probs = jnp.einsum(
        "qhgd,khd->hgqk", attended_gradient, value_rows, preferred_element_type=jnp.float32
    )
    inner_sum = jnp.sum(probs * grad_probs, -1, keepdims=True)
    grad_scores = (probs * (grad_probs - inner_sum) * factor).astype(jnp.bfloat16)
    grad_values = jnp.einsum(
        "hgqk,qhgd->khd",
        probs.astype(jnp.bfloat16),
        attended_gradient,
        preferred_element_type=jnp.float32,
    )
    grad_query = jnp.einsum(
        "hgqk,khd->qhgd", grad_scores, key_rows, preferred_element_type=jnp.float32
    )
    grad_keys = jnp.einsum(
        "hgqk,qhgd->khd", grad_scores, query_block, preferred_element_type=jnp.float32
    )
    return (grad_query, grad_keys, grad_values)


def join_grads(grad_query, grad_keys, grad_values, cosine_table, sine_table):
    sequence_length = grad_query.shape[0]
    grad_query = apply_rotary(grad_query, cosine_table, -sine_table, 2).reshape(sequence_length, -1)
    grad_keys = apply_rotary(grad_keys, cosine_table, -sine_table, 1).reshape(sequence_length, -1)
    return jnp.concatenate(
        [grad_query, grad_keys, grad_values.reshape(sequence_length, -1)], -1
    ).astype(jnp.bfloat16)


def adam_step(weight, grad, first, second, step_rate, shrink):
    first = beta_one * first + (1.0 - beta_one) * grad
    second = beta_two * second + (1.0 - beta_two) * grad * grad
    update = first / correct_one / (jnp.sqrt(second / correct_two) + adam_eps)
    return (weight - step_rate * (update + shrink * weight), first, second)


NARROW = jnp.bfloat16
WIDE = jnp.float32
DISTANCE = (0, 1, -1, 2)
HOP_CORE, HOP_X, HOP_Y = 1, 2, 4


def swap(rows, pick):
    count = lax.axis_size("dp")
    return lax.ppermute(rows, "dp", [(i, i ^ pick(i)) for i in range(count)])


def first_hop(i):
    return HOP_X if i & 1 else HOP_Y


def second_hop(i):
    return HOP_Y if i & 1 else HOP_X


def swap_core(rows):
    return swap(rows, lambda i: HOP_CORE)


def swap_first(rows):
    return swap(rows, first_hop)


def swap_second(rows):
    return swap(rows, second_hop)


def turn(rows, step):
    count = lax.axis_size("expert")
    return lax.ppermute(rows, "expert", [(i, (i + step) % count) for i in range(count)])


def after(values, *others):
    return lax.optimization_barrier((values, others))[0]


def along_first(part):
    return jnp.concatenate([part, swap_first(part)], 0)


def gather_plane_last(block):
    ahead, behind = turn(block, 1), turn(block, -1)
    far = turn(ahead, 1)
    found = []
    for part in (block, ahead, behind, far):
        pair = jnp.concatenate([part, swap_first(part)], 0)
        found.append((pair, swap_second(pair)))
    return found, far


def gather_ring(block):
    pair = jnp.concatenate([block, swap_first(block)], 0)
    ahead, behind = turn(pair, 1), turn(pair, -1)
    return pair, ahead, behind, turn(ahead, 1)


def ring_sum(parts, gate=()):
    behind = turn(parts[2].astype(NARROW), 1)
    far = turn(parts[3].astype(NARROW), -1)
    ahead = turn((parts[1] + far.astype(WIDE)).astype(NARROW), -1)
    behind, ahead = after((behind, ahead), gate)
    return parts[0] + behind.astype(WIDE) + ahead.astype(WIDE)


def add_second(near, away, gate=()):
    return near + after(swap_second(away.astype(NARROW)), gate).astype(WIDE)


def add_first(rows, gate=()):
    half = rows.shape[0] // 2
    return rows[:half] + after(swap_first(rows[half:].astype(NARROW)), gate).astype(WIDE)


def gathered_sources(count_dp, count_expert):
    table = np.zeros((count_dp, count_expert, 4, 2, 2, 2), np.int32)
    for i in range(count_dp):
        for z in range(count_expert):
            for spot, distance in enumerate(DISTANCE):
                for second in range(2):
                    for first in range(2):
                        plane = i ^ (first_hop(i) * first) ^ (second_hop(i) * second)
                        table[i, z, spot, second, first] = plane, (z - distance) % count_expert
    return table.reshape(count_dp, count_expert, 16, 2)


def split_three(values):
    high = values.astype(NARROW)
    left = values - high.astype(WIDE)
    middle = left.astype(NARROW)
    return [high, middle, (left - middle.astype(WIDE)).astype(NARROW)]


def select_columns(values, chosen):
    rows = values.shape[0]
    parts = jnp.dot(
        jnp.concatenate(split_three(values), 0), chosen, preferred_element_type=jnp.float32
    )
    return parts[:rows] + parts[rows : 2 * rows] + parts[2 * rows :]


def parity_columns(rows, parity):
    count = rows.shape[0]
    query_total_width = QUERY_HEADS * HEAD_SIZE
    key_columns_width = KEY_VALUE_HEADS * HEAD_SIZE
    bounds = (
        (0, query_total_width),
        (query_total_width, query_total_width + key_columns_width),
        (query_total_width + key_columns_width, query_total_width + 2 * key_columns_width),
    )
    return jnp.concatenate(
        [
            rows[:, low:high].reshape(count, KEY_VALUE_HEADS // 2, 2, -1)[:, :, parity]
            .reshape(count, -1)
            for low, high in bounds
        ],
        1,
    )


def join_parities(even, odd):
    count = even.shape[0]
    query_half = QUERY_HEADS * HEAD_SIZE // 2
    key_half = KEY_VALUE_HEADS * HEAD_SIZE // 2
    bounds = (
        (0, query_half),
        (query_half, query_half + key_half),
        (query_half + key_half, query_half + 2 * key_half),
    )
    heads = KEY_VALUE_HEADS // 2
    return jnp.concatenate(
        [
            jnp.stack(
                [
                    even[:, low:high].reshape(count, heads, -1),
                    odd[:, low:high].reshape(count, heads, -1),
                ],
                2,
            ).reshape(count, -1)
            for low, high in bounds
        ],
        1,
    )


def split_head_group(projected_rows, cosine_table, sine_table):
    sequences, length = projected_rows.shape[:2]
    heads = KEY_VALUE_HEADS // 2
    group = QUERY_HEADS // KEY_VALUE_HEADS
    query_width = heads * group * HEAD_SIZE
    key_width = heads * HEAD_SIZE
    query_block = projected_rows[..., :query_width].reshape(
        sequences, length, heads, group, HEAD_SIZE
    )
    key_rows = projected_rows[..., query_width : query_width + key_width].reshape(
        sequences, length, heads, HEAD_SIZE
    )
    value_rows = projected_rows[..., query_width + key_width :].reshape(
        sequences, length, heads, HEAD_SIZE
    )
    query_block = jax.vmap(lambda a: apply_rotary(a, cosine_table, sine_table, 2))(query_block)
    key_rows = jax.vmap(lambda a: apply_rotary(a, cosine_table, sine_table, 1))(key_rows)
    return (
        query_block.astype(jnp.bfloat16),
        key_rows.astype(jnp.bfloat16),
        value_rows.astype(jnp.bfloat16),
    )


def spread_columns_kernel(weight_ref, out_ref):
    chips, _, _, lanes = out_ref.shape
    for chip in range(chips):
        for part in range(2):
            columns = slice(part * FF + chip * lanes, part * FF + (chip + 1) * lanes)
            out_ref[chip, part] = weight_ref[0, :, columns].astype(out_ref.dtype)


def spread_columns(weight, chips):
    experts, rows, both = weight.shape
    lanes = both // 2 // chips
    return pl.pallas_call(
        spread_columns_kernel,
        grid=(experts,),
        in_specs=[pl.BlockSpec((1, rows, both), lambda e: (e, 0, 0))],
        out_specs=pl.BlockSpec((chips, 2, rows, lanes), lambda e: (0, 0, 0, e)),
        out_shape=jax.ShapeDtypeStruct((chips, 2, rows, experts * lanes), jnp.bfloat16),
        cost_estimate=pl.CostEstimate(
            flops=0, bytes_accessed=6 * experts * rows * both, transcendentals=0
        ),
    )(weight)


def stack_rows_kernel(place_ref, mine_ref, theirs_ref, gate_ref, upper_ref, sems):
    core = place_ref[1]
    chips, _, rows, _ = mine_ref.shape
    copies = []
    for chip in range(chips):
        for mate, ref in enumerate((mine_ref, theirs_ref)):
            start = pl.multiple_of((chip * 2 + (core ^ mate)) * rows, rows)
            for part, out_ref in enumerate((gate_ref, upper_ref)):
                copies.append(
                    pltpu.make_async_copy(
                        ref.at[chip, part],
                        out_ref.at[pl.ds(start, rows), :],
                        sems.at[len(copies)],
                    )
                )
    for copy in copies:
        copy.start()
    for copy in copies:
        copy.wait()


def stack_rows(place, mine, theirs):
    chips, _, rows, columns = mine.shape
    shape = jax.ShapeDtypeStruct((2 * chips * rows, columns), jnp.bfloat16)
    return pl.pallas_call(
        stack_rows_kernel,
        in_specs=[pl.BlockSpec(memory_space=pltpu.SMEM)]
        + [pl.BlockSpec(memory_space=pltpu.VMEM)] * 2,
        out_specs=[pl.BlockSpec(memory_space=pl.ANY)] * 2,
        out_shape=[shape] * 2,
        scratch_shapes=[pltpu.SemaphoreType.DMA((4 * chips,))],
        cost_estimate=pl.CostEstimate(
            flops=0, bytes_accessed=16 * chips * rows * columns, transcendentals=0
        ),
    )(place, mine, theirs)


def stack_attention_kernel(*refs):
    blocks, (qkv_ref, gain_ref, out_ref, sems) = refs[:-4], refs[-4:]
    wide, lanes = qkv_ref.shape[1], gain_ref.shape[1]
    owned = out_ref.shape[0] // (2 * len(blocks))
    copies = []
    for i, block in enumerate(blocks):
        for j in range(2):
            top, spot = 3 * owned * j, 2 * i + j
            pairs = (
                (
                    block.at[pl.ds(top, 2 * owned), pl.ds(0, wide)],
                    qkv_ref.at[pl.ds(2 * owned * spot, 2 * owned), :],
                ),
                (
                    block.at[pl.ds(top, 2 * owned), pl.ds(wide, lanes)],
                    gain_ref.at[pl.ds(2 * owned * spot, 2 * owned), :],
                ),
                (
                    block.at[pl.ds(top + 2 * owned, owned), :],
                    out_ref.at[pl.ds(owned * spot, owned), :],
                ),
            )
            for source, target in pairs:
                copies.append(pltpu.make_async_copy(source, target, sems.at[len(copies)]))
    for copy in copies:
        copy.start()
    for copy in copies:
        copy.wait()


def stack_attention(blocks, wide, lanes):
    owned = blocks[0].shape[0] // 6
    count = 2 * len(blocks)
    b16 = lambda r, c: jax.ShapeDtypeStruct((r, c), jnp.bfloat16)
    return pl.pallas_call(
        stack_attention_kernel,
        in_specs=[pl.BlockSpec(memory_space=pltpu.VMEM)] * len(blocks),
        out_specs=[pl.BlockSpec(memory_space=pl.ANY)] * 3,
        out_shape=[
            b16(2 * owned * count, wide),
            b16(2 * owned * count, lanes),
            b16(owned * count, blocks[0].shape[1]),
        ],
        scratch_shapes=[pltpu.SemaphoreType.DMA((3 * count,))],
        cost_estimate=pl.CostEstimate(
            flops=0, bytes_accessed=4 * 3 * owned * count * MODEL_WIDTH, transcendentals=0
        ),
    )(*blocks)


def attention_grads_kernel(
    normed_ref, joined_ref, attended_ref, grads_ref, gain_ref, near_ref, away_ref
):
    contract = (((0,), (0,)), ((), ()))
    wide, lanes = joined_ref.shape[1], gain_ref.shape[1]
    spots = near_ref.shape[0]
    owned = near_ref.shape[1] // 6
    joined, grads = joined_ref[...], grads_ref[...]

    def place(spot, second, first, row, columns, values):
        rows = pl.ds(3 * owned * first + row, values.shape[0])
        if second:
            away_ref[spot, rows, columns] = values.astype(away_ref.dtype)
        else:
            near_ref[spot, rows, columns] = values

    for spot in range(spots):
        rows = 8 * owned
        qkv = lax.dot_general(
            normed_ref[:, rows * spot : rows * (spot + 1)],
            joined,
            contract,
            preferred_element_type=jnp.float32,
        )
        for i in range(4):
            part = slice(2 * owned * i, 2 * owned * (i + 1))
            place(spot, i // 2, i % 2, 0, pl.ds(0, wide), qkv[part])
            gain = gain_ref[pl.ds(rows * spot + 2 * owned * i, 2 * owned), :]
            place(spot, i // 2, i % 2, 0, pl.ds(wide, lanes), gain)
            place(spot, i // 2, i % 2, 0, pl.ds(wide + lanes, lanes), jnp.zeros_like(gain))
        if spot % 2 == 0:
            out = lax.dot_general(
                attended_ref[:, 4 * owned * spot : 4 * owned * (spot + 2)],
                grads,
                contract,
                preferred_element_type=jnp.float32,
            )
            for i in range(8):
                part = slice(owned * i, owned * (i + 1))
                place(
                    spot + i // 4,
                    i // 2 % 2,
                    i % 2,
                    2 * owned,
                    pl.ds(0, out.shape[1]),
                    out[part],
                )


def attention_grads(normed, joined, attended, grads, gain, owned):
    spots = len(DISTANCE)
    shape = (spots, 6 * owned, grads.shape[1])
    return pl.pallas_call(
        attention_grads_kernel,
        out_shape=[
            jax.ShapeDtypeStruct(shape, jnp.float32),
            jax.ShapeDtypeStruct(shape, jnp.bfloat16),
        ],
        compiler_params=pltpu.CompilerParams(vmem_limit_bytes=44 * 1024 * 1024),
        cost_estimate=pl.CostEstimate(
            flops=2 * normed.shape[0] * normed.shape[1] * (joined.shape[1] + grads.shape[1] // 2),
            bytes_accessed=20 * 1024 * 1024,
            transcendentals=0,
        ),
    )(normed, joined, attended, grads, gain)


def expert_kernel(place_ref, *refs, per_step, count):
    source_refs = refs[:count]
    given_ref, gate_ref, upper_ref, down_ref = refs[count : count + 4]
    back_refs = refs[-9 - count : -9]
    hidden_ref, grad_gate_ref, grad_upper_ref, rows_ref, grads_ref, narrow_ref = refs[-9:-3]
    route_ref, out_ref, back_ref = refs[-3:]
    step = pl.program_id(0)
    half, width = source_refs[0].shape

    @pl.when(step == 0)
    def _():
        for i, ref in enumerate(source_refs):
            rows_ref[half * i : half * (i + 1), :] = ref[...]
        grads_ref[...] = given_ref[:, :width]
        lanes = lax.broadcasted_iota(jnp.int32, route_ref.shape, 1)
        expert = (lanes + place_ref[2]).astype(jnp.float32)
        routes = given_ref[:, width:].astype(jnp.float32)
        weights = (
            routes[:, TOP : 2 * TOP]
            + routes[:, 2 * TOP : 3 * TOP]
            + routes[:, 3 * TOP : 4 * TOP]
        )
        dense = jnp.zeros_like(expert)
        for k in range(TOP):
            dense += jnp.where(expert == routes[:, k : k + 1], weights[:, k : k + 1], 0.0)
        route_ref[...] = dense
        out_ref[...] = jnp.zeros_like(out_ref)
        back_ref[...] = jnp.zeros_like(back_ref)

    rows = rows_ref[...]
    grads = grads_ref[...]
    contract_last = (((1,), (1,)), ((), ()))
    gate = jnp.dot(rows, gate_ref[...], preferred_element_type=jnp.float32)
    upper = jnp.dot(rows, upper_ref[...], preferred_element_type=jnp.float32)
    grad_hidden = lax.dot_general(
        grads, down_ref[...], contract_last, preferred_element_type=jnp.float32
    )
    route = route_ref[...]
    lanes = lax.broadcasted_iota(jnp.int32, route.shape, 1)
    columns = gate.shape[1] // per_step
    spread = []
    for i in range(per_step):
        one = jnp.sum(jnp.where(lanes == step * per_step + i, route, 0.0), 1, keepdims=True)
        spread.append(jnp.broadcast_to(one, (route.shape[0], columns)))
    weight = jnp.concatenate(spread, 1)
    sigma = 1.0 / (1.0 + jnp.exp(-gate))
    active = gate * sigma
    hidden = (weight * active * upper).astype(jnp.bfloat16)
    weighted = weight * grad_hidden
    grad_gate = (weighted * upper * sigma * (1.0 + gate * (1.0 - sigma))).astype(jnp.bfloat16)
    grad_upper = (weighted * active).astype(jnp.bfloat16)
    hidden_ref[...] = hidden
    grad_gate_ref[...] = grad_gate
    grad_upper_ref[...] = grad_upper
    out_ref[...] += jnp.dot(hidden, down_ref[...], preferred_element_type=jnp.float32)
    back_ref[...] += lax.dot_general(
        grad_gate, gate_ref[...], contract_last, preferred_element_type=jnp.float32
    ) + lax.dot_general(
        grad_upper, upper_ref[...], contract_last, preferred_element_type=jnp.float32
    )

    @pl.when(step == pl.num_programs(0) - 1)
    def _():
        narrow_ref[...] = out_ref[...].astype(jnp.bfloat16)
        for i, ref in enumerate(back_refs):
            ref[...] = back_ref[half * i : half * (i + 1), :].astype(ref.dtype)


def expert_block(place, spot, second, sources, given, weights, experts, filled):
    gate_w, upper_w, down_w = weights
    half, width = sources[0].shape
    wide = given.shape[1]
    total = gate_w.shape[1]
    per_step = 2
    steps = experts // per_step
    columns = total // steps
    count = len(sources)
    rows = half * count
    every = 2 * half * len(DISTANCE)
    at = (2 * spot + second) // count
    of = lambda p: p[3 + spot] * (2 // count) + second
    dtypes = (jnp.float32, jnp.bfloat16)[second : second + count]
    b16 = lambda r, c: jax.ShapeDtypeStruct((r, c), jnp.bfloat16)
    fixed = pl.BlockSpec((half, width), lambda i, p: (0, 0))
    part = pl.BlockSpec((rows, columns), lambda i, p: (at, i))
    kept = pl.BlockSpec((rows, width), lambda i, p: (at, 0))
    inputs = (place, *sources, given, gate_w, upper_w, down_w)
    return pl.pallas_call(
        functools.partial(expert_kernel, per_step=per_step, count=count),
        grid_spec=pltpu.PrefetchScalarGridSpec(
            num_scalar_prefetch=1,
            grid=(steps,),
            in_specs=[fixed] * count
            + [
                pl.BlockSpec((rows, wide), lambda i, p: (of(p), 0)),
                pl.BlockSpec((width, columns), lambda i, p: (0, i)),
                pl.BlockSpec((width, columns), lambda i, p: (0, i)),
                pl.BlockSpec((columns, width), lambda i, p: (i, 0)),
            ]
            + [pl.BlockSpec(memory_space=pl.ANY)] * len(filled),
            out_specs=[fixed] * count
            + [part] * 3
            + [kept] * 2
            + [pl.BlockSpec((rows, width), lambda i, p: (of(p), 0))],
            scratch_shapes=[
                pltpu.VMEM((rows, wide - width), jnp.float32),
                pltpu.VMEM((rows, width), jnp.float32),
                pltpu.VMEM((rows, width), jnp.float32),
            ],
        ),
        out_shape=[jax.ShapeDtypeStruct((half, width), dtype) for dtype in dtypes]
        + [b16(every, total)] * 3
        + [b16(every, width)] * 3,
        input_output_aliases={len(inputs) + i: count + i for i in range(len(filled))},
        compiler_params=pltpu.CompilerParams(vmem_limit_bytes=48 * 1024 * 1024),
        cost_estimate=pl.CostEstimate(
            flops=2 * rows * width * total * 6,
            bytes_accessed=2 * (3 * width * total + 3 * rows * total + 12 * rows * width),
            transcendentals=rows * total,
        ),
    )(*inputs, *filled)


def column_grads_kernel(
    place_ref, rows_ref, grad_gate_ref, grad_upper_ref, *refs
):
    keep_ref, give_ref, full_ref = refs[-3:]
    core = place_ref[1]
    contract = (((0,), (0,)), ((), ()))
    chips, _, plane_rows, _ = keep_ref.shape
    for part, ref in enumerate((grad_gate_ref, grad_upper_ref)):
        full_ref[...] = lax.dot_general(
            rows_ref[...], ref[...], contract, preferred_element_type=jnp.float32
        )
        for chip in range(chips):
            mine = pl.multiple_of((2 * chip + core) * plane_rows, plane_rows)
            theirs = pl.multiple_of((2 * chip + 1 - core) * plane_rows, plane_rows)
            keep_ref[chip, part] = full_ref[pl.ds(mine, plane_rows), :]
            give_ref[chip, part] = full_ref[pl.ds(theirs, plane_rows), :].astype(give_ref.dtype)


def column_grads(place, step, steps, rows_all, grad_gate, grad_upper, chips, filled):
    tokens, width = rows_all.shape
    total = grad_gate.shape[1]
    columns = total // steps
    plane_rows = width // (2 * chips)
    part = pl.BlockSpec((tokens, columns), lambda i, p: (0, step))
    wide = pl.BlockSpec((chips, 2, plane_rows, columns), lambda i, p: (0, 0, 0, step))
    shape = (chips, 2, plane_rows, total)
    return pl.pallas_call(
        column_grads_kernel,
        grid_spec=pltpu.PrefetchScalarGridSpec(
            num_scalar_prefetch=1,
            grid=(1,),
            in_specs=[pl.BlockSpec((tokens, width), lambda i, p: (0, 0)), part, part]
            + [pl.BlockSpec(memory_space=pl.ANY)] * len(filled),
            out_specs=[wide, wide],
            scratch_shapes=[pltpu.VMEM((width, columns), jnp.float32)],
        ),
        out_shape=[
            jax.ShapeDtypeStruct(shape, jnp.float32),
            jax.ShapeDtypeStruct(shape, jnp.bfloat16),
        ],
        input_output_aliases={4 + i: i for i in range(len(filled))},
        compiler_params=pltpu.CompilerParams(vmem_limit_bytes=56 * 1024 * 1024),
        cost_estimate=pl.CostEstimate(
            flops=4 * tokens * width * columns,
            bytes_accessed=2 * tokens * (width + 2 * columns) + 6 * 2 * width * columns,
            transcendentals=0,
        ),
    )(place, rows_all, grad_gate, grad_upper, *filled)


def down_grads_kernel(place_ref, grads_ref, hidden_ref, keep_ref, give_ref, full_ref):
    core = place_ref[1]
    full_ref[...] = lax.dot_general(
        hidden_ref[...],
        grads_ref[...],
        (((0,), (0,)), ((), ())),
        preferred_element_type=jnp.float32,
    )
    experts, down_rows, _ = keep_ref.shape
    for e in range(experts):
        mine = pl.multiple_of((2 * e + core) * down_rows, down_rows)
        theirs = pl.multiple_of((2 * e + 1 - core) * down_rows, down_rows)
        keep_ref[e] = full_ref[pl.ds(mine, down_rows), :]
        give_ref[e] = full_ref[pl.ds(theirs, down_rows), :]


def down_grads(place, steps, grads_all, hidden, experts):
    tokens, width = grads_all.shape
    total = hidden.shape[1]
    columns = total // steps
    per_step = experts // steps
    down_rows = total // experts // 2
    down = pl.BlockSpec((per_step, down_rows, width), lambda i, p: (i, 0, 0))
    return pl.pallas_call(
        down_grads_kernel,
        grid_spec=pltpu.PrefetchScalarGridSpec(
            num_scalar_prefetch=1,
            grid=(steps,),
            in_specs=[
                pl.BlockSpec((tokens, width), lambda i, p: (0, 0)),
                pl.BlockSpec((tokens, columns), lambda i, p: (0, i)),
            ],
            out_specs=[down, down],
            scratch_shapes=[pltpu.VMEM((columns, width), jnp.float32)],
        ),
        out_shape=[jax.ShapeDtypeStruct((experts, down_rows, width), jnp.float32)] * 2,
        compiler_params=pltpu.CompilerParams(vmem_limit_bytes=36 * 1024 * 1024),
        cost_estimate=pl.CostEstimate(
            flops=2 * tokens * width * total,
            bytes_accessed=2 * tokens * (width + total) + 4 * width * total,
            transcendentals=0,
        ),
    )(place, grads_all, hidden)


def adam_columns_kernel(w_ref, first_ref, second_ref, grad_ref, *outs):
    chips, _, _, lanes = grad_ref.shape
    for chip in range(chips):
        for part in range(2):
            columns = slice(part * FF + chip * lanes, part * FF + (chip + 1) * lanes)
            grad = grad_ref[chip, part].astype(jnp.float32)
            found = adam_step(
                w_ref[0, :, columns],
                grad,
                first_ref[0, :, columns],
                second_ref[0, :, columns],
                learn_rate,
                weight_decay,
            )
            for out_ref, value in zip(outs, (grad,) + found):
                out_ref[0, :, columns] = value


def adam_columns(weight, first, second, grads):
    experts, rows, both = weight.shape
    chips = grads.shape[0]
    lanes = grads.shape[3] // experts
    block = pl.BlockSpec((1, rows, both), lambda e: (e, 0, 0))
    return pl.pallas_call(
        adam_columns_kernel,
        grid=(experts,),
        in_specs=[block] * 3 + [pl.BlockSpec((chips, 2, rows, lanes), lambda e: (0, 0, 0, e))],
        out_specs=[block] * 4,
        out_shape=[jax.ShapeDtypeStruct(weight.shape, jnp.float32)] * 4,
        compiler_params=pltpu.CompilerParams(vmem_limit_bytes=56 * 1024 * 1024),
        cost_estimate=pl.CostEstimate(
            flops=20 * experts * rows * both,
            bytes_accessed=30 * experts * rows * both,
            transcendentals=experts * rows * both,
        ),
    )(weight, first, second, grads)


def shards_moved(
    tokens,
    cotangent,
    segments,
    expert_ids,
    route_weights,
    w_qkv,
    w_out,
    gains,
    w_gate_up,
    w_down,
    first_moment_projection,
    first_out,
    first_gains,
    first_gate_up,
    first_down,
    second_moment_projection,
    second_out,
    second_gains,
    second_gate_up,
    second_down,
):
    sequence_length = segments.shape[1]
    count_dp, count_expert = lax.axis_size("dp"), lax.axis_size("expert")
    place_dp, place_expert = lax.axis_index("dp"), lax.axis_index("expert")
    core = place_dp % 2
    chip = place_dp // 2
    chips = count_dp // 2
    local_experts = EXPERTS // count_expert
    owned = w_qkv.shape[0]
    half_columns = w_qkv.shape[1] // 2
    half_width = MODEL_WIDTH // 2
    lane_pad = 128

    narrow_qkv = w_qkv.astype(NARROW)
    even_columns, odd_columns = parity_columns(narrow_qkv, 0), parity_columns(narrow_qkv, 1)
    gain_columns = jnp.pad(gains.astype(NARROW).T, ((0, 0), (0, lane_pad - 2)))
    kept = jnp.where(core == 0, even_columns, odd_columns)
    given = jnp.where(core == 0, odd_columns, even_columns)
    rest = jnp.zeros((owned, MODEL_WIDTH - half_columns - lane_pad), NARROW)
    taken = swap_core(jnp.concatenate([given, gain_columns], 1))
    block = jnp.concatenate(
        [
            jnp.concatenate([kept, gain_columns, rest], 1),
            jnp.concatenate([taken, rest], 1),
            w_out.astype(NARROW),
        ],
        0,
    )
    share = local_experts * (FF // chips)
    ahead, behind = turn(block, 1), turn(block, -1)
    pieces = spread_columns(after(w_gate_up, taken), chips)
    attention_ring = [block, ahead, behind, turn(after(ahead, pieces), 1)]
    attention_pairs = [along_first(part) for part in attention_ring[:2]]
    routes = jnp.concatenate([expert_ids.astype(NARROW)] + split_three(route_weights), 1)
    cotangent_rows = jnp.concatenate(
        [
            cotangent.astype(NARROW),
            jnp.pad(routes, ((0, 0), (0, lane_pad - routes.shape[1]))),
        ],
        1,
    )
    cotangent_pair = along_first(cotangent_rows)
    cotangent_here = jnp.concatenate([cotangent_pair, swap_second(cotangent_pair)], 0)
    cotangent_all = lax.all_gather(
        after(cotangent_here, attention_ring), "expert", axis=0, tiled=True
    )
    attention_pairs.append(along_first(attention_ring[2]))
    attention_pairs.append(along_first(after(attention_ring[3], cotangent_here)))
    attention_blocks = [(pair, swap_second(pair)) for pair in attention_pairs]

    sources = jnp.asarray(gathered_sources(count_dp, count_expert))[place_dp, place_expert]
    from_dp, from_expert = sources[:, 0], sources[:, 1]
    row_in = jnp.arange(owned, dtype=jnp.int32)
    feature = (
        ((from_dp[:, None] ^ jnp.arange(2, dtype=jnp.int32)[None, :]) * count_expert
         + from_expert[:, None])[:, :, None] * owned + row_in
    ).reshape(-1)
    head_feature = (
        ((from_dp // 2 * count_expert + from_expert) * owned)[:, None] + row_in
    ).reshape(-1)
    places = jnp.arange(MODEL_WIDTH, dtype=jnp.int32)
    to_gathered = (places[:, None] == feature[None, :]).astype(NARROW)
    from_gathered = (feature[:, None] == places[None, :]).astype(NARROW)
    head_places = places[: half_width]
    heads_to_gathered = (head_places[:, None] == head_feature[None, :]).astype(NARROW)
    heads_from_gathered = (head_feature[:, None] == head_places[None, :]).astype(NARROW)

    found_at = (place_expert - jnp.asarray(DISTANCE, jnp.int32)) % count_expert
    place = jnp.concatenate(
        [jnp.stack([chip, core, place_expert * local_experts]).astype(jnp.int32), found_at]
    )
    parities = [list(range(i, count_dp, 2)) for i in range(2)]
    pieces = lax.all_to_all(
        pieces, "dp", 0, 0, axis_index_groups=parities, tiled=True
    )
    down_mine = after(w_down, attention_pairs[0]).astype(NARROW)
    down_theirs = swap_core(down_mine)
    down_w = jnp.where(
        core == 0,
        jnp.concatenate([down_mine, down_theirs], 1),
        jnp.concatenate([down_theirs, down_mine], 1),
    ).reshape(share, MODEL_WIDTH)
    attention_blocks = after(attention_blocks, (down_w, pieces))

    cosine_table, sine_table = rotary_tables(sequence_length, HEAD_SIZE // 2)
    inputs = tokens.astype(WIDE)
    pair_tokens = jnp.concatenate([tokens, swap_core(tokens)], 0)
    pair_segments = jnp.concatenate([segments, swap_core(segments)], 0)
    scale_pair = norm_scale(pair_tokens.astype(WIDE))
    scale_one = scale_pair[:sequence_length]
    pair_gathered = jnp.dot(pair_tokens, to_gathered, preferred_element_type=jnp.float32)
    blocks = [half for pair in attention_blocks for half in pair]
    qkv_here, gain_here, out_here = stack_attention(blocks, half_columns, lane_pad)
    gain_here = gain_here[:, :2].T
    gain_attn = gain_here[0].astype(WIDE)
    gains_placed = jnp.dot(gain_here, from_gathered, preferred_element_type=jnp.float32)
    gain_moe = gains_placed[1]
    normed_one = (pair_gathered * scale_pair * gain_attn).astype(NARROW)
    projected = jnp.dot(normed_one, qkv_here, preferred_element_type=jnp.float32)
    query_block, key_rows, value_rows = split_head_group(
        projected.reshape(2, sequence_length, -1), cosine_table, sine_table
    )
    attended, logsums = jax.vmap(attend)(query_block, key_rows, value_rows, pair_segments)
    attended = attended.reshape(2 * sequence_length, half_width)
    attended = jnp.dot(attended, heads_to_gathered, preferred_element_type=jnp.float32).astype(
        NARROW
    )
    resid_parts = jnp.dot(attended, out_here, preferred_element_type=jnp.float32)
    resid = inputs + resid_parts[:sequence_length] + swap_core(resid_parts[sequence_length:])
    scale_two = norm_scale(resid)
    normed_two = (resid * scale_two * gain_moe).astype(NARROW)
    normed_two = after(normed_two, pieces)

    normed_ring = [normed_two] + [turn(normed_two, distance) for distance in DISTANCE[1:]]
    gate_w, upper_w = stack_rows(place, pieces, after(swap_core(pieces), normed_two))
    back_parts, filled = [], []
    second_parts, begun = [], ()
    for spot, part in enumerate(normed_ring):
        near = along_first(after(part, begun))
        away = swap_second(near)
        if spot >= 2:
            near = after(near, (second_parts[spot - 2], back_parts[: spot - 2]))
        back = []
        for second, sources in ((0, [near]), (1, [away])) if spot < 2 else ((0, [near, away]),):
            done = expert_block(
                place,
                spot,
                second,
                sources,
                cotangent_all,
                (gate_w, upper_w, down_w),
                local_experts,
                filled,
            )
            back += done[: len(sources)]
            filled = done[len(sources) :]
            begun = begun or (back[0],)
        if spot < len(DISTANCE) - 1:
            second_parts.append(add_second(*back))
            back_parts.append(add_first(second_parts[-1]))
    hidden, grad_gate, grad_upper, rows_all, grads_all, out_all = filled
    steps = local_experts // 2
    kept_grads = []
    for step in range(steps):
        kept_grads = column_grads(
            place, step, steps, rows_all, grad_gate, grad_upper, chips, kept_grads
        )
        if step == 0:
            last = add_second(*back, kept_grads)
        elif step == 1:
            back_parts.append(add_first(last, kept_grads))
        elif step == 2:
            found = [
                turn(part.astype(NARROW), -distance)
                for part, distance in zip(back_parts[1:], DISTANCE[1:])
            ]
            grad_normed_two = back_parts[0] + sum(
                part.astype(WIDE) for part in after(found, kept_grads)
            )
            rows_all = after(rows_all, grad_normed_two)
    keep, give = kept_grads
    taken = swap_core(give)
    expert_sums = (keep + taken.astype(WIDE)).astype(NARROW)
    parities = [list(range(i, count_dp, 2)) for i in range(2)]
    collected = lax.all_to_all(
        expert_sums, "dp", 0, 0, axis_index_groups=parities, tiled=True
    )
    out_sums = lax.psum_scatter(
        after(out_all, grad_normed_two), "expert", scatter_dimension=0, tiled=True
    )

    hat_two = grad_normed_two * gain_moe
    grad_gain_moe = jnp.sum(grad_normed_two * resid * scale_two, 0)
    grad_resid = cotangent + scale_two * (
        hat_two - resid * scale_two**2 * jnp.mean(hat_two * resid, -1, keepdims=True)
    )
    grad_resid_half = grad_resid.astype(NARROW)
    pair_grads = jnp.concatenate([grad_resid_half, swap_core(grad_resid_half)], 0)
    attended_gradient = lax.dot_general(
        pair_grads, out_here, (((1,), (1,)), ((), ())), preferred_element_type=jnp.float32
    ).astype(NARROW)
    attended_gradient = (
        jnp.dot(attended_gradient, heads_from_gathered, preferred_element_type=jnp.float32)
        .astype(NARROW)
        .reshape(query_block.shape)
    )
    grad_query, grad_keys, grad_values = jax.vmap(attend_back)(
        query_block, key_rows, value_rows, pair_segments, logsums, attended_gradient
    )
    joined = jax.vmap(lambda a, b, c: join_grads(a, b, c, cosine_table, sine_table))(
        grad_query, grad_keys, grad_values
    ).reshape(2 * sequence_length, -1)
    joined = after(joined, expert_sums)
    grad_normed_parts = lax.dot_general(
        joined, qkv_here, (((1,), (1,)), ((), ())), preferred_element_type=jnp.float32
    )
    grad_gain_attn = jnp.sum(grad_normed_parts * pair_gathered * scale_pair, 0)
    gain_parts = jnp.stack(
        [grad_gain_attn, select_columns(grad_gain_moe[None], to_gathered)[0]], 1
    )
    near_parts, away_parts = attention_grads(
        normed_one,
        joined,
        attended,
        pair_grads,
        jnp.pad(gain_parts, ((0, 0), (0, lane_pad - 2))),
        owned,
    )
    keep_down, give_down = down_grads(
        place, steps, after(grads_all, near_parts), hidden, local_experts
    )
    part_down = keep_down + swap_core(give_down)
    new_down, new_first_down, new_second_down = adam_step(
        w_down, part_down, first_down, second_down, learn_rate, weight_decay
    )
    part_gate_up, new_gate_up, new_first_gate_up, new_second_gate_up = adam_columns(
        w_gate_up, first_gate_up, second_gate_up, after(collected, near_parts)
    )
    in_plane = [None] * len(DISTANCE)
    for i in (3, 1, 2, 0):
        in_plane[i] = add_second(near_parts[i], away_parts[i], new_gate_up)
    for i in (3, 1, 2, 0):
        in_plane[i] = add_first(in_plane[i])
    out_sums = after(out_sums, in_plane[3]).astype(WIDE)
    out_half = out_sums.shape[0] // 2
    out_sums = add_second(out_sums[:out_half], out_sums[out_half:])
    summed = ring_sum(in_plane, (new_down, out_sums))
    out_tokens = resid + add_first(out_sums, summed)
    here, there, part_out = summed[:owned], summed[owned : 2 * owned], summed[2 * owned :]
    there = swap_core(there[:, : half_columns + lane_pad])
    part_gains = (
        here[:, half_columns : half_columns + 2] + there[:, half_columns : half_columns + 2]
    ).T
    here, there = here[:, :half_columns], there[:, :half_columns]
    part_qkv = join_parities(
        jnp.where(core == 0, here, there), jnp.where(core == 0, there, here)
    )

    grad_normed_parts = select_columns(grad_normed_parts, from_gathered)
    grad_normed_one = grad_normed_parts[:sequence_length] + swap_core(
        grad_normed_parts[sequence_length:]
    )
    hat_one = grad_normed_one * gains_placed[0]
    grad_tokens = grad_resid + scale_one * (
        hat_one - inputs * scale_one**2 * jnp.mean(hat_one * inputs, -1, keepdims=True)
    )

    new_qkv, new_first_qkv, new_second_qkv = adam_step(
        w_qkv, part_qkv, first_moment_projection, second_moment_projection, learn_rate, weight_decay
    )
    new_out, new_first_out, new_second_out = adam_step(
        w_out, part_out, first_out, second_out, out_rate, weight_decay
    )
    new_gains, new_first_gains, new_second_gains = adam_step(
        gains, part_gains, first_gains, second_gains, gain_rate, 0.0
    )
    return (
        out_tokens,
        grad_tokens,
        part_qkv,
        part_out,
        part_gains,
        part_gate_up,
        part_down,
        new_qkv,
        new_out,
        new_gains,
        new_gate_up,
        new_down,
        new_first_qkv,
        new_first_out,
        new_first_gains,
        new_first_gate_up,
        new_first_down,
        new_second_qkv,
        new_second_out,
        new_second_gains,
        new_second_gate_up,
        new_second_down,
    )


def shards_plain(
    tokens,
    cotangent,
    segments,
    expert_ids,
    route_weights,
    w_qkv,
    w_out,
    gains,
    w_gate_up,
    w_down,
    first_moment_projection,
    first_out,
    first_gains,
    first_gate_up,
    first_down,
    second_moment_projection,
    second_out,
    second_gains,
    second_gate_up,
    second_down,
):
    sequence_count = segments.shape[0]
    sequence_length = segments.shape[1]
    groups_expert = lax.axis_size("expert")
    local_experts = EXPERTS // groups_expert
    slot_rows = groups_expert * CAP
    qkv_full, out_full, gain_full = (
        lax.all_gather(w_qkv.astype(jnp.bfloat16), ("dp", "expert"), axis=0, tiled=True),
        lax.all_gather(w_out.astype(jnp.bfloat16), ("dp", "expert"), axis=0, tiled=True),
        lax.all_gather(gains.astype(jnp.bfloat16), ("dp", "expert"), axis=1, tiled=True),
    )
    gate_up_full, down_full = (
        lax.all_gather(w_gate_up.astype(jnp.bfloat16), "dp", axis=1, tiled=True),
        lax.all_gather(w_down.astype(jnp.bfloat16), "dp", axis=1, tiled=True),
    )
    gain_attn = gain_full[0].astype(jnp.float32)
    gain_moe = gain_full[1].astype(jnp.float32)
    cosine_table, sine_table = rotary_tables(sequence_length, HEAD_SIZE // 2)
    inputs = tokens.astype(jnp.float32)
    scale_one = norm_scale(inputs)
    normed_one = (inputs * scale_one * gain_attn).astype(jnp.bfloat16)
    projected_rows = jnp.dot(normed_one, qkv_full, preferred_element_type=jnp.float32)
    query_block, key_rows, value_rows = split_heads(
        projected_rows, sequence_count, sequence_length, cosine_table, sine_table
    )
    index = 0
    attended_seq, logsum = attend(
        query_block[index], key_rows[index], value_rows[index], segments[index]
    )
    pieces = attended_seq.reshape(sequence_length, QUERY_HEADS * HEAD_SIZE)
    logsums = [logsum]
    resid = inputs + jnp.dot(pieces, out_full, preferred_element_type=jnp.float32)
    scale_two = norm_scale(resid)
    normed_two = (resid * scale_two * gain_moe).astype(jnp.bfloat16)
    flat_ids = expert_ids.reshape(-1)
    pair_count = flat_ids.shape[0]
    one_hot = (flat_ids[:, None] == jnp.arange(EXPERTS, dtype=jnp.int32)[None, :]).astype(jnp.int32)
    ranking = jnp.sum(jnp.cumsum(one_hot, 0) * one_hot, 1) - 1
    target = flat_ids * CAP + ranking
    owners = (
        jnp.full((EXPERTS * CAP,), -1, jnp.int32)
        .at[target]
        .set(jnp.arange(pair_count, dtype=jnp.int32))
    )
    filled = (owners >= 0)[:, None]
    safe_owner = jnp.maximum(owners, 0)
    send_rows = jnp.where(filled, normed_two[safe_owner // TOP], jnp.zeros((), jnp.bfloat16))
    received = lax.all_to_all(
        send_rows.reshape(groups_expert, local_experts, CAP, MODEL_WIDTH),
        "expert",
        split_axis=0,
        concat_axis=2,
        tiled=True,
    )
    received = received.reshape(local_experts, slot_rows, MODEL_WIDTH)
    mixed = jnp.einsum("erd,edf->erf", received, gate_up_full, preferred_element_type=jnp.float32)
    gate = mixed[..., :FF]
    upper = mixed[..., FF:]
    hidden = (jax.nn.silu(gate) * upper).astype(jnp.bfloat16)
    expert_out = jnp.einsum(
        "erf,efd->erd", hidden, down_full, preferred_element_type=jnp.float32
    ).astype(jnp.bfloat16)
    returned = lax.all_to_all(
        expert_out.reshape(1, local_experts, slot_rows, MODEL_WIDTH),
        "expert",
        split_axis=2,
        concat_axis=0,
        tiled=True,
    )
    picked = returned.reshape(EXPERTS * CAP, MODEL_WIDTH)[target].reshape(-1, TOP, MODEL_WIDTH)
    out_tokens = resid + jnp.sum(route_weights[..., None] * picked.astype(jnp.float32), 1)
    gate_up_back, down_back = (
        lax.all_gather(w_gate_up.astype(jnp.bfloat16), "dp", axis=1, tiled=True),
        lax.all_gather(w_down.astype(jnp.bfloat16), "dp", axis=1, tiled=True),
    )
    grad_routed = (
        (route_weights[..., None] * cotangent[:, None, :])
        .astype(jnp.bfloat16)
        .reshape(pair_count, MODEL_WIDTH)
    )
    send_grads = jnp.where(filled, grad_routed[safe_owner], jnp.zeros((), jnp.bfloat16))
    grad_expert = lax.all_to_all(
        send_grads.reshape(groups_expert, local_experts, CAP, MODEL_WIDTH),
        "expert",
        split_axis=0,
        concat_axis=2,
        tiled=True,
    )
    grad_expert = grad_expert.reshape(local_experts, slot_rows, MODEL_WIDTH)
    grad_hidden = jnp.einsum(
        "erd,efd->erf", grad_expert, down_back, preferred_element_type=jnp.float32
    )
    grad_down = jnp.einsum("erf,erd->efd", hidden, grad_expert, preferred_element_type=jnp.float32)
    sigma = jax.nn.sigmoid(gate)
    grad_mixed = jnp.concatenate(
        [grad_hidden * upper * sigma * (1.0 + gate * (1.0 - sigma)), grad_hidden * gate * sigma], -1
    ).astype(jnp.bfloat16)
    grad_gate_up = jnp.einsum(
        "erd,erf->edf", received, grad_mixed, preferred_element_type=jnp.float32
    )
    grad_received = jnp.einsum(
        "erf,edf->erd", grad_mixed, gate_up_back, preferred_element_type=jnp.float32
    ).astype(jnp.bfloat16)
    grad_back = lax.all_to_all(
        grad_received.reshape(1, local_experts, slot_rows, MODEL_WIDTH),
        "expert",
        split_axis=2,
        concat_axis=0,
        tiled=True,
    )
    grad_normed_two = jnp.sum(
        grad_back.reshape(EXPERTS * CAP, MODEL_WIDTH)[target]
        .reshape(-1, TOP, MODEL_WIDTH)
        .astype(jnp.float32),
        1,
    )
    hat_two = grad_normed_two * gain_moe
    grad_gain_moe = jnp.sum(grad_normed_two * resid * scale_two, 0)
    grad_resid = cotangent + scale_two * (
        hat_two - resid * scale_two**2 * jnp.mean(hat_two * resid, -1, keepdims=True)
    )
    grad_resid_half = grad_resid.astype(jnp.bfloat16)
    qkv_back, out_back = (
        lax.all_gather(w_qkv.astype(jnp.bfloat16), ("dp", "expert"), axis=0, tiled=True),
        lax.all_gather(w_out.astype(jnp.bfloat16), ("dp", "expert"), axis=0, tiled=True),
    )
    grad_out = jnp.dot(pieces.T, grad_resid_half, preferred_element_type=jnp.float32)
    attended_gradient = jnp.dot(
        grad_resid_half, out_back.T, preferred_element_type=jnp.float32
    ).astype(jnp.bfloat16)
    attended_gradient = attended_gradient.reshape(
        sequence_count, sequence_length, KEY_VALUE_HEADS, QUERY_HEADS // KEY_VALUE_HEADS, HEAD_SIZE
    )
    index = 0
    grad_query, grad_keys, grad_values = attend_back(
        query_block[index],
        key_rows[index],
        value_rows[index],
        segments[index],
        logsums[index],
        attended_gradient[index],
    )
    joined = join_grads(grad_query, grad_keys, grad_values, cosine_table, sine_table)
    grad_qkv = jnp.dot(normed_one.T, joined, preferred_element_type=jnp.float32)
    grad_normed_one = jnp.dot(joined, qkv_back.T, preferred_element_type=jnp.float32)
    hat_one = grad_normed_one * gain_attn
    grad_gain_attn = jnp.sum(grad_normed_one * inputs * scale_one, 0)
    grad_tokens = grad_resid + scale_one * (
        hat_one - inputs * scale_one**2 * jnp.mean(hat_one * inputs, -1, keepdims=True)
    )
    grad_gains = jnp.stack([grad_gain_attn, grad_gain_moe])
    part_qkv, part_out, part_gains = (
        lax.psum_scatter(grad_qkv, ("dp", "expert"), scatter_dimension=0, tiled=True),
        lax.psum_scatter(grad_out, ("dp", "expert"), scatter_dimension=0, tiled=True),
        lax.psum_scatter(grad_gains, ("dp", "expert"), scatter_dimension=1, tiled=True),
    )
    part_gate_up, part_down = (
        lax.psum_scatter(grad_gate_up, "dp", scatter_dimension=1, tiled=True),
        lax.psum_scatter(grad_down, "dp", scatter_dimension=1, tiled=True),
    )
    new_qkv, new_first_qkv, new_second_qkv = adam_step(
        w_qkv, part_qkv, first_moment_projection, second_moment_projection, learn_rate, weight_decay
    )
    new_out, new_first_out, new_second_out = adam_step(
        w_out, part_out, first_out, second_out, out_rate, weight_decay
    )
    new_gains, new_first_gains, new_second_gains = adam_step(
        gains, part_gains, first_gains, second_gains, gain_rate, 0.0
    )
    new_gate_up, new_first_gate_up, new_second_gate_up = adam_step(
        w_gate_up, part_gate_up, first_gate_up, second_gate_up, learn_rate, weight_decay
    )
    new_down, new_first_down, new_second_down = adam_step(
        w_down, part_down, first_down, second_down, learn_rate, weight_decay
    )
    return (
        out_tokens,
        grad_tokens,
        part_qkv,
        part_out,
        part_gains,
        part_gate_up,
        part_down,
        new_qkv,
        new_out,
        new_gains,
        new_gate_up,
        new_down,
        new_first_qkv,
        new_first_out,
        new_first_gains,
        new_first_gate_up,
        new_first_down,
        new_second_qkv,
        new_second_out,
        new_second_gains,
        new_second_gate_up,
        new_second_down,
    )


def solution(mesh):
    by_heads = mesh.shape["dp"] == KEY_VALUE_HEADS and mesh.shape["expert"] == 4
    return jax.shard_map(
        shards_moved if by_heads else shards_plain,
        mesh=mesh,
        in_specs=(
            P(("dp", "expert"), None),
            P(("dp", "expert"), None),
            P(("dp", "expert"), None),
            P(("dp", "expert"), None),
            P(("dp", "expert"), None),
            P(("dp", "expert"), None),
            P(("dp", "expert"), None),
            P(None, ("dp", "expert")),
            P("expert", "dp", None),
            P("expert", "dp", None),
            P(("dp", "expert"), None),
            P(("dp", "expert"), None),
            P(None, ("dp", "expert")),
            P("expert", "dp", None),
            P("expert", "dp", None),
            P(("dp", "expert"), None),
            P(("dp", "expert"), None),
            P(None, ("dp", "expert")),
            P("expert", "dp", None),
            P("expert", "dp", None),
        ),
        out_specs=(
            P(("dp", "expert"), None),
            P(("dp", "expert"), None),
            P(("dp", "expert"), None),
            P(("dp", "expert"), None),
            P(None, ("dp", "expert")),
            P("expert", "dp", None),
            P("expert", "dp", None),
            P(("dp", "expert"), None),
            P(("dp", "expert"), None),
            P(None, ("dp", "expert")),
            P("expert", "dp", None),
            P("expert", "dp", None),
            P(("dp", "expert"), None),
            P(("dp", "expert"), None),
            P(None, ("dp", "expert")),
            P("expert", "dp", None),
            P("expert", "dp", None),
            P(("dp", "expert"), None),
            P(("dp", "expert"), None),
            P(None, ("dp", "expert")),
            P("expert", "dp", None),
            P("expert", "dp", None),
        ),
        check_vma=False,
    )
```

```python
import functools

import jax
import jax.numpy as jnp
import numpy as np
from jax import lax
from jax.experimental import pallas as pl
from jax.experimental.pallas import tpu as pltpu
from jax.sharding import PartitionSpec as P

MODEL_WIDTH = 1536
QUERY_HEADS = 24
KEY_VALUE_HEADS = 8
HEAD_SIZE = 64
FF = 512
EXPERTS = 40
TOP = 8
CAP = 32


eps_norm = 1e-05
beta_one = 0.9
beta_two = 0.95
adam_eps = 1e-08
learn_rate = 0.01
out_rate = 0.04
gain_rate = 0.2
weight_decay = 0.1
correct_one = 1.0 - beta_one**3
correct_two = 1.0 - beta_two**3


def norm_scale(rows):
    return lax.rsqrt(jnp.mean(rows * rows, -1, keepdims=True) + eps_norm)


def rotary_tables(sequence_length, half_dim):
    position = jnp.arange(sequence_length, dtype=jnp.float32)[:, None]
    frequency = 10000.0 ** (-jnp.arange(half_dim, dtype=jnp.float32) / half_dim)
    angles = position * frequency[None, :]
    return (jnp.cos(angles), jnp.sin(angles))


def apply_rotary(value_rows, cosine_table, sine_table, middle):
    half_dim = value_rows.shape[-1] // 2
    shape = (cosine_table.shape[0],) + (1,) * middle + (half_dim,)
    cosine_table = cosine_table.reshape(shape)
    sine_table = sine_table.reshape(shape)
    first = value_rows[..., :half_dim]
    second = value_rows[..., half_dim:]
    return jnp.concatenate(
        [first * cosine_table - second * sine_table, second * cosine_table + first * sine_table], -1
    )


def split_heads(projected_rows, sequence_count, sequence_length, cosine_table, sine_table):
    query_total_width = QUERY_HEADS * HEAD_SIZE
    key_columns_width = KEY_VALUE_HEADS * HEAD_SIZE
    reshaped_rows = projected_rows.reshape(sequence_count, sequence_length, -1)
    query_block = apply_rotary(
        reshaped_rows[..., :query_total_width].reshape(
            sequence_count,
            sequence_length,
            KEY_VALUE_HEADS,
            QUERY_HEADS // KEY_VALUE_HEADS,
            HEAD_SIZE,
        ),
        cosine_table,
        sine_table,
        2,
    )
    key_rows = apply_rotary(
        reshaped_rows[..., query_total_width : query_total_width + key_columns_width].reshape(
            sequence_count, sequence_length, KEY_VALUE_HEADS, HEAD_SIZE
        ),
        cosine_table,
        sine_table,
        1,
    )
    value_rows = reshaped_rows[..., query_total_width + key_columns_width :].reshape(
        sequence_count, sequence_length, KEY_VALUE_HEADS, HEAD_SIZE
    )
    return (
        query_block.astype(jnp.bfloat16),
        key_rows.astype(jnp.bfloat16),
        value_rows.astype(jnp.bfloat16),
    )


def allowed_mask(segment):
    spots = jnp.arange(segment.shape[0])
    return (spots[:, None] >= spots[None, :]) & (segment[:, None] == segment[None, :])


def score_block(query_block, key_rows, segment):
    scores = jnp.einsum(
        "qhgd,khd->hgqk", query_block, key_rows, preferred_element_type=jnp.float32
    ) * query_block.shape[-1] ** (-0.5)
    return jnp.where(allowed_mask(segment)[None, None], scores, -1e30)


def attend(query_block, key_rows, value_rows, segment):
    scores = score_block(query_block, key_rows, segment)
    highest = jnp.max(scores, -1, keepdims=True)
    logsum = highest + jnp.log(jnp.sum(jnp.exp(scores - highest), -1, keepdims=True))
    probs = jnp.exp(scores - logsum).astype(jnp.bfloat16)
    attended = jnp.einsum("hgqk,khd->qhgd", probs, value_rows, preferred_element_type=jnp.float32)
    return (attended.astype(jnp.bfloat16), logsum)


def attend_back(query_block, key_rows, value_rows, segment, logsum, attended_gradient):
    factor = query_block.shape[-1] ** (-0.5)
    probs = jnp.exp(score_block(query_block, key_rows, segment) - logsum)
    grad_probs = jnp.einsum(
        "qhgd,khd->hgqk", attended_gradient, value_rows, preferred_element_type=jnp.float32
    )
    inner_sum = jnp.sum(probs * grad_probs, -1, keepdims=True)
    grad_scores = (probs * (grad_probs - inner_sum) * factor).astype(jnp.bfloat16)
    grad_values = jnp.einsum(
        "hgqk,qhgd->khd",
        probs.astype(jnp.bfloat16),
        attended_gradient,
        preferred_element_type=jnp.float32,
    )
    grad_query = jnp.einsum(
        "hgqk,khd->qhgd", grad_scores, key_rows, preferred_element_type=jnp.float32
    )
    grad_keys = jnp.einsum(
        "hgqk,qhgd->khd", grad_scores, query_block, preferred_element_type=jnp.float32
    )
    return (grad_query, grad_keys, grad_values)


def join_grads(grad_query, grad_keys, grad_values, cosine_table, sine_table):
    sequence_length = grad_query.shape[0]
    grad_query = apply_rotary(grad_query, cosine_table, -sine_table, 2).reshape(sequence_length, -1)
    grad_keys = apply_rotary(grad_keys, cosine_table, -sine_table, 1).reshape(sequence_length, -1)
    return jnp.concatenate(
        [grad_query, grad_keys, grad_values.reshape(sequence_length, -1)], -1
    ).astype(jnp.bfloat16)


def adam_step(weight, grad, first, second, step_rate, shrink):
    first = beta_one * first + (1.0 - beta_one) * grad
    second = beta_two * second + (1.0 - beta_two) * grad * grad
    update = first / correct_one / (jnp.sqrt(second / correct_two) + adam_eps)
    return (weight - step_rate * (update + shrink * weight), first, second)


NARROW = jnp.bfloat16
WIDE = jnp.float32
DISTANCE = (0, 1, -1, 2)
HOP_CORE, HOP_X, HOP_Y = 1, 2, 4


def swap(rows, pick):
    count = lax.axis_size("dp")
    return lax.ppermute(rows, "dp", [(i, i ^ pick(i)) for i in range(count)])


def first_hop(i):
    return HOP_X if i & 1 else HOP_Y


def second_hop(i):
    return HOP_Y if i & 1 else HOP_X


def swap_core(rows):
    return swap(rows, lambda i: HOP_CORE)


def swap_first(rows):
    return swap(rows, first_hop)


def swap_second(rows):
    return swap(rows, second_hop)


def turn(rows, step):
    count = lax.axis_size("expert")
    return lax.ppermute(rows, "expert", [(i, (i + step) % count) for i in range(count)])


def after(values, *others):
    return lax.optimization_barrier((values, others))[0]


def along_first(part):
    return jnp.concatenate([part, swap_first(part)], 0)


def gather_plane_last(block):
    ahead, behind = turn(block, 1), turn(block, -1)
    far = turn(ahead, 1)
    found = []
    for part in (block, ahead, behind, far):
        pair = jnp.concatenate([part, swap_first(part)], 0)
        found.append((pair, swap_second(pair)))
    return found, far


def gather_ring(block):
    pair = jnp.concatenate([block, swap_first(block)], 0)
    ahead, behind = turn(pair, 1), turn(pair, -1)
    return pair, ahead, behind, turn(ahead, 1)


def ring_sum(parts, gate=()):
    behind = turn(parts[2].astype(NARROW), 1)
    far = turn(parts[3].astype(NARROW), -1)
    ahead = turn((parts[1] + far.astype(WIDE)).astype(NARROW), -1)
    behind, ahead = after((behind, ahead), gate)
    return parts[0] + behind.astype(WIDE) + ahead.astype(WIDE)


def add_second(near, away, gate=()):
    return near + after(swap_second(away.astype(NARROW)), gate).astype(WIDE)


def add_first(rows, gate=()):
    half = rows.shape[0] // 2
    return rows[:half] + after(swap_first(rows[half:].astype(NARROW)), gate).astype(WIDE)


def gathered_sources(count_dp, count_expert):
    table = np.zeros((count_dp, count_expert, 4, 2, 2, 2), np.int32)
    for i in range(count_dp):
        for z in range(count_expert):
            for spot, distance in enumerate(DISTANCE):
                for second in range(2):
                    for first in range(2):
                        plane = i ^ (first_hop(i) * first) ^ (second_hop(i) * second)
                        table[i, z, spot, second, first] = plane, (z - distance) % count_expert
    return table.reshape(count_dp, count_expert, 16, 2)


def split_three(values):
    high = values.astype(NARROW)
    left = values - high.astype(WIDE)
    middle = left.astype(NARROW)
    return [high, middle, (left - middle.astype(WIDE)).astype(NARROW)]


def select_columns(values, chosen):
    rows = values.shape[0]
    parts = jnp.dot(
        jnp.concatenate(split_three(values), 0), chosen, preferred_element_type=jnp.float32
    )
    return parts[:rows] + parts[rows : 2 * rows] + parts[2 * rows :]


def parity_columns(rows, parity):
    count = rows.shape[0]
    query_total_width = QUERY_HEADS * HEAD_SIZE
    key_columns_width = KEY_VALUE_HEADS * HEAD_SIZE
    bounds = (
        (0, query_total_width),
        (query_total_width, query_total_width + key_columns_width),
        (query_total_width + key_columns_width, query_total_width + 2 * key_columns_width),
    )
    return jnp.concatenate(
        [
            rows[:, low:high].reshape(count, KEY_VALUE_HEADS // 2, 2, -1)[:, :, parity]
            .reshape(count, -1)
            for low, high in bounds
        ],
        1,
    )


def join_parities(even, odd):
    count = even.shape[0]
    query_half = QUERY_HEADS * HEAD_SIZE // 2
    key_half = KEY_VALUE_HEADS * HEAD_SIZE // 2
    bounds = (
        (0, query_half),
        (query_half, query_half + key_half),
        (query_half + key_half, query_half + 2 * key_half),
    )
    heads = KEY_VALUE_HEADS // 2
    return jnp.concatenate(
        [
            jnp.stack(
                [
                    even[:, low:high].reshape(count, heads, -1),
                    odd[:, low:high].reshape(count, heads, -1),
                ],
                2,
            ).reshape(count, -1)
            for low, high in bounds
        ],
        1,
    )


def split_head_group(projected_rows, cosine_table, sine_table):
    sequences, length = projected_rows.shape[:2]
    heads = KEY_VALUE_HEADS // 2
    group = QUERY_HEADS // KEY_VALUE_HEADS
    query_width = heads * group * HEAD_SIZE
    key_width = heads * HEAD_SIZE
    query_block = projected_rows[..., :query_width].reshape(
        sequences, length, heads, group, HEAD_SIZE
    )
    key_rows = projected_rows[..., query_width : query_width + key_width].reshape(
        sequences, length, heads, HEAD_SIZE
    )
    value_rows = projected_rows[..., query_width + key_width :].reshape(
        sequences, length, heads, HEAD_SIZE
    )
    query_block = jax.vmap(lambda a: apply_rotary(a, cosine_table, sine_table, 2))(query_block)
    key_rows = jax.vmap(lambda a: apply_rotary(a, cosine_table, sine_table, 1))(key_rows)
    return (
        query_block.astype(jnp.bfloat16),
        key_rows.astype(jnp.bfloat16),
        value_rows.astype(jnp.bfloat16),
    )


def spread_columns_kernel(weight_ref, out_ref):
    chips, _, _, lanes = out_ref.shape
    for chip in range(chips):
        for part in range(2):
            columns = slice(part * FF + chip * lanes, part * FF + (chip + 1) * lanes)
            out_ref[chip, part] = weight_ref[0, :, columns].astype(out_ref.dtype)


def spread_columns(weight, chips):
    experts, rows, both = weight.shape
    lanes = both // 2 // chips
    return pl.pallas_call(
        spread_columns_kernel,
        grid=(experts,),
        in_specs=[pl.BlockSpec((1, rows, both), lambda e: (e, 0, 0))],
        out_specs=pl.BlockSpec((chips, 2, rows, lanes), lambda e: (0, 0, 0, e)),
        out_shape=jax.ShapeDtypeStruct((chips, 2, rows, experts * lanes), jnp.bfloat16),
        cost_estimate=pl.CostEstimate(
            flops=0, bytes_accessed=6 * experts * rows * both, transcendentals=0
        ),
    )(weight)


def stack_rows_kernel(place_ref, mine_ref, theirs_ref, gate_ref, upper_ref, sems):
    core = place_ref[1]
    chips, _, rows, _ = mine_ref.shape
    copies = []
    for chip in range(chips):
        for mate, ref in enumerate((mine_ref, theirs_ref)):
            start = pl.multiple_of((chip * 2 + (core ^ mate)) * rows, rows)
            for part, out_ref in enumerate((gate_ref, upper_ref)):
                copies.append(
                    pltpu.make_async_copy(
                        ref.at[chip, part],
                        out_ref.at[pl.ds(start, rows), :],
                        sems.at[len(copies)],
                    )
                )
    for copy in copies:
        copy.start()
    for copy in copies:
        copy.wait()


def stack_rows(place, mine, theirs):
    chips, _, rows, columns = mine.shape
    shape = jax.ShapeDtypeStruct((2 * chips * rows, columns), jnp.bfloat16)
    return pl.pallas_call(
        stack_rows_kernel,
        in_specs=[pl.BlockSpec(memory_space=pltpu.SMEM)]
        + [pl.BlockSpec(memory_space=pltpu.VMEM)] * 2,
        out_specs=[pl.BlockSpec(memory_space=pl.ANY)] * 2,
        out_shape=[shape] * 2,
        scratch_shapes=[pltpu.SemaphoreType.DMA((4 * chips,))],
        cost_estimate=pl.CostEstimate(
            flops=0, bytes_accessed=16 * chips * rows * columns, transcendentals=0
        ),
    )(place, mine, theirs)


def stack_attention_kernel(*refs):
    blocks, (qkv_ref, gain_ref, out_ref, sems) = refs[:-4], refs[-4:]
    wide, lanes = qkv_ref.shape[1], gain_ref.shape[1]
    owned = out_ref.shape[0] // (2 * len(blocks))
    copies = []
    for i, block in enumerate(blocks):
        for j in range(2):
            top, spot = 3 * owned * j, 2 * i + j
            pairs = (
                (
                    block.at[pl.ds(top, 2 * owned), pl.ds(0, wide)],
                    qkv_ref.at[pl.ds(2 * owned * spot, 2 * owned), :],
                ),
                (
                    block.at[pl.ds(top, 2 * owned), pl.ds(wide, lanes)],
                    gain_ref.at[pl.ds(2 * owned * spot, 2 * owned), :],
                ),
                (
                    block.at[pl.ds(top + 2 * owned, owned), :],
                    out_ref.at[pl.ds(owned * spot, owned), :],
                ),
            )
            for source, target in pairs:
                copies.append(pltpu.make_async_copy(source, target, sems.at[len(copies)]))
    for copy in copies:
        copy.start()
    for copy in copies:
        copy.wait()


def stack_attention(blocks, wide, lanes):
    owned = blocks[0].shape[0] // 6
    count = 2 * len(blocks)
    b16 = lambda r, c: jax.ShapeDtypeStruct((r, c), jnp.bfloat16)
    return pl.pallas_call(
        stack_attention_kernel,
        in_specs=[pl.BlockSpec(memory_space=pltpu.VMEM)] * len(blocks),
        out_specs=[pl.BlockSpec(memory_space=pl.ANY)] * 3,
        out_shape=[
            b16(2 * owned * count, wide),
            b16(2 * owned * count, lanes),
            b16(owned * count, blocks[0].shape[1]),
        ],
        scratch_shapes=[pltpu.SemaphoreType.DMA((3 * count,))],
        cost_estimate=pl.CostEstimate(
            flops=0, bytes_accessed=4 * 3 * owned * count * MODEL_WIDTH, transcendentals=0
        ),
    )(*blocks)


def attention_grads_kernel(
    normed_ref, joined_ref, attended_ref, grads_ref, gain_ref, near_ref, away_ref
):
    contract = (((0,), (0,)), ((), ()))
    wide, lanes = joined_ref.shape[1], gain_ref.shape[1]
    spots = near_ref.shape[0]
    owned = near_ref.shape[1] // 6
    joined, grads = joined_ref[...], grads_ref[...]

    def place(spot, second, first, row, columns, values):
        rows = pl.ds(3 * owned * first + row, values.shape[0])
        if second:
            away_ref[spot, rows, columns] = values.astype(away_ref.dtype)
        else:
            near_ref[spot, rows, columns] = values

    for spot in range(spots):
        rows = 8 * owned
        qkv = lax.dot_general(
            normed_ref[:, rows * spot : rows * (spot + 1)],
            joined,
            contract,
            preferred_element_type=jnp.float32,
        )
        for i in range(4):
            part = slice(2 * owned * i, 2 * owned * (i + 1))
            place(spot, i // 2, i % 2, 0, pl.ds(0, wide), qkv[part])
            gain = gain_ref[pl.ds(rows * spot + 2 * owned * i, 2 * owned), :]
            place(spot, i // 2, i % 2, 0, pl.ds(wide, lanes), gain)
            place(spot, i // 2, i % 2, 0, pl.ds(wide + lanes, lanes), jnp.zeros_like(gain))
        if spot % 2 == 0:
            out = lax.dot_general(
                attended_ref[:, 4 * owned * spot : 4 * owned * (spot + 2)],
                grads,
                contract,
                preferred_element_type=jnp.float32,
            )
            for i in range(8):
                part = slice(owned * i, owned * (i + 1))
                place(
                    spot + i // 4,
                    i // 2 % 2,
                    i % 2,
                    2 * owned,
                    pl.ds(0, out.shape[1]),
                    out[part],
                )


def attention_grads(normed, joined, attended, grads, gain, owned):
    spots = len(DISTANCE)
    shape = (spots, 6 * owned, grads.shape[1])
    return pl.pallas_call(
        attention_grads_kernel,
        out_shape=[
            jax.ShapeDtypeStruct(shape, jnp.float32),
            jax.ShapeDtypeStruct(shape, jnp.bfloat16),
        ],
        compiler_params=pltpu.CompilerParams(vmem_limit_bytes=44 * 1024 * 1024),
        cost_estimate=pl.CostEstimate(
            flops=2 * normed.shape[0] * normed.shape[1] * (joined.shape[1] + grads.shape[1] // 2),
            bytes_accessed=20 * 1024 * 1024,
            transcendentals=0,
        ),
    )(normed, joined, attended, grads, gain)


def expert_kernel(place_ref, *refs, per_step, count):
    source_refs = refs[:count]
    given_ref, gate_ref, upper_ref, down_ref = refs[count : count + 4]
    back_refs = refs[-9 - count : -9]
    hidden_ref, grad_gate_ref, grad_upper_ref, rows_ref, grads_ref, narrow_ref = refs[-9:-3]
    route_ref, out_ref, back_ref = refs[-3:]
    step = pl.program_id(0)
    half, width = source_refs[0].shape

    @pl.when(step == 0)
    def _():
        for i, ref in enumerate(source_refs):
            rows_ref[half * i : half * (i + 1), :] = ref[...]
        grads_ref[...] = given_ref[:, :width]
        lanes = lax.broadcasted_iota(jnp.int32, route_ref.shape, 1)
        expert = (lanes + place_ref[2]).astype(jnp.float32)
        routes = given_ref[:, width:].astype(jnp.float32)
        weights = (
            routes[:, TOP : 2 * TOP]
            + routes[:, 2 * TOP : 3 * TOP]
            + routes[:, 3 * TOP : 4 * TOP]
        )
        dense = jnp.zeros_like(expert)
        for k in range(TOP):
            dense += jnp.where(expert == routes[:, k : k + 1], weights[:, k : k + 1], 0.0)
        route_ref[...] = dense
        out_ref[...] = jnp.zeros_like(out_ref)
        back_ref[...] = jnp.zeros_like(back_ref)

    rows = rows_ref[...]
    grads = grads_ref[...]
    contract_last = (((1,), (1,)), ((), ()))
    gate = jnp.dot(rows, gate_ref[...], preferred_element_type=jnp.float32)
    upper = jnp.dot(rows, upper_ref[...], preferred_element_type=jnp.float32)
    grad_hidden = lax.dot_general(
        grads, down_ref[...], contract_last, preferred_element_type=jnp.float32
    )
    route = route_ref[...]
    lanes = lax.broadcasted_iota(jnp.int32, route.shape, 1)
    columns = gate.shape[1] // per_step
    spread = []
    for i in range(per_step):
        one = jnp.sum(jnp.where(lanes == step * per_step + i, route, 0.0), 1, keepdims=True)
        spread.append(jnp.broadcast_to(one, (route.shape[0], columns)))
    weight = jnp.concatenate(spread, 1)
    sigma = 1.0 / (1.0 + jnp.exp(-gate))
    active = gate * sigma
    hidden = (weight * active * upper).astype(jnp.bfloat16)
    weighted = weight * grad_hidden
    grad_gate = (weighted * upper * sigma * (1.0 + gate * (1.0 - sigma))).astype(jnp.bfloat16)
    grad_upper = (weighted * active).astype(jnp.bfloat16)
    hidden_ref[...] = hidden
    grad_gate_ref[...] = grad_gate
    grad_upper_ref[...] = grad_upper
    out_ref[...] += jnp.dot(hidden, down_ref[...], preferred_element_type=jnp.float32)
    back_ref[...] += lax.dot_general(
        grad_gate, gate_ref[...], contract_last, preferred_element_type=jnp.float32
    ) + lax.dot_general(
        grad_upper, upper_ref[...], contract_last, preferred_element_type=jnp.float32
    )

    @pl.when(step == pl.num_programs(0) - 1)
    def _():
        narrow_ref[...] = out_ref[...].astype(jnp.bfloat16)
        for i, ref in enumerate(back_refs):
            ref[...] = back_ref[half * i : half * (i + 1), :].astype(ref.dtype)


def expert_block(place, spot, second, sources, given, weights, experts, filled):
    gate_w, upper_w, down_w = weights
    half, width = sources[0].shape
    wide = given.shape[1]
    total = gate_w.shape[1]
    per_step = 2
    steps = experts // per_step
    columns = total // steps
    count = len(sources)
    rows = half * count
    every = 2 * half * len(DISTANCE)
    at = (2 * spot + second) // count
    of = lambda p: p[3 + spot] * (2 // count) + second
    dtypes = (jnp.float32, jnp.bfloat16)[second : second + count]
    b16 = lambda r, c: jax.ShapeDtypeStruct((r, c), jnp.bfloat16)
    fixed = pl.BlockSpec((half, width), lambda i, p: (0, 0))
    part = pl.BlockSpec((rows, columns), lambda i, p: (at, i))
    kept = pl.BlockSpec((rows, width), lambda i, p: (at, 0))
    inputs = (place, *sources, given, gate_w, upper_w, down_w)
    return pl.pallas_call(
        functools.partial(expert_kernel, per_step=per_step, count=count),
        grid_spec=pltpu.PrefetchScalarGridSpec(
            num_scalar_prefetch=1,
            grid=(steps,),
            in_specs=[fixed] * count
            + [
                pl.BlockSpec((rows, wide), lambda i, p: (of(p), 0)),
                pl.BlockSpec((width, columns), lambda i, p: (0, i)),
                pl.BlockSpec((width, columns), lambda i, p: (0, i)),
                pl.BlockSpec((columns, width), lambda i, p: (i, 0)),
            ]
            + [pl.BlockSpec(memory_space=pl.ANY)] * len(filled),
            out_specs=[fixed] * count
            + [part] * 3
            + [kept] * 2
            + [pl.BlockSpec((rows, width), lambda i, p: (of(p), 0))],
            scratch_shapes=[
                pltpu.VMEM((rows, wide - width), jnp.float32),
                pltpu.VMEM((rows, width), jnp.float32),
                pltpu.VMEM((rows, width), jnp.float32),
            ],
        ),
        out_shape=[jax.ShapeDtypeStruct((half, width), dtype) for dtype in dtypes]
        + [b16(every, total)] * 3
        + [b16(every, width)] * 3,
        input_output_aliases={len(inputs) + i: count + i for i in range(len(filled))},
        compiler_params=pltpu.CompilerParams(vmem_limit_bytes=48 * 1024 * 1024),
        cost_estimate=pl.CostEstimate(
            flops=2 * rows * width * total * 6,
            bytes_accessed=2 * (3 * width * total + 3 * rows * total + 12 * rows * width),
            transcendentals=rows * total,
        ),
    )(*inputs, *filled)


def column_grads_kernel(
    place_ref, rows_ref, grad_gate_ref, grad_upper_ref, *refs
):
    keep_ref, give_ref, full_ref = refs[-3:]
    core = place_ref[1]
    contract = (((0,), (0,)), ((), ()))
    chips, _, plane_rows, _ = keep_ref.shape
    for part, ref in enumerate((grad_gate_ref, grad_upper_ref)):
        full_ref[...] = lax.dot_general(
            rows_ref[...], ref[...], contract, preferred_element_type=jnp.float32
        )
        for chip in range(chips):
            mine = pl.multiple_of((2 * chip + core) * plane_rows, plane_rows)
            theirs = pl.multiple_of((2 * chip + 1 - core) * plane_rows, plane_rows)
            keep_ref[chip, part] = full_ref[pl.ds(mine, plane_rows), :]
            give_ref[chip, part] = full_ref[pl.ds(theirs, plane_rows), :].astype(give_ref.dtype)


def column_grads(place, step, steps, rows_all, grad_gate, grad_upper, chips, filled):
    tokens, width = rows_all.shape
    total = grad_gate.shape[1]
    columns = total // steps
    plane_rows = width // (2 * chips)
    part = pl.BlockSpec((tokens, columns), lambda i, p: (0, step))
    wide = pl.BlockSpec((chips, 2, plane_rows, columns), lambda i, p: (0, 0, 0, step))
    shape = (chips, 2, plane_rows, total)
    return pl.pallas_call(
        column_grads_kernel,
        grid_spec=pltpu.PrefetchScalarGridSpec(
            num_scalar_prefetch=1,
            grid=(1,),
            in_specs=[pl.BlockSpec((tokens, width), lambda i, p: (0, 0)), part, part]
            + [pl.BlockSpec(memory_space=pl.ANY)] * len(filled),
            out_specs=[wide, wide],
            scratch_shapes=[pltpu.VMEM((width, columns), jnp.float32)],
        ),
        out_shape=[
            jax.ShapeDtypeStruct(shape, jnp.float32),
            jax.ShapeDtypeStruct(shape, jnp.bfloat16),
        ],
        input_output_aliases={4 + i: i for i in range(len(filled))},
        compiler_params=pltpu.CompilerParams(vmem_limit_bytes=56 * 1024 * 1024),
        cost_estimate=pl.CostEstimate(
            flops=4 * tokens * width * columns,
            bytes_accessed=2 * tokens * (width + 2 * columns) + 6 * 2 * width * columns,
            transcendentals=0,
        ),
    )(place, rows_all, grad_gate, grad_upper, *filled)


def down_grads_kernel(place_ref, grads_ref, hidden_ref, keep_ref, give_ref, full_ref):
    core = place_ref[1]
    full_ref[...] = lax.dot_general(
        hidden_ref[...],
        grads_ref[...],
        (((0,), (0,)), ((), ())),
        preferred_element_type=jnp.float32,
    )
    experts, down_rows, _ = keep_ref.shape
    for e in range(experts):
        mine = pl.multiple_of((2 * e + core) * down_rows, down_rows)
        theirs = pl.multiple_of((2 * e + 1 - core) * down_rows, down_rows)
        keep_ref[e] = full_ref[pl.ds(mine, down_rows), :]
        give_ref[e] = full_ref[pl.ds(theirs, down_rows), :]


def down_grads(place, steps, grads_all, hidden, experts):
    tokens, width = grads_all.shape
    total = hidden.shape[1]
    columns = total // steps
    per_step = experts // steps
    down_rows = total // experts // 2
    down = pl.BlockSpec((per_step, down_rows, width), lambda i, p: (i, 0, 0))
    return pl.pallas_call(
        down_grads_kernel,
        grid_spec=pltpu.PrefetchScalarGridSpec(
            num_scalar_prefetch=1,
            grid=(steps,),
            in_specs=[
                pl.BlockSpec((tokens, width), lambda i, p: (0, 0)),
                pl.BlockSpec((tokens, columns), lambda i, p: (0, i)),
            ],
            out_specs=[down, down],
            scratch_shapes=[pltpu.VMEM((columns, width), jnp.float32)],
        ),
        out_shape=[jax.ShapeDtypeStruct((experts, down_rows, width), jnp.float32)] * 2,
        compiler_params=pltpu.CompilerParams(vmem_limit_bytes=36 * 1024 * 1024),
        cost_estimate=pl.CostEstimate(
            flops=2 * tokens * width * total,
            bytes_accessed=2 * tokens * (width + total) + 4 * width * total,
            transcendentals=0,
        ),
    )(place, grads_all, hidden)


def adam_columns_kernel(w_ref, first_ref, second_ref, grad_ref, *outs):
    chips, _, _, lanes = grad_ref.shape
    for chip in range(chips):
        for part in range(2):
            columns = slice(part * FF + chip * lanes, part * FF + (chip + 1) * lanes)
            grad = grad_ref[chip, part].astype(jnp.float32)
            found = adam_step(
                w_ref[0, :, columns],
                grad,
                first_ref[0, :, columns],
                second_ref[0, :, columns],
                learn_rate,
                weight_decay,
            )
            for out_ref, value in zip(outs, (grad,) + found):
                out_ref[0, :, columns] = value


def adam_columns(weight, first, second, grads):
    experts, rows, both = weight.shape
    chips = grads.shape[0]
    lanes = grads.shape[3] // experts
    block = pl.BlockSpec((1, rows, both), lambda e: (e, 0, 0))
    return pl.pallas_call(
        adam_columns_kernel,
        grid=(experts,),
        in_specs=[block] * 3 + [pl.BlockSpec((chips, 2, rows, lanes), lambda e: (0, 0, 0, e))],
        out_specs=[block] * 4,
        out_shape=[jax.ShapeDtypeStruct(weight.shape, jnp.float32)] * 4,
        compiler_params=pltpu.CompilerParams(vmem_limit_bytes=56 * 1024 * 1024),
        cost_estimate=pl.CostEstimate(
            flops=20 * experts * rows * both,
            bytes_accessed=30 * experts * rows * both,
            transcendentals=experts * rows * both,
        ),
    )(weight, first, second, grads)


def shards_moved(
    tokens,
    cotangent,
    segments,
    expert_ids,
    route_weights,
    w_qkv,
    w_out,
    gains,
    w_gate_up,
    w_down,
    first_moment_projection,
    first_out,
    first_gains,
    first_gate_up,
    first_down,
    second_moment_projection,
    second_out,
    second_gains,
    second_gate_up,
    second_down,
):
    sequence_length = segments.shape[1]
    count_dp, count_expert = lax.axis_size("dp"), lax.axis_size("expert")
    place_dp, place_expert = lax.axis_index("dp"), lax.axis_index("expert")
    core = place_dp % 2
    chip = place_dp // 2
    chips = count_dp // 2
    local_experts = EXPERTS // count_expert
    owned = w_qkv.shape[0]
    half_columns = w_qkv.shape[1] // 2
    half_width = MODEL_WIDTH // 2
    lane_pad = 128

    narrow_qkv = w_qkv.astype(NARROW)
    even_columns, odd_columns = parity_columns(narrow_qkv, 0), parity_columns(narrow_qkv, 1)
    gain_columns = jnp.pad(gains.astype(NARROW).T, ((0, 0), (0, lane_pad - 2)))
    kept = jnp.where(core == 0, even_columns, odd_columns)
    given = jnp.where(core == 0, odd_columns, even_columns)
    rest = jnp.zeros((owned, MODEL_WIDTH - half_columns - lane_pad), NARROW)
    taken = swap_core(jnp.concatenate([given, gain_columns], 1))
    block = jnp.concatenate(
        [
            jnp.concatenate([kept, gain_columns, rest], 1),
            jnp.concatenate([taken, rest], 1),
            w_out.astype(NARROW),
        ],
        0,
    )
    share = local_experts * (FF // chips)
    ahead, behind = turn(block, 1), turn(block, -1)
    pieces = spread_columns(after(w_gate_up, taken), chips)
    attention_ring = [block, ahead, behind, turn(after(ahead, pieces), 1)]
    attention_pairs = [along_first(part) for part in attention_ring[:2]]
    routes = jnp.concatenate([expert_ids.astype(NARROW)] + split_three(route_weights), 1)
    cotangent_rows = jnp.concatenate(
        [
            cotangent.astype(NARROW),
            jnp.pad(routes, ((0, 0), (0, lane_pad - routes.shape[1]))),
        ],
        1,
    )
    cotangent_pair = along_first(cotangent_rows)
    cotangent_here = jnp.concatenate([cotangent_pair, swap_second(cotangent_pair)], 0)
    cotangent_all = lax.all_gather(
        after(cotangent_here, attention_ring), "expert", axis=0, tiled=True
    )
    attention_pairs.append(along_first(attention_ring[2]))
    attention_pairs.append(along_first(after(attention_ring[3], cotangent_here)))
    attention_blocks = [(pair, swap_second(pair)) for pair in attention_pairs]

    sources = jnp.asarray(gathered_sources(count_dp, count_expert))[place_dp, place_expert]
    from_dp, from_expert = sources[:, 0], sources[:, 1]
    row_in = jnp.arange(owned, dtype=jnp.int32)
    feature = (
        ((from_dp[:, None] ^ jnp.arange(2, dtype=jnp.int32)[None, :]) * count_expert
         + from_expert[:, None])[:, :, None] * owned + row_in
    ).reshape(-1)
    head_feature = (
        ((from_dp // 2 * count_expert + from_expert) * owned)[:, None] + row_in
    ).reshape(-1)
    places = jnp.arange(MODEL_WIDTH, dtype=jnp.int32)
    to_gathered = (places[:, None] == feature[None, :]).astype(NARROW)
    from_gathered = (feature[:, None] == places[None, :]).astype(NARROW)
    head_places = places[: half_width]
    heads_to_gathered = (head_places[:, None] == head_feature[None, :]).astype(NARROW)
    heads_from_gathered = (head_feature[:, None] == head_places[None, :]).astype(NARROW)

    found_at = (place_expert - jnp.asarray(DISTANCE, jnp.int32)) % count_expert
    place = jnp.concatenate(
        [jnp.stack([chip, core, place_expert * local_experts]).astype(jnp.int32), found_at]
    )
    parities = [list(range(i, count_dp, 2)) for i in range(2)]
    pieces = lax.all_to_all(
        pieces, "dp", 0, 0, axis_index_groups=parities, tiled=True
    )
    down_mine = after(w_down, attention_pairs[0]).astype(NARROW)
    down_theirs = swap_core(down_mine)
    down_w = jnp.where(
        core == 0,
        jnp.concatenate([down_mine, down_theirs], 1),
        jnp.concatenate([down_theirs, down_mine], 1),
    ).reshape(share, MODEL_WIDTH)
    attention_blocks = after(attention_blocks, (down_w, pieces))

    cosine_table, sine_table = rotary_tables(sequence_length, HEAD_SIZE // 2)
    inputs = tokens.astype(WIDE)
    pair_tokens = jnp.concatenate([tokens, swap_core(tokens)], 0)
    pair_segments = jnp.concatenate([segments, swap_core(segments)], 0)
    scale_pair = norm_scale(pair_tokens.astype(WIDE))
    scale_one = scale_pair[:sequence_length]
    pair_gathered = jnp.dot(pair_tokens, to_gathered, preferred_element_type=jnp.float32)
    blocks = [half for pair in attention_blocks for half in pair]
    qkv_here, gain_here, out_here = stack_attention(blocks, half_columns, lane_pad)
    gain_here = gain_here[:, :2].T
    gain_attn = gain_here[0].astype(WIDE)
    gains_placed = jnp.dot(gain_here, from_gathered, preferred_element_type=jnp.float32)
    gain_moe = gains_placed[1]
    normed_one = (pair_gathered * scale_pair * gain_attn).astype(NARROW)
    projected = jnp.dot(normed_one, qkv_here, preferred_element_type=jnp.float32)
    query_block, key_rows, value_rows = split_head_group(
        projected.reshape(2, sequence_length, -1), cosine_table, sine_table
    )
    attended, logsums = jax.vmap(attend)(query_block, key_rows, value_rows, pair_segments)
    attended = attended.reshape(2 * sequence_length, half_width)
    attended = jnp.dot(attended, heads_to_gathered, preferred_element_type=jnp.float32).astype(
        NARROW
    )
    resid_parts = jnp.dot(attended, out_here, preferred_element_type=jnp.float32)
    resid = inputs + resid_parts[:sequence_length] + swap_core(resid_parts[sequence_length:])
    scale_two = norm_scale(resid)
    normed_two = (resid * scale_two * gain_moe).astype(NARROW)
    normed_two = after(normed_two, pieces)

    normed_ring = [normed_two] + [turn(normed_two, distance) for distance in DISTANCE[1:]]
    gate_w, upper_w = stack_rows(place, pieces, after(swap_core(pieces), normed_two))
    back_parts, filled = [], []
    second_parts, begun, halves, backs = [], (), [], {}
    for spot, second in ((0, 0), (0, 1), (1, 0), (2, 0), (1, 1), (2, 1), (3, 0)):
        if second == 0:
            near = along_first(after(normed_ring[spot], begun))
            halves.append((near, swap_second(near)))
        sources = halves[spot] if spot == 3 else halves[spot][second : second + 1]
        if spot >= 2 and (spot, second) != (2, 0):
            gate = (second_parts[spot - 2], back_parts[: spot - 2])
            sources = after(sources, gate)
        done = expert_block(
            place,
            spot,
            second,
            sources,
            cotangent_all,
            (gate_w, upper_w, down_w),
            local_experts,
            filled,
        )
        backs.setdefault(spot, []).extend(done[: len(sources)])
        filled = done[len(sources) :]
        begun = begun or (done[0],)
        if second == 1:
            second_parts.append(add_second(*backs[spot]))
            back_parts.append(add_first(second_parts[-1]))
    back = backs[3]
    hidden, grad_gate, grad_upper, rows_all, grads_all, out_all = filled
    steps = local_experts // 2
    kept_grads = []
    for step in range(steps):
        kept_grads = column_grads(
            place, step, steps, rows_all, grad_gate, grad_upper, chips, kept_grads
        )
        if step == 0:
            last = add_second(*back, kept_grads)
        elif step == 1:
            back_parts.append(add_first(last, kept_grads))
        elif step == 2:
            found = [
                turn(part.astype(NARROW), -distance)
                for part, distance in zip(back_parts[1:], DISTANCE[1:])
            ]
            grad_normed_two = back_parts[0] + sum(
                part.astype(WIDE) for part in after(found, kept_grads)
            )
            rows_all = after(rows_all, grad_normed_two)
    keep, give = kept_grads
    taken = swap_core(give)
    expert_sums = (keep + taken.astype(WIDE)).astype(NARROW)
    parities = [list(range(i, count_dp, 2)) for i in range(2)]
    collected = lax.all_to_all(
        expert_sums, "dp", 0, 0, axis_index_groups=parities, tiled=True
    )
    out_sums = lax.psum_scatter(
        after(out_all, grad_normed_two), "expert", scatter_dimension=0, tiled=True
    )

    hat_two = grad_normed_two * gain_moe
    grad_gain_moe = jnp.sum(grad_normed_two * resid * scale_two, 0)
    grad_resid = cotangent + scale_two * (
        hat_two - resid * scale_two**2 * jnp.mean(hat_two * resid, -1, keepdims=True)
    )
    grad_resid_half = grad_resid.astype(NARROW)
    pair_grads = jnp.concatenate([grad_resid_half, swap_core(grad_resid_half)], 0)
    attended_gradient = lax.dot_general(
        pair_grads, out_here, (((1,), (1,)), ((), ())), preferred_element_type=jnp.float32
    ).astype(NARROW)
    attended_gradient = (
        jnp.dot(attended_gradient, heads_from_gathered, preferred_element_type=jnp.float32)
        .astype(NARROW)
        .reshape(query_block.shape)
    )
    grad_query, grad_keys, grad_values = jax.vmap(attend_back)(
        query_block, key_rows, value_rows, pair_segments, logsums, attended_gradient
    )
    joined = jax.vmap(lambda a, b, c: join_grads(a, b, c, cosine_table, sine_table))(
        grad_query, grad_keys, grad_values
    ).reshape(2 * sequence_length, -1)
    joined = after(joined, expert_sums)
    grad_normed_parts = lax.dot_general(
        joined, qkv_here, (((1,), (1,)), ((), ())), preferred_element_type=jnp.float32
    )
    grad_gain_attn = jnp.sum(grad_normed_parts * pair_gathered * scale_pair, 0)
    gain_parts = jnp.stack(
        [grad_gain_attn, select_columns(grad_gain_moe[None], to_gathered)[0]], 1
    )
    near_parts, away_parts = attention_grads(
        normed_one,
        joined,
        attended,
        pair_grads,
        jnp.pad(gain_parts, ((0, 0), (0, lane_pad - 2))),
        owned,
    )
    keep_down, give_down = down_grads(
        place, steps, after(grads_all, near_parts), hidden, local_experts
    )
    part_down = keep_down + swap_core(give_down)
    new_down, new_first_down, new_second_down = adam_step(
        w_down, part_down, first_down, second_down, learn_rate, weight_decay
    )
    part_gate_up, new_gate_up, new_first_gate_up, new_second_gate_up = adam_columns(
        w_gate_up, first_gate_up, second_gate_up, after(collected, near_parts)
    )
    in_plane = [None] * len(DISTANCE)
    for i in (3, 1, 2, 0):
        in_plane[i] = add_second(near_parts[i], away_parts[i], new_gate_up)
    for i in (3, 1, 2, 0):
        in_plane[i] = add_first(in_plane[i])
    out_sums = after(out_sums, in_plane[3]).astype(WIDE)
    out_half = out_sums.shape[0] // 2
    out_sums = add_second(out_sums[:out_half], out_sums[out_half:])
    summed = ring_sum(in_plane, (new_down, out_sums))
    out_tokens = resid + add_first(out_sums, summed)
    here, there, part_out = summed[:owned], summed[owned : 2 * owned], summed[2 * owned :]
    there = swap_core(there[:, : half_columns + lane_pad])
    part_gains = (
        here[:, half_columns : half_columns + 2] + there[:, half_columns : half_columns + 2]
    ).T
    here, there = here[:, :half_columns], there[:, :half_columns]
    part_qkv = join_parities(
        jnp.where(core == 0, here, there), jnp.where(core == 0, there, here)
    )

    grad_normed_parts = select_columns(grad_normed_parts, from_gathered)
    grad_normed_one = grad_normed_parts[:sequence_length] + swap_core(
        grad_normed_parts[sequence_length:]
    )
    hat_one = grad_normed_one * gains_placed[0]
    grad_tokens = grad_resid + scale_one * (
        hat_one - inputs * scale_one**2 * jnp.mean(hat_one * inputs, -1, keepdims=True)
    )

    new_qkv, new_first_qkv, new_second_qkv = adam_step(
        w_qkv, part_qkv, first_moment_projection, second_moment_projection, learn_rate, weight_decay
    )
    new_out, new_first_out, new_second_out = adam_step(
        w_out, part_out, first_out, second_out, out_rate, weight_decay
    )
    new_gains, new_first_gains, new_second_gains = adam_step(
        gains, part_gains, first_gains, second_gains, gain_rate, 0.0
    )
    return (
        out_tokens,
        grad_tokens,
        part_qkv,
        part_out,
        part_gains,
        part_gate_up,
        part_down,
        new_qkv,
        new_out,
        new_gains,
        new_gate_up,
        new_down,
        new_first_qkv,
        new_first_out,
        new_first_gains,
        new_first_gate_up,
        new_first_down,
        new_second_qkv,
        new_second_out,
        new_second_gains,
        new_second_gate_up,
        new_second_down,
    )


def shards_plain(
    tokens,
    cotangent,
    segments,
    expert_ids,
    route_weights,
    w_qkv,
    w_out,
    gains,
    w_gate_up,
    w_down,
    first_moment_projection,
    first_out,
    first_gains,
    first_gate_up,
    first_down,
    second_moment_projection,
    second_out,
    second_gains,
    second_gate_up,
    second_down,
):
    sequence_count = segments.shape[0]
    sequence_length = segments.shape[1]
    groups_expert = lax.axis_size("expert")
    local_experts = EXPERTS // groups_expert
    slot_rows = groups_expert * CAP
    qkv_full, out_full, gain_full = (
        lax.all_gather(w_qkv.astype(jnp.bfloat16), ("dp", "expert"), axis=0, tiled=True),
        lax.all_gather(w_out.astype(jnp.bfloat16), ("dp", "expert"), axis=0, tiled=True),
        lax.all_gather(gains.astype(jnp.bfloat16), ("dp", "expert"), axis=1, tiled=True),
    )
    gate_up_full, down_full = (
        lax.all_gather(w_gate_up.astype(jnp.bfloat16), "dp", axis=1, tiled=True),
        lax.all_gather(w_down.astype(jnp.bfloat16), "dp", axis=1, tiled=True),
    )
    gain_attn = gain_full[0].astype(jnp.float32)
    gain_moe = gain_full[1].astype(jnp.float32)
    cosine_table, sine_table = rotary_tables(sequence_length, HEAD_SIZE // 2)
    inputs = tokens.astype(jnp.float32)
    scale_one = norm_scale(inputs)
    normed_one = (inputs * scale_one * gain_attn).astype(jnp.bfloat16)
    projected_rows = jnp.dot(normed_one, qkv_full, preferred_element_type=jnp.float32)
    query_block, key_rows, value_rows = split_heads(
        projected_rows, sequence_count, sequence_length, cosine_table, sine_table
    )
    index = 0
    attended_seq, logsum = attend(
        query_block[index], key_rows[index], value_rows[index], segments[index]
    )
    pieces = attended_seq.reshape(sequence_length, QUERY_HEADS * HEAD_SIZE)
    logsums = [logsum]
    resid = inputs + jnp.dot(pieces, out_full, preferred_element_type=jnp.float32)
    scale_two = norm_scale(resid)
    normed_two = (resid * scale_two * gain_moe).astype(jnp.bfloat16)
    flat_ids = expert_ids.reshape(-1)
    pair_count = flat_ids.shape[0]
    one_hot = (flat_ids[:, None] == jnp.arange(EXPERTS, dtype=jnp.int32)[None, :]).astype(jnp.int32)
    ranking = jnp.sum(jnp.cumsum(one_hot, 0) * one_hot, 1) - 1
    target = flat_ids * CAP + ranking
    owners = (
        jnp.full((EXPERTS * CAP,), -1, jnp.int32)
        .at[target]
        .set(jnp.arange(pair_count, dtype=jnp.int32))
    )
    filled = (owners >= 0)[:, None]
    safe_owner = jnp.maximum(owners, 0)
    send_rows = jnp.where(filled, normed_two[safe_owner // TOP], jnp.zeros((), jnp.bfloat16))
    received = lax.all_to_all(
        send_rows.reshape(groups_expert, local_experts, CAP, MODEL_WIDTH),
        "expert",
        split_axis=0,
        concat_axis=2,
        tiled=True,
    )
    received = received.reshape(local_experts, slot_rows, MODEL_WIDTH)
    mixed = jnp.einsum("erd,edf->erf", received, gate_up_full, preferred_element_type=jnp.float32)
    gate = mixed[..., :FF]
    upper = mixed[..., FF:]
    hidden = (jax.nn.silu(gate) * upper).astype(jnp.bfloat16)
    expert_out = jnp.einsum(
        "erf,efd->erd", hidden, down_full, preferred_element_type=jnp.float32
    ).astype(jnp.bfloat16)
    returned = lax.all_to_all(
        expert_out.reshape(1, local_experts, slot_rows, MODEL_WIDTH),
        "expert",
        split_axis=2,
        concat_axis=0,
        tiled=True,
    )
    picked = returned.reshape(EXPERTS * CAP, MODEL_WIDTH)[target].reshape(-1, TOP, MODEL_WIDTH)
    out_tokens = resid + jnp.sum(route_weights[..., None] * picked.astype(jnp.float32), 1)
    gate_up_back, down_back = (
        lax.all_gather(w_gate_up.astype(jnp.bfloat16), "dp", axis=1, tiled=True),
        lax.all_gather(w_down.astype(jnp.bfloat16), "dp", axis=1, tiled=True),
    )
    grad_routed = (
        (route_weights[..., None] * cotangent[:, None, :])
        .astype(jnp.bfloat16)
        .reshape(pair_count, MODEL_WIDTH)
    )
    send_grads = jnp.where(filled, grad_routed[safe_owner], jnp.zeros((), jnp.bfloat16))
    grad_expert = lax.all_to_all(
        send_grads.reshape(groups_expert, local_experts, CAP, MODEL_WIDTH),
        "expert",
        split_axis=0,
        concat_axis=2,
        tiled=True,
    )
    grad_expert = grad_expert.reshape(local_experts, slot_rows, MODEL_WIDTH)
    grad_hidden = jnp.einsum(
        "erd,efd->erf", grad_expert, down_back, preferred_element_type=jnp.float32
    )
    grad_down = jnp.einsum("erf,erd->efd", hidden, grad_expert, preferred_element_type=jnp.float32)
    sigma = jax.nn.sigmoid(gate)
    grad_mixed = jnp.concatenate(
        [grad_hidden * upper * sigma * (1.0 + gate * (1.0 - sigma)), grad_hidden * gate * sigma], -1
    ).astype(jnp.bfloat16)
    grad_gate_up = jnp.einsum(
        "erd,erf->edf", received, grad_mixed, preferred_element_type=jnp.float32
    )
    grad_received = jnp.einsum(
        "erf,edf->erd", grad_mixed, gate_up_back, preferred_element_type=jnp.float32
    ).astype(jnp.bfloat16)
    grad_back = lax.all_to_all(
        grad_received.reshape(1, local_experts, slot_rows, MODEL_WIDTH),
        "expert",
        split_axis=2,
        concat_axis=0,
        tiled=True,
    )
    grad_normed_two = jnp.sum(
        grad_back.reshape(EXPERTS * CAP, MODEL_WIDTH)[target]
        .reshape(-1, TOP, MODEL_WIDTH)
        .astype(jnp.float32),
        1,
    )
    hat_two = grad_normed_two * gain_moe
    grad_gain_moe = jnp.sum(grad_normed_two * resid * scale_two, 0)
    grad_resid = cotangent + scale_two * (
        hat_two - resid * scale_two**2 * jnp.mean(hat_two * resid, -1, keepdims=True)
    )
    grad_resid_half = grad_resid.astype(jnp.bfloat16)
    qkv_back, out_back = (
        lax.all_gather(w_qkv.astype(jnp.bfloat16), ("dp", "expert"), axis=0, tiled=True),
        lax.all_gather(w_out.astype(jnp.bfloat16), ("dp", "expert"), axis=0, tiled=True),
    )
    grad_out = jnp.dot(pieces.T, grad_resid_half, preferred_element_type=jnp.float32)
    attended_gradient = jnp.dot(
        grad_resid_half, out_back.T, preferred_element_type=jnp.float32
    ).astype(jnp.bfloat16)
    attended_gradient = attended_gradient.reshape(
        sequence_count, sequence_length, KEY_VALUE_HEADS, QUERY_HEADS // KEY_VALUE_HEADS, HEAD_SIZE
    )
    index = 0
    grad_query, grad_keys, grad_values = attend_back(
        query_block[index],
        key_rows[index],
        value_rows[index],
        segments[index],
        logsums[index],
        attended_gradient[index],
    )
    joined = join_grads(grad_query, grad_keys, grad_values, cosine_table, sine_table)
    grad_qkv = jnp.dot(normed_one.T, joined, preferred_element_type=jnp.float32)
    grad_normed_one = jnp.dot(joined, qkv_back.T, preferred_element_type=jnp.float32)
    hat_one = grad_normed_one * gain_attn
    grad_gain_attn = jnp.sum(grad_normed_one * inputs * scale_one, 0)
    grad_tokens = grad_resid + scale_one * (
        hat_one - inputs * scale_one**2 * jnp.mean(hat_one * inputs, -1, keepdims=True)
    )
    grad_gains = jnp.stack([grad_gain_attn, grad_gain_moe])
    part_qkv, part_out, part_gains = (
        lax.psum_scatter(grad_qkv, ("dp", "expert"), scatter_dimension=0, tiled=True),
        lax.psum_scatter(grad_out, ("dp", "expert"), scatter_dimension=0, tiled=True),
        lax.psum_scatter(grad_gains, ("dp", "expert"), scatter_dimension=1, tiled=True),
    )
    part_gate_up, part_down = (
        lax.psum_scatter(grad_gate_up, "dp", scatter_dimension=1, tiled=True),
        lax.psum_scatter(grad_down, "dp", scatter_dimension=1, tiled=True),
    )
    new_qkv, new_first_qkv, new_second_qkv = adam_step(
        w_qkv, part_qkv, first_moment_projection, second_moment_projection, learn_rate, weight_decay
    )
    new_out, new_first_out, new_second_out = adam_step(
        w_out, part_out, first_out, second_out, out_rate, weight_decay
    )
    new_gains, new_first_gains, new_second_gains = adam_step(
        gains, part_gains, first_gains, second_gains, gain_rate, 0.0
    )
    new_gate_up, new_first_gate_up, new_second_gate_up = adam_step(
        w_gate_up, part_gate_up, first_gate_up, second_gate_up, learn_rate, weight_decay
    )
    new_down, new_first_down, new_second_down = adam_step(
        w_down, part_down, first_down, second_down, learn_rate, weight_decay
    )
    return (
        out_tokens,
        grad_tokens,
        part_qkv,
        part_out,
        part_gains,
        part_gate_up,
        part_down,
        new_qkv,
        new_out,
        new_gains,
        new_gate_up,
        new_down,
        new_first_qkv,
        new_first_out,
        new_first_gains,
        new_first_gate_up,
        new_first_down,
        new_second_qkv,
        new_second_out,
        new_second_gains,
        new_second_gate_up,
        new_second_down,
    )


def solution(mesh):
    by_heads = mesh.shape["dp"] == KEY_VALUE_HEADS and mesh.shape["expert"] == 4
    return jax.shard_map(
        shards_moved if by_heads else shards_plain,
        mesh=mesh,
        in_specs=(
            P(("dp", "expert"), None),
            P(("dp", "expert"), None),
            P(("dp", "expert"), None),
            P(("dp", "expert"), None),
            P(("dp", "expert"), None),
            P(("dp", "expert"), None),
            P(("dp", "expert"), None),
            P(None, ("dp", "expert")),
            P("expert", "dp", None),
            P("expert", "dp", None),
            P(("dp", "expert"), None),
            P(("dp", "expert"), None),
            P(None, ("dp", "expert")),
            P("expert", "dp", None),
            P("expert", "dp", None),
            P(("dp", "expert"), None),
            P(("dp", "expert"), None),
            P(None, ("dp", "expert")),
            P("expert", "dp", None),
            P("expert", "dp", None),
        ),
        out_specs=(
            P(("dp", "expert"), None),
            P(("dp", "expert"), None),
            P(("dp", "expert"), None),
            P(("dp", "expert"), None),
            P(None, ("dp", "expert")),
            P("expert", "dp", None),
            P("expert", "dp", None),
            P(("dp", "expert"), None),
            P(("dp", "expert"), None),
            P(None, ("dp", "expert")),
            P("expert", "dp", None),
            P("expert", "dp", None),
            P(("dp", "expert"), None),
            P(("dp", "expert"), None),
            P(None, ("dp", "expert")),
            P("expert", "dp", None),
            P("expert", "dp", None),
            P(("dp", "expert"), None),
            P(("dp", "expert"), None),
            P(None, ("dp", "expert")),
            P("expert", "dp", None),
            P("expert", "dp", None),
        ),
        check_vma=False,
    )
```

```python
import functools

import jax
import jax.numpy as jnp
import numpy as np
from jax import lax
from jax.experimental import pallas as pl
from jax.experimental.pallas import tpu as pltpu
from jax.sharding import PartitionSpec as P

MODEL_WIDTH = 1536
QUERY_HEADS = 24
KEY_VALUE_HEADS = 8
HEAD_SIZE = 64
FF = 512
EXPERTS = 40
TOP = 8
CAP = 32


eps_norm = 1e-05
beta_one = 0.9
beta_two = 0.95
adam_eps = 1e-08
learn_rate = 0.01
out_rate = 0.04
gain_rate = 0.2
weight_decay = 0.1
correct_one = 1.0 - beta_one**3
correct_two = 1.0 - beta_two**3


def norm_scale(rows):
    return lax.rsqrt(jnp.mean(rows * rows, -1, keepdims=True) + eps_norm)


def rotary_tables(sequence_length, half_dim):
    position = jnp.arange(sequence_length, dtype=jnp.float32)[:, None]
    frequency = 10000.0 ** (-jnp.arange(half_dim, dtype=jnp.float32) / half_dim)
    angles = position * frequency[None, :]
    return (jnp.cos(angles), jnp.sin(angles))


def apply_rotary(value_rows, cosine_table, sine_table, middle):
    half_dim = value_rows.shape[-1] // 2
    shape = (cosine_table.shape[0],) + (1,) * middle + (half_dim,)
    cosine_table = cosine_table.reshape(shape)
    sine_table = sine_table.reshape(shape)
    first = value_rows[..., :half_dim]
    second = value_rows[..., half_dim:]
    return jnp.concatenate(
        [first * cosine_table - second * sine_table, second * cosine_table + first * sine_table], -1
    )


def split_heads(projected_rows, sequence_count, sequence_length, cosine_table, sine_table):
    query_total_width = QUERY_HEADS * HEAD_SIZE
    key_columns_width = KEY_VALUE_HEADS * HEAD_SIZE
    reshaped_rows = projected_rows.reshape(sequence_count, sequence_length, -1)
    query_block = apply_rotary(
        reshaped_rows[..., :query_total_width].reshape(
            sequence_count,
            sequence_length,
            KEY_VALUE_HEADS,
            QUERY_HEADS // KEY_VALUE_HEADS,
            HEAD_SIZE,
        ),
        cosine_table,
        sine_table,
        2,
    )
    key_rows = apply_rotary(
        reshaped_rows[..., query_total_width : query_total_width + key_columns_width].reshape(
            sequence_count, sequence_length, KEY_VALUE_HEADS, HEAD_SIZE
        ),
        cosine_table,
        sine_table,
        1,
    )
    value_rows = reshaped_rows[..., query_total_width + key_columns_width :].reshape(
        sequence_count, sequence_length, KEY_VALUE_HEADS, HEAD_SIZE
    )
    return (
        query_block.astype(jnp.bfloat16),
        key_rows.astype(jnp.bfloat16),
        value_rows.astype(jnp.bfloat16),
    )


def allowed_mask(segment):
    spots = jnp.arange(segment.shape[0])
    return (spots[:, None] >= spots[None, :]) & (segment[:, None] == segment[None, :])


def score_block(query_block, key_rows, segment):
    scores = jnp.einsum(
        "qhgd,khd->hgqk", query_block, key_rows, preferred_element_type=jnp.float32
    ) * query_block.shape[-1] ** (-0.5)
    return jnp.where(allowed_mask(segment)[None, None], scores, -1e30)


def attend(query_block, key_rows, value_rows, segment):
    scores = score_block(query_block, key_rows, segment)
    highest = jnp.max(scores, -1, keepdims=True)
    logsum = highest + jnp.log(jnp.sum(jnp.exp(scores - highest), -1, keepdims=True))
    probs = jnp.exp(scores - logsum).astype(jnp.bfloat16)
    attended = jnp.einsum("hgqk,khd->qhgd", probs, value_rows, preferred_element_type=jnp.float32)
    return (attended.astype(jnp.bfloat16), logsum)


def attend_back(query_block, key_rows, value_rows, segment, logsum, attended_gradient):
    factor = query_block.shape[-1] ** (-0.5)
    probs = jnp.exp(score_block(query_block, key_rows, segment) - logsum)
    grad_probs = jnp.einsum(
        "qhgd,khd->hgqk", attended_gradient, value_rows, preferred_element_type=jnp.float32
    )
    inner_sum = jnp.sum(probs * grad_probs, -1, keepdims=True)
    grad_scores = (probs * (grad_probs - inner_sum) * factor).astype(jnp.bfloat16)
    grad_values = jnp.einsum(
        "hgqk,qhgd->khd",
        probs.astype(jnp.bfloat16),
        attended_gradient,
        preferred_element_type=jnp.float32,
    )
    grad_query = jnp.einsum(
        "hgqk,khd->qhgd", grad_scores, key_rows, preferred_element_type=jnp.float32
    )
    grad_keys = jnp.einsum(
        "hgqk,qhgd->khd", grad_scores, query_block, preferred_element_type=jnp.float32
    )
    return (grad_query, grad_keys, grad_values)


def join_grads(grad_query, grad_keys, grad_values, cosine_table, sine_table):
    sequence_length = grad_query.shape[0]
    grad_query = apply_rotary(grad_query, cosine_table, -sine_table, 2).reshape(sequence_length, -1)
    grad_keys = apply_rotary(grad_keys, cosine_table, -sine_table, 1).reshape(sequence_length, -1)
    return jnp.concatenate(
        [grad_query, grad_keys, grad_values.reshape(sequence_length, -1)], -1
    ).astype(jnp.bfloat16)


def adam_step(weight, grad, first, second, step_rate, shrink):
    first = beta_one * first + (1.0 - beta_one) * grad
    second = beta_two * second + (1.0 - beta_two) * grad * grad
    update = first / correct_one / (jnp.sqrt(second / correct_two) + adam_eps)
    return (weight - step_rate * (update + shrink * weight), first, second)


NARROW = jnp.bfloat16
WIDE = jnp.float32
DISTANCE = (0, 1, -1, 2)
HOP_CORE, HOP_X, HOP_Y = 1, 2, 4


def swap(rows, pick):
    count = lax.axis_size("dp")
    return lax.ppermute(rows, "dp", [(i, i ^ pick(i)) for i in range(count)])


def first_hop(i):
    return HOP_X if i & 1 else HOP_Y


def second_hop(i):
    return HOP_Y if i & 1 else HOP_X


def swap_core(rows):
    return swap(rows, lambda i: HOP_CORE)


def swap_first(rows):
    return swap(rows, first_hop)


def swap_second(rows):
    return swap(rows, second_hop)


def turn(rows, step):
    count = lax.axis_size("expert")
    return lax.ppermute(rows, "expert", [(i, (i + step) % count) for i in range(count)])


def after(values, *others):
    return lax.optimization_barrier((values, others))[0]


def along_first(part):
    return jnp.concatenate([part, swap_first(part)], 0)


def gather_plane_last(block):
    ahead, behind = turn(block, 1), turn(block, -1)
    far = turn(ahead, 1)
    found = []
    for part in (block, ahead, behind, far):
        pair = jnp.concatenate([part, swap_first(part)], 0)
        found.append((pair, swap_second(pair)))
    return found, far


def gather_ring(block):
    pair = jnp.concatenate([block, swap_first(block)], 0)
    ahead, behind = turn(pair, 1), turn(pair, -1)
    return pair, ahead, behind, turn(ahead, 1)


def ring_sum(parts, gate=()):
    behind = turn(parts[2].astype(NARROW), 1)
    far = turn(parts[3].astype(NARROW), -1)
    ahead = turn((parts[1] + far.astype(WIDE)).astype(NARROW), -1)
    behind, ahead = after((behind, ahead), gate)
    return parts[0] + behind.astype(WIDE) + ahead.astype(WIDE)


def add_second(near, away, gate=()):
    return near + after(swap_second(away.astype(NARROW)), gate).astype(WIDE)


def add_first(rows, gate=()):
    half = rows.shape[0] // 2
    return rows[:half] + after(swap_first(rows[half:].astype(NARROW)), gate).astype(WIDE)


def gathered_sources(count_dp, count_expert):
    table = np.zeros((count_dp, count_expert, 4, 2, 2, 2), np.int32)
    for i in range(count_dp):
        for z in range(count_expert):
            for spot, distance in enumerate(DISTANCE):
                for second in range(2):
                    for first in range(2):
                        plane = i ^ (first_hop(i) * first) ^ (second_hop(i) * second)
                        table[i, z, spot, second, first] = plane, (z - distance) % count_expert
    return table.reshape(count_dp, count_expert, 16, 2)


def split_three(values):
    high = values.astype(NARROW)
    left = values - high.astype(WIDE)
    middle = left.astype(NARROW)
    return [high, middle, (left - middle.astype(WIDE)).astype(NARROW)]


def select_columns(values, chosen):
    rows = values.shape[0]
    parts = jnp.dot(
        jnp.concatenate(split_three(values), 0), chosen, preferred_element_type=jnp.float32
    )
    return parts[:rows] + parts[rows : 2 * rows] + parts[2 * rows :]


def parity_columns(rows, parity):
    count = rows.shape[0]
    query_total_width = QUERY_HEADS * HEAD_SIZE
    key_columns_width = KEY_VALUE_HEADS * HEAD_SIZE
    bounds = (
        (0, query_total_width),
        (query_total_width, query_total_width + key_columns_width),
        (query_total_width + key_columns_width, query_total_width + 2 * key_columns_width),
    )
    return jnp.concatenate(
        [
            rows[:, low:high].reshape(count, KEY_VALUE_HEADS // 2, 2, -1)[:, :, parity]
            .reshape(count, -1)
            for low, high in bounds
        ],
        1,
    )


def split_head_group(projected_rows, cosine_table, sine_table):
    sequences, length = projected_rows.shape[:2]
    heads = KEY_VALUE_HEADS // 2
    group = QUERY_HEADS // KEY_VALUE_HEADS
    query_width = heads * group * HEAD_SIZE
    key_width = heads * HEAD_SIZE
    query_block = projected_rows[..., :query_width].reshape(
        sequences, length, heads, group, HEAD_SIZE
    )
    key_rows = projected_rows[..., query_width : query_width + key_width].reshape(
        sequences, length, heads, HEAD_SIZE
    )
    value_rows = projected_rows[..., query_width + key_width :].reshape(
        sequences, length, heads, HEAD_SIZE
    )
    query_block = jax.vmap(lambda a: apply_rotary(a, cosine_table, sine_table, 2))(query_block)
    key_rows = jax.vmap(lambda a: apply_rotary(a, cosine_table, sine_table, 1))(key_rows)
    return (
        query_block.astype(jnp.bfloat16),
        key_rows.astype(jnp.bfloat16),
        value_rows.astype(jnp.bfloat16),
    )


def spread_columns_kernel(weight_ref, out_ref):
    chips, _, _, lanes = out_ref.shape
    for chip in range(chips):
        for part in range(2):
            columns = slice(part * FF + chip * lanes, part * FF + (chip + 1) * lanes)
            out_ref[chip, part] = weight_ref[0, :, columns].astype(out_ref.dtype)


def spread_columns(weight, chips):
    experts, rows, both = weight.shape
    lanes = both // 2 // chips
    return pl.pallas_call(
        spread_columns_kernel,
        grid=(experts,),
        in_specs=[pl.BlockSpec((1, rows, both), lambda e: (e, 0, 0))],
        out_specs=pl.BlockSpec((chips, 2, rows, lanes), lambda e: (0, 0, 0, e)),
        out_shape=jax.ShapeDtypeStruct((chips, 2, rows, experts * lanes), jnp.bfloat16),
        cost_estimate=pl.CostEstimate(
            flops=0, bytes_accessed=6 * experts * rows * both, transcendentals=0
        ),
    )(weight)


def stack_rows_kernel(place_ref, mine_ref, theirs_ref, gate_ref, upper_ref, sems):
    core = place_ref[1]
    chips, _, rows, _ = mine_ref.shape
    copies = []
    for chip in range(chips):
        for mate, ref in enumerate((mine_ref, theirs_ref)):
            start = pl.multiple_of((chip * 2 + (core ^ mate)) * rows, rows)
            for part, out_ref in enumerate((gate_ref, upper_ref)):
                copies.append(
                    pltpu.make_async_copy(
                        ref.at[chip, part],
                        out_ref.at[pl.ds(start, rows), :],
                        sems.at[len(copies)],
                    )
                )
    for copy in copies:
        copy.start()
    for copy in copies:
        copy.wait()


def stack_rows(place, mine, theirs):
    chips, _, rows, columns = mine.shape
    shape = jax.ShapeDtypeStruct((2 * chips * rows, columns), jnp.bfloat16)
    return pl.pallas_call(
        stack_rows_kernel,
        in_specs=[pl.BlockSpec(memory_space=pltpu.SMEM)]
        + [pl.BlockSpec(memory_space=pltpu.VMEM)] * 2,
        out_specs=[pl.BlockSpec(memory_space=pl.ANY)] * 2,
        out_shape=[shape] * 2,
        scratch_shapes=[pltpu.SemaphoreType.DMA((4 * chips,))],
        cost_estimate=pl.CostEstimate(
            flops=0, bytes_accessed=16 * chips * rows * columns, transcendentals=0
        ),
    )(place, mine, theirs)


def stack_attention_kernel(*refs):
    blocks, (qkv_ref, gain_ref, out_ref, sems) = refs[:-4], refs[-4:]
    wide, lanes = qkv_ref.shape[1], gain_ref.shape[1]
    owned = out_ref.shape[0] // (2 * len(blocks))
    copies = []
    for i, block in enumerate(blocks):
        for j in range(2):
            top, spot = 3 * owned * j, 2 * i + j
            pairs = (
                (
                    block.at[pl.ds(top, 2 * owned), pl.ds(0, wide)],
                    qkv_ref.at[pl.ds(2 * owned * spot, 2 * owned), :],
                ),
                (
                    block.at[pl.ds(top, 2 * owned), pl.ds(wide, lanes)],
                    gain_ref.at[pl.ds(2 * owned * spot, 2 * owned), :],
                ),
                (
                    block.at[pl.ds(top + 2 * owned, owned), :],
                    out_ref.at[pl.ds(owned * spot, owned), :],
                ),
            )
            for source, target in pairs:
                copies.append(pltpu.make_async_copy(source, target, sems.at[len(copies)]))
    for copy in copies:
        copy.start()
    for copy in copies:
        copy.wait()


def stack_attention(blocks, wide, lanes):
    owned = blocks[0].shape[0] // 6
    count = 2 * len(blocks)
    b16 = lambda r, c: jax.ShapeDtypeStruct((r, c), jnp.bfloat16)
    return pl.pallas_call(
        stack_attention_kernel,
        in_specs=[pl.BlockSpec(memory_space=pltpu.VMEM)] * len(blocks),
        out_specs=[pl.BlockSpec(memory_space=pl.ANY)] * 3,
        out_shape=[
            b16(2 * owned * count, wide),
            b16(2 * owned * count, lanes),
            b16(owned * count, blocks[0].shape[1]),
        ],
        scratch_shapes=[pltpu.SemaphoreType.DMA((3 * count,))],
        cost_estimate=pl.CostEstimate(
            flops=0, bytes_accessed=4 * 3 * owned * count * MODEL_WIDTH, transcendentals=0
        ),
    )(*blocks)


def attention_grads_kernel(
    normed_ref, joined_ref, attended_ref, grads_ref, gain_ref, near_ref, away_ref
):
    contract = (((0,), (0,)), ((), ()))
    wide, lanes = joined_ref.shape[1], gain_ref.shape[1]
    spots = near_ref.shape[0]
    owned = near_ref.shape[1] // 6
    joined, grads = joined_ref[...], grads_ref[...]

    def place(spot, second, first, row, columns, values):
        rows = pl.ds(3 * owned * first + row, values.shape[0])
        if second:
            away_ref[spot, rows, columns] = values.astype(away_ref.dtype)
        else:
            near_ref[spot, rows, columns] = values

    for spot in range(spots):
        rows = 8 * owned
        qkv = lax.dot_general(
            normed_ref[:, rows * spot : rows * (spot + 1)],
            joined,
            contract,
            preferred_element_type=jnp.float32,
        )
        for i in range(4):
            part = slice(2 * owned * i, 2 * owned * (i + 1))
            place(spot, i // 2, i % 2, 0, pl.ds(0, wide), qkv[part])
            gain = gain_ref[pl.ds(rows * spot + 2 * owned * i, 2 * owned), :]
            place(spot, i // 2, i % 2, 0, pl.ds(wide, lanes), gain)
            place(spot, i // 2, i % 2, 0, pl.ds(wide + lanes, lanes), jnp.zeros_like(gain))
        if spot % 2 == 0:
            out = lax.dot_general(
                attended_ref[:, 4 * owned * spot : 4 * owned * (spot + 2)],
                grads,
                contract,
                preferred_element_type=jnp.float32,
            )
            for i in range(8):
                part = slice(owned * i, owned * (i + 1))
                place(
                    spot + i // 4,
                    i // 2 % 2,
                    i % 2,
                    2 * owned,
                    pl.ds(0, out.shape[1]),
                    out[part],
                )


def attention_grads(normed, joined, attended, grads, gain, owned):
    spots = len(DISTANCE)
    shape = (spots, 6 * owned, grads.shape[1])
    return pl.pallas_call(
        attention_grads_kernel,
        out_shape=[
            jax.ShapeDtypeStruct(shape, jnp.float32),
            jax.ShapeDtypeStruct(shape, jnp.bfloat16),
        ],
        compiler_params=pltpu.CompilerParams(vmem_limit_bytes=44 * 1024 * 1024),
        cost_estimate=pl.CostEstimate(
            flops=2 * normed.shape[0] * normed.shape[1] * (joined.shape[1] + grads.shape[1] // 2),
            bytes_accessed=20 * 1024 * 1024,
            transcendentals=0,
        ),
    )(normed, joined, attended, grads, gain)


def expert_kernel(place_ref, *refs, per_step, count):
    source_refs = refs[:count]
    given_ref, gate_ref, upper_ref, down_ref = refs[count : count + 4]
    back_refs = refs[-9 - count : -9]
    hidden_ref, grad_gate_ref, grad_upper_ref, rows_ref, grads_ref, narrow_ref = refs[-9:-3]
    route_ref, out_ref, back_ref = refs[-3:]
    step = pl.program_id(0)
    half, width = source_refs[0].shape

    @pl.when(step == 0)
    def _():
        for i, ref in enumerate(source_refs):
            rows_ref[half * i : half * (i + 1), :] = ref[...]
        grads_ref[...] = given_ref[:, :width]
        lanes = lax.broadcasted_iota(jnp.int32, route_ref.shape, 1)
        expert = (lanes + place_ref[2]).astype(jnp.float32)
        routes = given_ref[:, width:].astype(jnp.float32)
        weights = (
            routes[:, TOP : 2 * TOP]
            + routes[:, 2 * TOP : 3 * TOP]
            + routes[:, 3 * TOP : 4 * TOP]
        )
        dense = jnp.zeros_like(expert)
        for k in range(TOP):
            dense += jnp.where(expert == routes[:, k : k + 1], weights[:, k : k + 1], 0.0)
        route_ref[...] = dense
        out_ref[...] = jnp.zeros_like(out_ref)
        back_ref[...] = jnp.zeros_like(back_ref)

    rows = rows_ref[...]
    grads = grads_ref[...]
    contract_last = (((1,), (1,)), ((), ()))
    gate = jnp.dot(rows, gate_ref[...], preferred_element_type=jnp.float32)
    upper = jnp.dot(rows, upper_ref[...], preferred_element_type=jnp.float32)
    grad_hidden = lax.dot_general(
        grads, down_ref[...], contract_last, preferred_element_type=jnp.float32
    )
    route = route_ref[...]
    lanes = lax.broadcasted_iota(jnp.int32, route.shape, 1)
    columns = gate.shape[1] // per_step
    spread = []
    for i in range(per_step):
        one = jnp.sum(jnp.where(lanes == step * per_step + i, route, 0.0), 1, keepdims=True)
        spread.append(jnp.broadcast_to(one, (route.shape[0], columns)))
    weight = jnp.concatenate(spread, 1)
    sigma = 1.0 / (1.0 + jnp.exp(-gate))
    active = gate * sigma
    hidden = (weight * active * upper).astype(jnp.bfloat16)
    weighted = weight * grad_hidden
    grad_gate = (weighted * upper * sigma * (1.0 + gate * (1.0 - sigma))).astype(jnp.bfloat16)
    grad_upper = (weighted * active).astype(jnp.bfloat16)
    hidden_ref[...] = hidden
    grad_gate_ref[...] = grad_gate
    grad_upper_ref[...] = grad_upper
    out_ref[...] += jnp.dot(hidden, down_ref[...], preferred_element_type=jnp.float32)
    back_ref[...] += lax.dot_general(
        grad_gate, gate_ref[...], contract_last, preferred_element_type=jnp.float32
    ) + lax.dot_general(
        grad_upper, upper_ref[...], contract_last, preferred_element_type=jnp.float32
    )

    @pl.when(step == pl.num_programs(0) - 1)
    def _():
        narrow_ref[...] = out_ref[...].astype(jnp.bfloat16)
        for i, ref in enumerate(back_refs):
            ref[...] = back_ref[half * i : half * (i + 1), :].astype(ref.dtype)


def expert_block(place, spot, second, sources, given, weights, experts, filled):
    gate_w, upper_w, down_w = weights
    half, width = sources[0].shape
    wide = given.shape[1]
    total = gate_w.shape[1]
    per_step = 2
    steps = experts // per_step
    columns = total // steps
    count = len(sources)
    rows = half * count
    every = 2 * half * len(DISTANCE)
    at = (2 * spot + second) // count
    of = lambda p: p[3 + spot] * (2 // count) + second
    dtypes = (jnp.float32, jnp.bfloat16)[second : second + count]
    b16 = lambda r, c: jax.ShapeDtypeStruct((r, c), jnp.bfloat16)
    fixed = pl.BlockSpec((half, width), lambda i, p: (0, 0))
    part = pl.BlockSpec((rows, columns), lambda i, p: (at, i))
    kept = pl.BlockSpec((rows, width), lambda i, p: (at, 0))
    inputs = (place, *sources, given, gate_w, upper_w, down_w)
    return pl.pallas_call(
        functools.partial(expert_kernel, per_step=per_step, count=count),
        grid_spec=pltpu.PrefetchScalarGridSpec(
            num_scalar_prefetch=1,
            grid=(steps,),
            in_specs=[fixed] * count
            + [
                pl.BlockSpec((rows, wide), lambda i, p: (of(p), 0)),
                pl.BlockSpec((width, columns), lambda i, p: (0, i)),
                pl.BlockSpec((width, columns), lambda i, p: (0, i)),
                pl.BlockSpec((columns, width), lambda i, p: (i, 0)),
            ]
            + [pl.BlockSpec(memory_space=pl.ANY)] * len(filled),
            out_specs=[fixed] * count
            + [part] * 3
            + [kept] * 2
            + [pl.BlockSpec((rows, width), lambda i, p: (of(p), 0))],
            scratch_shapes=[
                pltpu.VMEM((rows, wide - width), jnp.float32),
                pltpu.VMEM((rows, width), jnp.float32),
                pltpu.VMEM((rows, width), jnp.float32),
            ],
        ),
        out_shape=[jax.ShapeDtypeStruct((half, width), dtype) for dtype in dtypes]
        + [b16(every, total)] * 3
        + [b16(every, width)] * 3,
        input_output_aliases={len(inputs) + i: count + i for i in range(len(filled))},
        compiler_params=pltpu.CompilerParams(vmem_limit_bytes=48 * 1024 * 1024),
        cost_estimate=pl.CostEstimate(
            flops=2 * rows * width * total * 6,
            bytes_accessed=2 * (3 * width * total + 3 * rows * total + 12 * rows * width),
            transcendentals=rows * total,
        ),
    )(*inputs, *filled)


def column_grads_kernel(
    place_ref, rows_ref, grad_gate_ref, grad_upper_ref, *refs
):
    keep_ref, give_ref, full_ref = refs[-3:]
    core = place_ref[1]
    contract = (((0,), (0,)), ((), ()))
    chips, _, plane_rows, _ = keep_ref.shape
    for part, ref in enumerate((grad_gate_ref, grad_upper_ref)):
        full_ref[...] = lax.dot_general(
            rows_ref[...], ref[...], contract, preferred_element_type=jnp.float32
        )
        for chip in range(chips):
            mine = pl.multiple_of((2 * chip + core) * plane_rows, plane_rows)
            theirs = pl.multiple_of((2 * chip + 1 - core) * plane_rows, plane_rows)
            keep_ref[chip, part] = full_ref[pl.ds(mine, plane_rows), :]
            give_ref[chip, part] = full_ref[pl.ds(theirs, plane_rows), :].astype(give_ref.dtype)


def column_grads(place, step, steps, rows_all, grad_gate, grad_upper, chips, filled):
    tokens, width = rows_all.shape
    total = grad_gate.shape[1]
    columns = total // steps
    plane_rows = width // (2 * chips)
    part = pl.BlockSpec((tokens, columns), lambda i, p: (0, step))
    wide = pl.BlockSpec((chips, 2, plane_rows, columns), lambda i, p: (0, 0, 0, step))
    shape = (chips, 2, plane_rows, total)
    return pl.pallas_call(
        column_grads_kernel,
        grid_spec=pltpu.PrefetchScalarGridSpec(
            num_scalar_prefetch=1,
            grid=(1,),
            in_specs=[pl.BlockSpec((tokens, width), lambda i, p: (0, 0)), part, part]
            + [pl.BlockSpec(memory_space=pl.ANY)] * len(filled),
            out_specs=[wide, wide],
            scratch_shapes=[pltpu.VMEM((width, columns), jnp.float32)],
        ),
        out_shape=[
            jax.ShapeDtypeStruct(shape, jnp.float32),
            jax.ShapeDtypeStruct(shape, jnp.bfloat16),
        ],
        input_output_aliases={4 + i: i for i in range(len(filled))},
        compiler_params=pltpu.CompilerParams(vmem_limit_bytes=56 * 1024 * 1024),
        cost_estimate=pl.CostEstimate(
            flops=4 * tokens * width * columns,
            bytes_accessed=2 * tokens * (width + 2 * columns) + 6 * 2 * width * columns,
            transcendentals=0,
        ),
    )(place, rows_all, grad_gate, grad_upper, *filled)


def down_grads_kernel(place_ref, grads_ref, hidden_ref, keep_ref, give_ref, full_ref):
    core = place_ref[1]
    full_ref[...] = lax.dot_general(
        hidden_ref[...],
        grads_ref[...],
        (((0,), (0,)), ((), ())),
        preferred_element_type=jnp.float32,
    )
    experts, down_rows, _ = keep_ref.shape
    for e in range(experts):
        mine = pl.multiple_of((2 * e + core) * down_rows, down_rows)
        theirs = pl.multiple_of((2 * e + 1 - core) * down_rows, down_rows)
        keep_ref[e] = full_ref[pl.ds(mine, down_rows), :]
        give_ref[e] = full_ref[pl.ds(theirs, down_rows), :]


def down_grads(place, steps, grads_all, hidden, experts):
    tokens, width = grads_all.shape
    total = hidden.shape[1]
    columns = total // steps
    per_step = experts // steps
    down_rows = total // experts // 2
    down = pl.BlockSpec((per_step, down_rows, width), lambda i, p: (i, 0, 0))
    return pl.pallas_call(
        down_grads_kernel,
        grid_spec=pltpu.PrefetchScalarGridSpec(
            num_scalar_prefetch=1,
            grid=(steps,),
            in_specs=[
                pl.BlockSpec((tokens, width), lambda i, p: (0, 0)),
                pl.BlockSpec((tokens, columns), lambda i, p: (0, i)),
            ],
            out_specs=[down, down],
            scratch_shapes=[pltpu.VMEM((columns, width), jnp.float32)],
        ),
        out_shape=[jax.ShapeDtypeStruct((experts, down_rows, width), jnp.float32)] * 2,
        compiler_params=pltpu.CompilerParams(vmem_limit_bytes=36 * 1024 * 1024),
        cost_estimate=pl.CostEstimate(
            flops=2 * tokens * width * total,
            bytes_accessed=2 * tokens * (width + total) + 4 * width * total,
            transcendentals=0,
        ),
    )(place, grads_all, hidden)


def adam_columns_kernel(w_ref, first_ref, second_ref, grad_ref, *outs):
    chips, _, _, lanes = grad_ref.shape
    for chip in range(chips):
        for part in range(2):
            columns = slice(part * FF + chip * lanes, part * FF + (chip + 1) * lanes)
            grad = grad_ref[chip, part].astype(jnp.float32)
            found = adam_step(
                w_ref[0, :, columns],
                grad,
                first_ref[0, :, columns],
                second_ref[0, :, columns],
                learn_rate,
                weight_decay,
            )
            for out_ref, value in zip(outs, (grad,) + found):
                out_ref[0, :, columns] = value


def adam_columns(weight, first, second, grads):
    experts, rows, both = weight.shape
    chips = grads.shape[0]
    lanes = grads.shape[3] // experts
    block = pl.BlockSpec((1, rows, both), lambda e: (e, 0, 0))
    return pl.pallas_call(
        adam_columns_kernel,
        grid=(experts,),
        in_specs=[block] * 3 + [pl.BlockSpec((chips, 2, rows, lanes), lambda e: (0, 0, 0, e))],
        out_specs=[block] * 4,
        out_shape=[jax.ShapeDtypeStruct(weight.shape, jnp.float32)] * 4,
        compiler_params=pltpu.CompilerParams(vmem_limit_bytes=56 * 1024 * 1024),
        cost_estimate=pl.CostEstimate(
            flops=20 * experts * rows * both,
            bytes_accessed=30 * experts * rows * both,
            transcendentals=experts * rows * both,
        ),
    )(weight, first, second, grads)


def adam_heads_kernel(
    place_ref, here_ref, there_ref, w_ref, first_ref, second_ref, grad_ref, *new_refs
):
    mine_even = place_ref[1] == 0
    rows = w_ref.shape[0]
    heads = KEY_VALUE_HEADS // 2
    start = 0
    for total in (QUERY_HEADS, KEY_VALUE_HEADS, KEY_VALUE_HEADS):
        width = total * HEAD_SIZE // KEY_VALUE_HEADS
        for i in range(heads):
            columns = slice(start // 2 + width * i, start // 2 + width * (i + 1))
            mine, theirs = here_ref[:rows, columns], there_ref[:rows, columns]
            at = start + 2 * width * i
            grad_ref[:, at : at + 2 * width] = jnp.concatenate(
                [jnp.where(mine_even, mine, theirs), jnp.where(mine_even, theirs, mine)], 1
            )
        start += 2 * width * heads
    found = adam_step(
        w_ref[...], grad_ref[...], first_ref[...], second_ref[...], learn_rate, weight_decay
    )
    for ref, value in zip(new_refs, found):
        ref[...] = value


def adam_heads(place, here, there, weight, first, second):
    return pl.pallas_call(
        adam_heads_kernel,
        in_specs=[pl.BlockSpec(memory_space=pltpu.SMEM)]
        + [pl.BlockSpec(memory_space=pltpu.VMEM)] * 5,
        out_shape=[jax.ShapeDtypeStruct(weight.shape, jnp.float32)] * 4,
        cost_estimate=pl.CostEstimate(
            flops=20 * weight.size, bytes_accessed=40 * weight.size, transcendentals=weight.size
        ),
    )(place, here, there, weight, first, second)


def shards_moved(
    tokens,
    cotangent,
    segments,
    expert_ids,
    route_weights,
    w_qkv,
    w_out,
    gains,
    w_gate_up,
    w_down,
    first_moment_projection,
    first_out,
    first_gains,
    first_gate_up,
    first_down,
    second_moment_projection,
    second_out,
    second_gains,
    second_gate_up,
    second_down,
):
    sequence_length = segments.shape[1]
    count_dp, count_expert = lax.axis_size("dp"), lax.axis_size("expert")
    place_dp, place_expert = lax.axis_index("dp"), lax.axis_index("expert")
    core = place_dp % 2
    chip = place_dp // 2
    chips = count_dp // 2
    local_experts = EXPERTS // count_expert
    owned = w_qkv.shape[0]
    half_columns = w_qkv.shape[1] // 2
    half_width = MODEL_WIDTH // 2
    lane_pad = 128

    narrow_qkv = w_qkv.astype(NARROW)
    even_columns, odd_columns = parity_columns(narrow_qkv, 0), parity_columns(narrow_qkv, 1)
    gain_columns = jnp.pad(gains.astype(NARROW).T, ((0, 0), (0, lane_pad - 2)))
    kept = jnp.where(core == 0, even_columns, odd_columns)
    given = jnp.where(core == 0, odd_columns, even_columns)
    rest = jnp.zeros((owned, MODEL_WIDTH - half_columns - lane_pad), NARROW)
    taken = swap_core(jnp.concatenate([given, gain_columns], 1))
    block = jnp.concatenate(
        [
            jnp.concatenate([kept, gain_columns, rest], 1),
            jnp.concatenate([taken, rest], 1),
            w_out.astype(NARROW),
        ],
        0,
    )
    share = local_experts * (FF // chips)
    ahead, behind = turn(block, 1), turn(block, -1)
    pieces = spread_columns(after(w_gate_up, taken), chips)
    attention_ring = [block, ahead, behind, turn(after(ahead, pieces), 1)]
    attention_pairs = [along_first(part) for part in attention_ring[:2]]
    routes = jnp.concatenate([expert_ids.astype(NARROW)] + split_three(route_weights), 1)
    cotangent_rows = jnp.concatenate(
        [
            cotangent.astype(NARROW),
            jnp.pad(routes, ((0, 0), (0, lane_pad - routes.shape[1]))),
        ],
        1,
    )
    cotangent_pair = along_first(cotangent_rows)
    cotangent_here = jnp.concatenate([cotangent_pair, swap_second(cotangent_pair)], 0)
    cotangent_all = lax.all_gather(
        after(cotangent_here, attention_ring), "expert", axis=0, tiled=True
    )
    attention_pairs.append(along_first(attention_ring[2]))
    attention_pairs.append(along_first(after(attention_ring[3], cotangent_here)))
    attention_blocks = [(pair, swap_second(pair)) for pair in attention_pairs]

    sources = jnp.asarray(gathered_sources(count_dp, count_expert))[place_dp, place_expert]
    from_dp, from_expert = sources[:, 0], sources[:, 1]
    row_in = jnp.arange(owned, dtype=jnp.int32)
    feature = (
        ((from_dp[:, None] ^ jnp.arange(2, dtype=jnp.int32)[None, :]) * count_expert
         + from_expert[:, None])[:, :, None] * owned + row_in
    ).reshape(-1)
    head_feature = (
        ((from_dp // 2 * count_expert + from_expert) * owned)[:, None] + row_in
    ).reshape(-1)
    places = jnp.arange(MODEL_WIDTH, dtype=jnp.int32)
    to_gathered = (places[:, None] == feature[None, :]).astype(NARROW)
    from_gathered = (feature[:, None] == places[None, :]).astype(NARROW)
    head_places = places[: half_width]
    heads_to_gathered = (head_places[:, None] == head_feature[None, :]).astype(NARROW)
    heads_from_gathered = (head_feature[:, None] == head_places[None, :]).astype(NARROW)

    found_at = (place_expert - jnp.asarray(DISTANCE, jnp.int32)) % count_expert
    place = jnp.concatenate(
        [jnp.stack([chip, core, place_expert * local_experts]).astype(jnp.int32), found_at]
    )
    parities = [list(range(i, count_dp, 2)) for i in range(2)]
    pieces = lax.all_to_all(
        pieces, "dp", 0, 0, axis_index_groups=parities, tiled=True
    )
    down_mine = after(w_down, attention_pairs[0]).astype(NARROW)
    down_theirs = swap_core(down_mine)
    down_w = jnp.where(
        core == 0,
        jnp.concatenate([down_mine, down_theirs], 1),
        jnp.concatenate([down_theirs, down_mine], 1),
    ).reshape(share, MODEL_WIDTH)
    attention_blocks = after(attention_blocks, (down_w, pieces))

    cosine_table, sine_table = rotary_tables(sequence_length, HEAD_SIZE // 2)
    inputs = tokens.astype(WIDE)
    pair_tokens = jnp.concatenate([tokens, swap_core(tokens)], 0)
    pair_segments = jnp.concatenate([segments, swap_core(segments)], 0)
    scale_pair = norm_scale(pair_tokens.astype(WIDE))
    scale_one = scale_pair[:sequence_length]
    pair_gathered = jnp.dot(pair_tokens, to_gathered, preferred_element_type=jnp.float32)
    blocks = [half for pair in attention_blocks for half in pair]
    qkv_here, gain_here, out_here = stack_attention(blocks, half_columns, lane_pad)
    gain_here = gain_here[:, :2].T
    gain_attn = gain_here[0].astype(WIDE)
    gains_placed = jnp.dot(gain_here, from_gathered, preferred_element_type=jnp.float32)
    gain_moe = gains_placed[1]
    normed_one = (pair_gathered * scale_pair * gain_attn).astype(NARROW)
    projected = jnp.dot(normed_one, qkv_here, preferred_element_type=jnp.float32)
    query_block, key_rows, value_rows = split_head_group(
        projected.reshape(2, sequence_length, -1), cosine_table, sine_table
    )
    attended, logsums = jax.vmap(attend)(query_block, key_rows, value_rows, pair_segments)
    attended = attended.reshape(2 * sequence_length, half_width)
    attended = jnp.dot(attended, heads_to_gathered, preferred_element_type=jnp.float32).astype(
        NARROW
    )
    resid_parts = jnp.dot(attended, out_here, preferred_element_type=jnp.float32)
    resid = inputs + resid_parts[:sequence_length] + swap_core(resid_parts[sequence_length:])
    scale_two = norm_scale(resid)
    normed_two = (resid * scale_two * gain_moe).astype(NARROW)
    normed_two = after(normed_two, pieces)

    normed_ring = [normed_two] + [turn(normed_two, distance) for distance in DISTANCE[1:]]
    gate_w, upper_w = stack_rows(place, pieces, after(swap_core(pieces), normed_two))
    back_parts, filled = [], []
    second_parts, begun, halves, backs = [], (), [], {}
    for spot, second in ((0, 0), (0, 1), (1, 0), (2, 0), (1, 1), (2, 1), (3, 0)):
        if second == 0:
            near = along_first(after(normed_ring[spot], begun))
            halves.append((near, swap_second(near)))
        sources = halves[spot] if spot == 3 else halves[spot][second : second + 1]
        if spot >= 2 and (spot, second) != (2, 0):
            gate = (second_parts[spot - 2], back_parts[: spot - 2])
            sources = after(sources, gate)
        done = expert_block(
            place,
            spot,
            second,
            sources,
            cotangent_all,
            (gate_w, upper_w, down_w),
            local_experts,
            filled,
        )
        backs.setdefault(spot, []).extend(done[: len(sources)])
        filled = done[len(sources) :]
        begun = begun or (done[0],)
        if second == 1:
            second_parts.append(add_second(*backs[spot]))
            back_parts.append(add_first(second_parts[-1]))
    back = backs[3]
    hidden, grad_gate, grad_upper, rows_all, grads_all, out_all = filled
    steps = local_experts // 2
    kept_grads = []
    for step in range(steps):
        kept_grads = column_grads(
            place, step, steps, rows_all, grad_gate, grad_upper, chips, kept_grads
        )
        if step == 0:
            last = add_second(*back, kept_grads)
        elif step == 1:
            back_parts.append(add_first(last, kept_grads))
        elif step == 2:
            found = [
                turn(part.astype(NARROW), -distance)
                for part, distance in zip(back_parts[1:], DISTANCE[1:])
            ]
            grad_normed_two = back_parts[0] + sum(
                part.astype(WIDE) for part in after(found, kept_grads)
            )
            rows_all = after(rows_all, grad_normed_two)
    keep, give = kept_grads
    taken = swap_core(give)
    expert_sums = (keep + taken.astype(WIDE)).astype(NARROW)
    parities = [list(range(i, count_dp, 2)) for i in range(2)]
    collected = lax.all_to_all(
        expert_sums, "dp", 0, 0, axis_index_groups=parities, tiled=True
    )
    out_sums = lax.psum_scatter(
        after(out_all, grad_normed_two), "expert", scatter_dimension=0, tiled=True
    )

    hat_two = grad_normed_two * gain_moe
    grad_gain_moe = jnp.sum(grad_normed_two * resid * scale_two, 0)
    grad_resid = cotangent + scale_two * (
        hat_two - resid * scale_two**2 * jnp.mean(hat_two * resid, -1, keepdims=True)
    )
    grad_resid_half = grad_resid.astype(NARROW)
    pair_grads = jnp.concatenate([grad_resid_half, swap_core(grad_resid_half)], 0)
    attended_gradient = lax.dot_general(
        pair_grads, out_here, (((1,), (1,)), ((), ())), preferred_element_type=jnp.float32
    ).astype(NARROW)
    attended_gradient = (
        jnp.dot(attended_gradient, heads_from_gathered, preferred_element_type=jnp.float32)
        .astype(NARROW)
        .reshape(query_block.shape)
    )
    grad_query, grad_keys, grad_values = jax.vmap(attend_back)(
        query_block, key_rows, value_rows, pair_segments, logsums, attended_gradient
    )
    joined = jax.vmap(lambda a, b, c: join_grads(a, b, c, cosine_table, sine_table))(
        grad_query, grad_keys, grad_values
    ).reshape(2 * sequence_length, -1)
    joined = after(joined, expert_sums)
    grad_normed_parts = lax.dot_general(
        joined, qkv_here, (((1,), (1,)), ((), ())), preferred_element_type=jnp.float32
    )
    grad_gain_attn = jnp.sum(grad_normed_parts * pair_gathered * scale_pair, 0)
    gain_parts = jnp.stack(
        [grad_gain_attn, select_columns(grad_gain_moe[None], to_gathered)[0]], 1
    )
    near_parts, away_parts = attention_grads(
        normed_one,
        joined,
        attended,
        pair_grads,
        jnp.pad(gain_parts, ((0, 0), (0, lane_pad - 2))),
        owned,
    )
    keep_down, give_down = down_grads(
        place, steps, after(grads_all, near_parts), hidden, local_experts
    )
    part_down = keep_down + swap_core(give_down)
    new_down, new_first_down, new_second_down = adam_step(
        w_down, part_down, first_down, second_down, learn_rate, weight_decay
    )
    part_gate_up, new_gate_up, new_first_gate_up, new_second_gate_up = adam_columns(
        w_gate_up, first_gate_up, second_gate_up, after(collected, near_parts)
    )
    in_plane = [None] * len(DISTANCE)
    for i in (3, 1, 2, 0):
        in_plane[i] = add_second(near_parts[i], away_parts[i], new_gate_up)
    for i in (3, 1, 2, 0):
        in_plane[i] = add_first(in_plane[i])
    out_sums = after(out_sums, in_plane[3]).astype(WIDE)
    out_half = out_sums.shape[0] // 2
    out_sums = add_second(out_sums[:out_half], out_sums[out_half:])
    summed = ring_sum(in_plane, (new_down, out_sums))
    out_tokens = resid + add_first(out_sums, summed)
    here, there, part_out = summed[:owned], summed[owned : 2 * owned], summed[2 * owned :]
    there = swap_core(there[:, : half_columns + lane_pad])
    part_gains = (
        here[:, half_columns : half_columns + 2] + there[:, half_columns : half_columns + 2]
    ).T
    part_qkv, new_qkv, new_first_qkv, new_second_qkv = adam_heads(
        place, summed, there, w_qkv, first_moment_projection, second_moment_projection
    )

    grad_normed_parts = select_columns(grad_normed_parts, from_gathered)
    grad_normed_one = grad_normed_parts[:sequence_length] + swap_core(
        grad_normed_parts[sequence_length:]
    )
    hat_one = grad_normed_one * gains_placed[0]
    grad_tokens = grad_resid + scale_one * (
        hat_one - inputs * scale_one**2 * jnp.mean(hat_one * inputs, -1, keepdims=True)
    )

    new_out, new_first_out, new_second_out = adam_step(
        w_out, part_out, first_out, second_out, out_rate, weight_decay
    )
    new_gains, new_first_gains, new_second_gains = adam_step(
        gains, part_gains, first_gains, second_gains, gain_rate, 0.0
    )
    return (
        out_tokens,
        grad_tokens,
        part_qkv,
        part_out,
        part_gains,
        part_gate_up,
        part_down,
        new_qkv,
        new_out,
        new_gains,
        new_gate_up,
        new_down,
        new_first_qkv,
        new_first_out,
        new_first_gains,
        new_first_gate_up,
        new_first_down,
        new_second_qkv,
        new_second_out,
        new_second_gains,
        new_second_gate_up,
        new_second_down,
    )


def shards_plain(
    tokens,
    cotangent,
    segments,
    expert_ids,
    route_weights,
    w_qkv,
    w_out,
    gains,
    w_gate_up,
    w_down,
    first_moment_projection,
    first_out,
    first_gains,
    first_gate_up,
    first_down,
    second_moment_projection,
    second_out,
    second_gains,
    second_gate_up,
    second_down,
):
    sequence_count = segments.shape[0]
    sequence_length = segments.shape[1]
    groups_expert = lax.axis_size("expert")
    local_experts = EXPERTS // groups_expert
    slot_rows = groups_expert * CAP
    qkv_full, out_full, gain_full = (
        lax.all_gather(w_qkv.astype(jnp.bfloat16), ("dp", "expert"), axis=0, tiled=True),
        lax.all_gather(w_out.astype(jnp.bfloat16), ("dp", "expert"), axis=0, tiled=True),
        lax.all_gather(gains.astype(jnp.bfloat16), ("dp", "expert"), axis=1, tiled=True),
    )
    gate_up_full, down_full = (
        lax.all_gather(w_gate_up.astype(jnp.bfloat16), "dp", axis=1, tiled=True),
        lax.all_gather(w_down.astype(jnp.bfloat16), "dp", axis=1, tiled=True),
    )
    gain_attn = gain_full[0].astype(jnp.float32)
    gain_moe = gain_full[1].astype(jnp.float32)
    cosine_table, sine_table = rotary_tables(sequence_length, HEAD_SIZE // 2)
    inputs = tokens.astype(jnp.float32)
    scale_one = norm_scale(inputs)
    normed_one = (inputs * scale_one * gain_attn).astype(jnp.bfloat16)
    projected_rows = jnp.dot(normed_one, qkv_full, preferred_element_type=jnp.float32)
    query_block, key_rows, value_rows = split_heads(
        projected_rows, sequence_count, sequence_length, cosine_table, sine_table
    )
    index = 0
    attended_seq, logsum = attend(
        query_block[index], key_rows[index], value_rows[index], segments[index]
    )
    pieces = attended_seq.reshape(sequence_length, QUERY_HEADS * HEAD_SIZE)
    logsums = [logsum]
    resid = inputs + jnp.dot(pieces, out_full, preferred_element_type=jnp.float32)
    scale_two = norm_scale(resid)
    normed_two = (resid * scale_two * gain_moe).astype(jnp.bfloat16)
    flat_ids = expert_ids.reshape(-1)
    pair_count = flat_ids.shape[0]
    one_hot = (flat_ids[:, None] == jnp.arange(EXPERTS, dtype=jnp.int32)[None, :]).astype(jnp.int32)
    ranking = jnp.sum(jnp.cumsum(one_hot, 0) * one_hot, 1) - 1
    target = flat_ids * CAP + ranking
    owners = (
        jnp.full((EXPERTS * CAP,), -1, jnp.int32)
        .at[target]
        .set(jnp.arange(pair_count, dtype=jnp.int32))
    )
    filled = (owners >= 0)[:, None]
    safe_owner = jnp.maximum(owners, 0)
    send_rows = jnp.where(filled, normed_two[safe_owner // TOP], jnp.zeros((), jnp.bfloat16))
    received = lax.all_to_all(
        send_rows.reshape(groups_expert, local_experts, CAP, MODEL_WIDTH),
        "expert",
        split_axis=0,
        concat_axis=2,
        tiled=True,
    )
    received = received.reshape(local_experts, slot_rows, MODEL_WIDTH)
    mixed = jnp.einsum("erd,edf->erf", received, gate_up_full, preferred_element_type=jnp.float32)
    gate = mixed[..., :FF]
    upper = mixed[..., FF:]
    hidden = (jax.nn.silu(gate) * upper).astype(jnp.bfloat16)
    expert_out = jnp.einsum(
        "erf,efd->erd", hidden, down_full, preferred_element_type=jnp.float32
    ).astype(jnp.bfloat16)
    returned = lax.all_to_all(
        expert_out.reshape(1, local_experts, slot_rows, MODEL_WIDTH),
        "expert",
        split_axis=2,
        concat_axis=0,
        tiled=True,
    )
    picked = returned.reshape(EXPERTS * CAP, MODEL_WIDTH)[target].reshape(-1, TOP, MODEL_WIDTH)
    out_tokens = resid + jnp.sum(route_weights[..., None] * picked.astype(jnp.float32), 1)
    gate_up_back, down_back = (
        lax.all_gather(w_gate_up.astype(jnp.bfloat16), "dp", axis=1, tiled=True),
        lax.all_gather(w_down.astype(jnp.bfloat16), "dp", axis=1, tiled=True),
    )
    grad_routed = (
        (route_weights[..., None] * cotangent[:, None, :])
        .astype(jnp.bfloat16)
        .reshape(pair_count, MODEL_WIDTH)
    )
    send_grads = jnp.where(filled, grad_routed[safe_owner], jnp.zeros((), jnp.bfloat16))
    grad_expert = lax.all_to_all(
        send_grads.reshape(groups_expert, local_experts, CAP, MODEL_WIDTH),
        "expert",
        split_axis=0,
        concat_axis=2,
        tiled=True,
    )
    grad_expert = grad_expert.reshape(local_experts, slot_rows, MODEL_WIDTH)
    grad_hidden = jnp.einsum(
        "erd,efd->erf", grad_expert, down_back, preferred_element_type=jnp.float32
    )
    grad_down = jnp.einsum("erf,erd->efd", hidden, grad_expert, preferred_element_type=jnp.float32)
    sigma = jax.nn.sigmoid(gate)
    grad_mixed = jnp.concatenate(
        [grad_hidden * upper * sigma * (1.0 + gate * (1.0 - sigma)), grad_hidden * gate * sigma], -1
    ).astype(jnp.bfloat16)
    grad_gate_up = jnp.einsum(
        "erd,erf->edf", received, grad_mixed, preferred_element_type=jnp.float32
    )
    grad_received = jnp.einsum(
        "erf,edf->erd", grad_mixed, gate_up_back, preferred_element_type=jnp.float32
    ).astype(jnp.bfloat16)
    grad_back = lax.all_to_all(
        grad_received.reshape(1, local_experts, slot_rows, MODEL_WIDTH),
        "expert",
        split_axis=2,
        concat_axis=0,
        tiled=True,
    )
    grad_normed_two = jnp.sum(
        grad_back.reshape(EXPERTS * CAP, MODEL_WIDTH)[target]
        .reshape(-1, TOP, MODEL_WIDTH)
        .astype(jnp.float32),
        1,
    )
    hat_two = grad_normed_two * gain_moe
    grad_gain_moe = jnp.sum(grad_normed_two * resid * scale_two, 0)
    grad_resid = cotangent + scale_two * (
        hat_two - resid * scale_two**2 * jnp.mean(hat_two * resid, -1, keepdims=True)
    )
    grad_resid_half = grad_resid.astype(jnp.bfloat16)
    qkv_back, out_back = (
        lax.all_gather(w_qkv.astype(jnp.bfloat16), ("dp", "expert"), axis=0, tiled=True),
        lax.all_gather(w_out.astype(jnp.bfloat16), ("dp", "expert"), axis=0, tiled=True),
    )
    grad_out = jnp.dot(pieces.T, grad_resid_half, preferred_element_type=jnp.float32)
    attended_gradient = jnp.dot(
        grad_resid_half, out_back.T, preferred_element_type=jnp.float32
    ).astype(jnp.bfloat16)
    attended_gradient = attended_gradient.reshape(
        sequence_count, sequence_length, KEY_VALUE_HEADS, QUERY_HEADS // KEY_VALUE_HEADS, HEAD_SIZE
    )
    index = 0
    grad_query, grad_keys, grad_values = attend_back(
        query_block[index],
        key_rows[index],
        value_rows[index],
        segments[index],
        logsums[index],
        attended_gradient[index],
    )
    joined = join_grads(grad_query, grad_keys, grad_values, cosine_table, sine_table)
    grad_qkv = jnp.dot(normed_one.T, joined, preferred_element_type=jnp.float32)
    grad_normed_one = jnp.dot(joined, qkv_back.T, preferred_element_type=jnp.float32)
    hat_one = grad_normed_one * gain_attn
    grad_gain_attn = jnp.sum(grad_normed_one * inputs * scale_one, 0)
    grad_tokens = grad_resid + scale_one * (
        hat_one - inputs * scale_one**2 * jnp.mean(hat_one * inputs, -1, keepdims=True)
    )
    grad_gains = jnp.stack([grad_gain_attn, grad_gain_moe])
    part_qkv, part_out, part_gains = (
        lax.psum_scatter(grad_qkv, ("dp", "expert"), scatter_dimension=0, tiled=True),
        lax.psum_scatter(grad_out, ("dp", "expert"), scatter_dimension=0, tiled=True),
        lax.psum_scatter(grad_gains, ("dp", "expert"), scatter_dimension=1, tiled=True),
    )
    part_gate_up, part_down = (
        lax.psum_scatter(grad_gate_up, "dp", scatter_dimension=1, tiled=True),
        lax.psum_scatter(grad_down, "dp", scatter_dimension=1, tiled=True),
    )
    new_qkv, new_first_qkv, new_second_qkv = adam_step(
        w_qkv, part_qkv, first_moment_projection, second_moment_projection, learn_rate, weight_decay
    )
    new_out, new_first_out, new_second_out = adam_step(
        w_out, part_out, first_out, second_out, out_rate, weight_decay
    )
    new_gains, new_first_gains, new_second_gains = adam_step(
        gains, part_gains, first_gains, second_gains, gain_rate, 0.0
    )
    new_gate_up, new_first_gate_up, new_second_gate_up = adam_step(
        w_gate_up, part_gate_up, first_gate_up, second_gate_up, learn_rate, weight_decay
    )
    new_down, new_first_down, new_second_down = adam_step(
        w_down, part_down, first_down, second_down, learn_rate, weight_decay
    )
    return (
        out_tokens,
        grad_tokens,
        part_qkv,
        part_out,
        part_gains,
        part_gate_up,
        part_down,
        new_qkv,
        new_out,
        new_gains,
        new_gate_up,
        new_down,
        new_first_qkv,
        new_first_out,
        new_first_gains,
        new_first_gate_up,
        new_first_down,
        new_second_qkv,
        new_second_out,
        new_second_gains,
        new_second_gate_up,
        new_second_down,
    )


def solution(mesh):
    by_heads = mesh.shape["dp"] == KEY_VALUE_HEADS and mesh.shape["expert"] == 4
    return jax.shard_map(
        shards_moved if by_heads else shards_plain,
        mesh=mesh,
        in_specs=(
            P(("dp", "expert"), None),
            P(("dp", "expert"), None),
            P(("dp", "expert"), None),
            P(("dp", "expert"), None),
            P(("dp", "expert"), None),
            P(("dp", "expert"), None),
            P(("dp", "expert"), None),
            P(None, ("dp", "expert")),
            P("expert", "dp", None),
            P("expert", "dp", None),
            P(("dp", "expert"), None),
            P(("dp", "expert"), None),
            P(None, ("dp", "expert")),
            P("expert", "dp", None),
            P("expert", "dp", None),
            P(("dp", "expert"), None),
            P(("dp", "expert"), None),
            P(None, ("dp", "expert")),
            P("expert", "dp", None),
            P("expert", "dp", None),
        ),
        out_specs=(
            P(("dp", "expert"), None),
            P(("dp", "expert"), None),
            P(("dp", "expert"), None),
            P(("dp", "expert"), None),
            P(None, ("dp", "expert")),
            P("expert", "dp", None),
            P("expert", "dp", None),
            P(("dp", "expert"), None),
            P(("dp", "expert"), None),
            P(None, ("dp", "expert")),
            P("expert", "dp", None),
            P("expert", "dp", None),
            P(("dp", "expert"), None),
            P(("dp", "expert"), None),
            P(None, ("dp", "expert")),
            P("expert", "dp", None),
            P("expert", "dp", None),
            P(("dp", "expert"), None),
            P(("dp", "expert"), None),
            P(None, ("dp", "expert")),
            P("expert", "dp", None),
            P("expert", "dp", None),
        ),
        check_vma=False,
    )
```
